32 devices in a mesh: ctx: 8 (over y, x, core), fsdp: 4 (over z).
Axes of the slice: x: 2, y: 2, z: 4, core: 2. Of those that a mesh axis runs over, the one named last changes fastest.
Arguments:
- tokens: bfloat16 [4, 6144, 960], P('fsdp', 'ctx'), may hold values from -6 to 6
- cotangent: bfloat16 [4, 6144, 960], P('fsdp', 'ctx'), may hold values from -6 to 6
- doc_lengths: int32 [4, 1, 4], P('fsdp'), may hold values from 1 to 3072, 6144 in all within a row
- deal: int32 [4, 48], P('fsdp'), may hold values from 0 to 47, each once within a row
- attn_gain: bfloat16 [960], P('fsdp'), may hold values from 0.25 to 1.75
- w_query: bfloat16 [960, 960], P('fsdp'), may hold values from -0.1875 to 0.1875
- w_key: bfloat16 [960, 320], P('fsdp'), may hold values from -0.1875 to 0.1875
- w_value: bfloat16 [960, 320], P('fsdp'), may hold values from -0.1875 to 0.1875
- w_out: bfloat16 [960, 960], P('fsdp'), may hold values from -1.5 to 1.5
- mlp_gain: bfloat16 [960], P('fsdp'), may hold values from 0.25 to 1.75
- w_gate: bfloat16 [960, 2560], P(None, 'fsdp'), may hold values from -0.1875 to 0.1875
- w_up: bfloat16 [960, 2560], P(None, 'fsdp'), may hold values from -0.1875 to 0.1875
- w_down: bfloat16 [2560, 960], P('fsdp'), may hold values from -0.125 to 0.125
Outputs:
- output: bfloat16 [4, 6144, 960], P('fsdp', 'ctx')
- input_grad: bfloat16 [4, 6144, 960], P('fsdp', 'ctx')
- attn_gain_grad: float32 [960], P('fsdp')
- query_grad: float32 [960, 960], P('fsdp')
- key_grad: float32 [960, 320], P('fsdp')
- value_grad: float32 [960, 320], P('fsdp')
- out_grad: float32 [960, 960], P('fsdp')
- mlp_gain_grad: float32 [960], P('fsdp')
- gate_grad: float32 [960, 2560], P(None, 'fsdp')
- up_grad: float32 [960, 2560], P(None, 'fsdp')
- down_grad: float32 [2560, 960], P('fsdp')
The draws below stay inside these ranges and needn't reach their ends.
Inputs may be any that keep to these rules, and one draw needn't show every extreme that they name: `deal`: each row orders the 48 sequence-order blocks of 128 tokens of one group: entry i names the block at dealt position i, and device j of ctx holds the positions from j * 6 on. `doc_lengths`: row [f, s] lists the lengths of the 4 documents of sequence s of group f in order, summing to 6144.
All inputs are finite; a program needn't handle non-finite values.
Results may differ from the reference program's by a relative error of at most 0.022.
Values may be sent and summed in bfloat16 or wider, within the bound.
No kernel may reach another device: no remote copies, remote signals or barrier semaphores. Data moves between devices by JAX's collectives and lax.ppermute only.
A program may use at most 320 MiB of HBM per device.

```python
import math
import jax
import jax.numpy as jnp
import numpy as np
from jax import lax

D = 960
FF = 2560
HQ = 15
KVH = 5
HD = 64
BLK = 128
WIN = 1024
DOCS = 4
QW = 960
KVW = 320
GROUP = 6144
SEQS = 1
LEN = 6144
NB = 48
N_FSDP = 4


def block_scale(stream_key, dims, split, smallest, high):
    level = 1.0
    for position, shards_of in split:
        steps = jax.random.uniform(jax.random.fold_in(jax.random.fold_in(stream_key, 6), position), (shards_of,), jnp.float32, smallest / len(split), high / len(split))
        level = level * jnp.repeat(jnp.exp(steps), dims[position] // shards_of).reshape((-1,) + (1,) * (len(dims) - 1 - position))
    return level


def split_up(count, total, most, lean):
    weights = [(1 << 20) // math.isqrt(standing ** lean) + 1 for standing in range(2, count + 1)]
    surplus, given = total - most - (count - 1), [1] * (count - 1)
    while surplus > 0:
        free = [i for i in range(count - 1) if given[i] < most]
        pool, remaining = sum([weights[i] for i in free]), surplus
        for i in free:
            more = min(most - given[i], max(1, remaining * weights[i] // pool), surplus)
            given[i] = given[i] + more
            surplus = surplus - more
    return np.array([most] + given)


def uneven_parts(rng, amount, total, reach, slope):
    if amount == 2:
        one = jax.random.randint(rng, (), max(1, total - reach), min(reach, total - 1) + 1)
        return jnp.stack([one, total - one])
    tallies = jnp.asarray(split_up(amount, total, reach, slope), jnp.int32)
    couples = (amount - 1) // 2
    source_of, taker = tallies[1:1 + 2 * couples:2], tallies[2:2 + 2 * couples:2]
    margin = jnp.minimum(source_of - 1, reach - taker)
    moved = jax.random.randint(jax.random.fold_in(rng, 1), (couples,), 0, 1 << 20) % (margin + 1)
    tallies = tallies.at[1:1 + 2 * couples:2].set(source_of - moved).at[2:2 + 2 * couples:2].set(taker + moved)
    return tallies[jax.random.permutation(jax.random.fold_in(rng, 2), amount)]


def scatter_about(key, dims, scale, bound, split=(), kind=jnp.bfloat16):
    gain = block_scale(key, dims, split, -0.22, 0.18) if split else 1.0
    drawn = jax.random.normal(key, dims, jnp.float32) * scale * gain
    return jnp.minimum(jnp.maximum(drawn, -bound), bound).astype(kind)


def setup_inputs(seed: int = 0) -> dict:
    arg_keys = jax.random.split(jax.random.key(seed), 14)
    return {
        "tokens": scatter_about(arg_keys[0], (N_FSDP, GROUP, D), 1.0, 6.0, ((0, 4), (1, 8))),
        "cotangent": scatter_about(arg_keys[1], (N_FSDP, GROUP, D), 1.0, 6.0, ((0, 4), (1, 8))),
        "doc_lengths": jax.vmap(lambda own: uneven_parts(own, DOCS, LEN, LEN // 2, 2))(jax.random.split(arg_keys[2], N_FSDP * SEQS)).reshape((N_FSDP, SEQS, DOCS)).astype(jnp.int32),
        "deal": jax.vmap(lambda own: jax.random.permutation(own, NB))(jax.random.split(arg_keys[3], N_FSDP)).reshape((N_FSDP, NB)).astype(jnp.int32),
        "attn_gain": jnp.clip(1.0 + 0.15 * jax.random.normal(arg_keys[4], (D,), jnp.float32), 0.25, 1.75).astype(jnp.bfloat16),
        "w_query": scatter_about(arg_keys[5], (D, QW), D ** -0.5, 0.1875, ((0, 4),)),
        "w_key": scatter_about(arg_keys[6], (D, KVW), D ** -0.5, 0.1875, ((0, 4),)),
        "w_value": scatter_about(arg_keys[7], (D, KVW), D ** -0.5, 0.1875, ((0, 4),)),
        "w_out": scatter_about(arg_keys[8], (QW, D), (max(1, QW // 64)) ** -0.5, 1.5, ((0, 4),)),
        "mlp_gain": jnp.clip(1.0 + 0.15 * jax.random.normal(arg_keys[9], (D,), jnp.float32), 0.25, 1.75).astype(jnp.bfloat16),
        "w_gate": scatter_about(arg_keys[10], (D, FF), D ** -0.5, 0.1875, ((1, 4),)),
        "w_up": scatter_about(arg_keys[11], (D, FF), D ** -0.5, 0.1875, ((1, 4),)),
        "w_down": scatter_about(arg_keys[12], (FF, D), FF ** -0.5, 0.125, ((0, 4),)),
    }


NORM_EPS = 1e-05
ROPE_THETA = 100000.0
MASK_FILL = -1e+30

@jax.custom_vjp
def low(v):
    return lax.optimization_barrier(v.astype(jnp.bfloat16)).astype(jnp.float32)

@jax.custom_vjp
def low_back(v):
    return v

def low_keep(v):
    return (low(v), None)

def low_pass(kept, grad):
    return (grad,)

def back_keep(v):
    return (v, None)

def back_low(kept, grad):
    return (low(grad),)
low.defvjp(low_keep, low_pass)
low_back.defvjp(back_keep, back_low)

def precise_dot(inputs, others):
    return jnp.dot(inputs, others, precision=lax.Precision.HIGHEST, preferred_element_type=jnp.float32)

def rms_norm(values, gain_vec):
    return values * lax.rsqrt(lax.optimization_barrier(jnp.mean(values * values, axis=-1, keepdims=True)) + NORM_EPS) * gain_vec

def rotate(values, positions, heads):
    half_dim = HD // 2
    freqs = ROPE_THETA ** (-jnp.arange(half_dim, dtype=jnp.float32) * (2.0 / HD))
    angle = positions.astype(jnp.float32)[:, None] * freqs[None, :]
    cos_tab = jnp.cos(angle)[:, None, :]
    sin_tab = jnp.sin(angle)[:, None, :]
    shaped = values.reshape(values.shape[0], heads, HD)
    first_half = shaped[..., :half_dim]
    second_half = shaped[..., half_dim:]
    turned = jnp.concatenate([first_half * cos_tab - second_half * sin_tab, second_half * cos_tab + first_half * sin_tab], axis=-1)
    return turned.reshape(values.shape[0], heads * HD)

def attend(queries, keys, values, doc_num):
    length = queries.shape[0]
    q_step = math.gcd(length, 512)
    key_span = WIN + q_step
    head_group = HQ // KVH
    score_scale = HD ** (-0.5)
    pad_keys = jnp.concatenate([jnp.zeros((WIN, keys.shape[1]), jnp.float32), keys], axis=0)
    pad_values = jnp.concatenate([jnp.zeros((WIN, values.shape[1]), jnp.float32), values], axis=0)
    pad_docs = jnp.concatenate([jnp.full((WIN,), -1, jnp.int32), doc_num], axis=0)

    def block(first_row):
        q_blk = lax.dynamic_slice_in_dim(queries, first_row, q_step, 0).reshape(q_step, KVH, head_group, HD)
        k_blk = lax.dynamic_slice_in_dim(pad_keys, first_row, key_span, 0).reshape(key_span, KVH, HD)
        v_blk = lax.dynamic_slice_in_dim(pad_values, first_row, key_span, 0).reshape(key_span, KVH, HD)
        q_docs = lax.dynamic_slice_in_dim(doc_num, first_row, q_step, 0)
        k_docs = lax.dynamic_slice_in_dim(pad_docs, first_row, key_span, 0)
        q_time = first_row + jnp.arange(q_step, dtype=jnp.int32)
        k_time = first_row - WIN + jnp.arange(key_span, dtype=jnp.int32)
        key_mask = (k_time[None, :] >= 0) & (k_time[None, :] <= q_time[:, None]) & (q_time[:, None] - k_time[None, :] < WIN) & (q_docs[:, None] == k_docs[None, :])
        scores = jnp.einsum('qhgd,khd->hgqk', q_blk, k_blk, precision=lax.Precision.HIGHEST) * score_scale
        scores = low_back(scores)
        scores = jnp.where(key_mask[None, None], scores, MASK_FILL)
        probabilities = low(jax.nn.softmax(scores, axis=-1))
        head_result = jnp.einsum('hgqk,khd->qhgd', probabilities, v_blk, precision=lax.Precision.HIGHEST)
        return head_result.reshape(q_step, HQ * HD)
    block_starts = (jnp.arange(length // q_step) * q_step).astype(jnp.int32)
    outputs = lax.map(jax.checkpoint(block), block_starts)
    return outputs.reshape(length, HQ * HD)

def layer(inputs, weights, positions, doc_num):
    gain_one, query_w, key_w, value_w, out_w, gain_two, gate_w, up_w, down_w = weights
    attn_in = low(rms_norm(inputs, gain_one))
    query_pre = low_back(precise_dot(attn_in, query_w))
    key_pre = low_back(precise_dot(attn_in, key_w))
    value_low = low(low_back(precise_dot(attn_in, value_w)))
    query_low = low(rotate(query_pre, positions, HQ))
    key_low = low(rotate(key_pre, positions, KVH))
    attn_mid = low(low_back(attend(query_low, key_low, value_low, doc_num)))
    hidden_one = inputs + low_back(precise_dot(attn_mid, out_w))
    mlp_in = low(rms_norm(hidden_one, gain_two))
    gate_pre = low_back(precise_dot(mlp_in, gate_w))
    up_pre = low_back(precise_dot(mlp_in, up_w))
    hidden_low = low(jax.nn.silu(gate_pre) * up_pre)
    return hidden_one + low_back(precise_dot(hidden_low, down_w))

def doc_info(doc_lens):
    doc_ends = jnp.cumsum(doc_lens).astype(jnp.int32)
    doc_starts = (doc_ends - doc_lens).astype(jnp.int32)
    t_values = jnp.arange(LEN, dtype=jnp.int32)
    doc_num = lax.optimization_barrier(jnp.sum((t_values[:, None] >= doc_ends[None, :]).astype(jnp.int32), axis=1)).astype(jnp.int32)
    doc_begin = lax.optimization_barrier(jnp.sum(jnp.where(doc_num[:, None] == jnp.arange(DOCS, dtype=jnp.int32)[None, :], doc_starts[None, :], 0), axis=1)).astype(jnp.int32)
    return (doc_num, (t_values - doc_begin).astype(jnp.int32))

def reference(tokens, cotangent, doc_lengths, deal, attn_gain, w_query, w_key, w_value, w_out, mlp_gain, w_gate, w_up, w_down):
    group_count = deal.shape[0]
    blocks = deal.shape[1]
    inverse = jnp.argsort(deal, axis=1).astype(jnp.int32)

    def to_sequence(array):
        shaped = array.astype(jnp.float32).reshape(group_count, blocks, BLK, D)
        ordered = jnp.take_along_axis(shaped, inverse[:, :, None, None], axis=1)
        return ordered.reshape(group_count * SEQS, LEN, D)

    def to_dealt(array):
        shaped = array.reshape(group_count, blocks, BLK, D)
        return jnp.take_along_axis(shaped, deal[:, :, None, None], axis=1).reshape(group_count, blocks * BLK, D)
    params = tuple((weight.astype(jnp.float32) for weight in (attn_gain, w_query, w_key, w_value, w_out, mlp_gain, w_gate, w_up, w_down)))
    seq_inputs = to_sequence(tokens)
    seq_grads = to_sequence(cotangent)
    lens_all = doc_lengths.reshape(group_count * SEQS, DOCS)

    def one_sequence(totals, packed):
        seq_in, seq_cot, doc_lens = packed
        doc_num, positions = doc_info(doc_lens)

        def run(seq_values, *weights):
            return layer(seq_values, weights, positions, doc_num)
        head_result, pullback = jax.vjp(run, seq_in, *params)
        grads = pullback(seq_cot)
        summed = tuple((running + extra for running, extra in zip(totals, grads[1:])))
        return (summed, (head_result, grads[0]))
    zeros_init = tuple((jnp.zeros_like(weight) for weight in params))
    totals, (results, input_grads) = lax.scan(one_sequence, zeros_init, (seq_inputs, seq_grads, lens_all))
    return (to_dealt(results).astype(jnp.bfloat16), to_dealt(input_grads).astype(jnp.bfloat16), totals[0], totals[1], totals[2], totals[3], totals[4], totals[5], totals[6], totals[7], totals[8])
```

```python
import jax
import jax.numpy as jnp
from jax import lax
from jax.experimental import pallas as pl
from jax.experimental.pallas import tpu as pltpu
from jax.sharding import PartitionSpec as P

HQ = 15
KVH = 5
HD = 64
BLK = 128
WIN = 1024
D = 960
KVW = 320
GRP = HQ // KVH
SPAN = WIN + BLK
NWB = SPAN // BLK
ROWS = 256
ZR = 240
ZP = 256
UNITS = 256

NORM_EPS = 1e-05
ROPE_THETA = 100000.0
MASK_FILL = -1e30
F32 = jnp.float32
BF16 = jnp.bfloat16
MIB = 1024 * 1024

VMEM = pl.BlockSpec(memory_space=pltpu.VMEM)
SMEM = pl.BlockSpec(memory_space=pltpu.SMEM)
ANY = pl.BlockSpec(memory_space=pl.ANY)


def dot(a, b):
    return jnp.dot(a, b, preferred_element_type=F32)


def dot_nt(a, b):
    return lax.dot_general(a, b, (((1,), (1,)), ((), ())), preferred_element_type=F32)


def dot_tn(a, b):
    return lax.dot_general(a, b, (((0,), (0,)), ((), ())), preferred_element_type=F32)


def params(mib, grid_dims=0):
    return pltpu.CompilerParams(
        vmem_limit_bytes=mib * MIB,
        dimension_semantics=("arbitrary",) * grid_dims if grid_dims else None,
    )


def cost(flops, moved, exps=0):
    return pl.CostEstimate(flops=int(flops), bytes_accessed=int(moved), transcendentals=int(exps))


def rope_slab(t, cos, sin_signed, first_half):
    swapped = jnp.where(first_half, pltpu.roll(t, 96, 1), pltpu.roll(t, 32, 1))
    return t * cos + swapped * sin_signed


def lane_masks(rows):
    lane = lax.broadcasted_iota(jnp.int32, (rows, 128), 1)
    return (lane % HD) < HD // 2, lane < HD


def pre_kernel(
    info, x_ref, gain_ref, cos_ref, sin_ref,
    a_own, b_own, m_up, m_dn, m_t1, m_t2, o_up, o_dn, o_t1, o_t2,
    attn_ref, q_ref, kv_ref, w_ref, sems,
):
    z, core = info[0], info[1]
    other = 1 - core
    half = 640

    def rows(shift):
        return pl.ds(pl.multiple_of(lax.rem(z + shift, 4) * ZR, 16), ZR)

    pairs = [
        (a_own, w_ref.at[0, rows(0)]),
        (b_own, w_ref.at[1, rows(0)]),
    ]
    for idx, (up, dn, t1, t2) in ((core, (m_up, m_dn, m_t1, m_t2)), (other, (o_up, o_dn, o_t1, o_t2))):
        pairs += [
            (up, w_ref.at[idx, rows(3)]),
            (dn, w_ref.at[idx, rows(1)]),
            (t1, w_ref.at[idx, rows(2), pl.ds(0, half)]),
            (t2, w_ref.at[idx, rows(2), pl.ds(half, half)]),
        ]
    copies = [pltpu.make_async_copy(s, d, sems.at[i]) for i, (s, d) in enumerate(pairs)]
    for c in copies:
        c.start()
    for c in copies:
        c.wait()
    first_half, low_head = lane_masks(ROWS)
    steps = x_ref.shape[0] // ROWS

    def body(i, _):
        r = pl.ds(pl.multiple_of(i * ROWS, ROWS), ROWS)
        x = x_ref[r, :].astype(F32)
        factor = lax.rsqrt(jnp.mean(x * x, axis=-1, keepdims=True) + NORM_EPS)
        a = (x * factor * gain_ref[...]).astype(BF16)
        attn_ref[r, :] = a
        qk = dot(a, w_ref[0])
        vv = dot(a, w_ref[1, :, 896:1280])
        cos, sin = cos_ref[r, :], sin_ref[r, :]
        slabs = [
            rope_slab(qk[:, 128 * j : 128 * j + 128], cos, sin, first_half) for j in range(10)
        ]
        for j in range(7):
            q_ref[r, 128 * j : 128 * j + 128] = slabs[j].astype(BF16)
        q_ref[r, 896:960] = slabs[7][:, :64].astype(BF16)
        mixed = jnp.where(low_head, pltpu.roll(slabs[7], 64, 1), vv[:, 0:128])
        for j, part in enumerate((slabs[8], slabs[9], mixed, vv[:, 128:256], vv[:, 256:384])):
            kv_ref[r, 128 * j : 128 * j + 128] = part.astype(BF16)
        return 0

    lax.fori_loop(0, steps, body, 0)


def pre_call(info, x, gain, cos, sin, pieces):
    t = x.shape[0]
    return pl.pallas_call(
        pre_kernel,
        out_shape=(
            jax.ShapeDtypeStruct((t, D), BF16),
            jax.ShapeDtypeStruct((t, D), BF16),
            jax.ShapeDtypeStruct((t, 2 * KVW), BF16),
            jax.ShapeDtypeStruct((2, D, 1280), BF16),
        ),
        in_specs=[SMEM] + [VMEM] * 4 + [ANY] * 10,
        out_specs=(VMEM,) * 4,
        scratch_shapes=[pltpu.SemaphoreType.DMA((10,))],
        compiler_params=params(40),
        cost_estimate=cost(2 * t * D * 1600, 15e6),
        name="pre",
    )(info, x, gain, cos, sin, *pieces)


PAIRS = ((0, 3, (0, 1)), (1, 4, (2, 3)), (2, 2, (4,)))


def start_window(tab, kvs, win, sem, blk, slot):
    def body(j, _):
        entry = tab[blk, j]
        which = entry // 1024
        idx = lax.rem(entry, 1024)
        dst = win.at[slot, pl.ds(pl.multiple_of(j * BLK, BLK), BLK)]
        for n, ref in enumerate(kvs):
            @pl.when(which == n)
            def _():
                src = ref.at[pl.ds(pl.multiple_of(idx * BLK, BLK), BLK)]
                pltpu.make_async_copy(src, dst, sem.at[slot]).start()
        return 0

    lax.fori_loop(0, NWB, body, 0)


def next_window(tab, kvs, win, sem):
    i = pl.program_id(0)
    slot = lax.rem(i, 2)

    @pl.when(i == 0)
    def _():
        start_window(tab, kvs, win, sem, i, slot)

    @pl.when(i + 1 < pl.num_programs(0))
    def _():
        start_window(tab, kvs, win, sem, i + 1, 1 - slot)

    pltpu.make_async_copy(win.at[slot], win.at[slot], sem.at[slot]).wait()
    return slot


def turned_heads(flat):
    rows = flat.astype(F32)
    padded = jnp.concatenate([rows, jnp.zeros((BLK, 64), F32)], axis=1)
    return padded.T


def spread_heads(turned, heads, low):
    width = GRP * BLK
    sides = []
    for g in heads:
        sides.append(
            jnp.concatenate(
                [turned[HD * h : HD * h + HD] for h in range(GRP * g, GRP * g + GRP)], axis=1
            )
        )
    empty = jnp.zeros((HD, width), turned.dtype)
    if len(heads) == 2:
        return jnp.concatenate(
            [jnp.concatenate([sides[0], empty], axis=1), jnp.concatenate([empty, sides[1]], axis=1)],
            axis=0,
        )
    return jnp.concatenate([sides[0], empty] if low else [empty, sides[0]], axis=0)


def fwd_kernel(n_kv, tab, lo_ref, q_ref, *refs):
    kvs = refs[:n_kv]
    mid_ref, rl_ref, p_ref, win, bias, scores, sem = refs[n_kv:]
    slot = next_window(tab, kvs, win, sem)
    row = lax.broadcasted_iota(jnp.int32, (SPAN, BLK), 0)
    lane = lax.broadcasted_iota(jnp.int32, (SPAN, BLK), 1)
    allowed = (row >= lo_ref[0]) & (row <= lane + WIN)
    bias[...] = jnp.where(allowed, 0.0, MASK_FILL)
    turned = (turned_heads(q_ref[...]) * (HD ** -0.5)).astype(BF16)
    outs, recips = [], []
    for k_slab, v_slab, heads in PAIRS:
        keys = win[slot, :, 128 * k_slab : 128 * k_slab + 128]
        vals = win[slot, :, 128 * v_slab : 128 * v_slab + 128]
        count = GRP * len(heads)
        width = BLK * count
        base = BLK * GRP * heads[0]
        scores[:, :width] = dot(keys, spread_heads(turned, heads, True))
        for j in range(count):
            s = scores[:, BLK * j : BLK * j + BLK] + bias[...]
            top = jnp.max(s, axis=0, keepdims=True)
            p_ref[0, :, base + BLK * j : base + BLK * j + BLK] = jnp.exp(s - top).astype(BF16)
        lhs = jnp.concatenate([vals.T, jnp.ones((16, SPAN), BF16)], axis=0)
        product = dot(lhs, p_ref[0, :, base : base + width])
        recip = 1.0 / product[128:129, :]
        for j in range(count):
            upper = (heads[0] == 4) or j >= GRP
            cols = slice(BLK * j, BLK * j + BLK)
            part = product[64:128, cols] if upper else product[0:64, cols]
            outs.append(part * recip[:, cols])
            recips.append(recip[:, cols])
    outs.append(jnp.zeros((64, BLK), F32))
    recips.append(jnp.zeros((1, BLK), F32))
    mid_ref[...] = jnp.concatenate(outs, axis=0).T[:, :D].astype(BF16)
    rl_ref[0] = jnp.concatenate(recips, axis=0)


def fwd_call(tab, lo, q, kvs):
    blocks = q.shape[0] // BLK
    n_kv = len(kvs)
    return pl.pallas_call(
        lambda *refs: fwd_kernel(n_kv, *refs),
        grid=(blocks,),
        out_shape=(
            jax.ShapeDtypeStruct((q.shape[0], D), BF16),
            jax.ShapeDtypeStruct((blocks, 16, BLK), F32),
            jax.ShapeDtypeStruct((blocks, SPAN, HQ * BLK), BF16),
        ),
        in_specs=[
            SMEM,
            pl.BlockSpec((1, 1, BLK), lambda i: (i, 0, 0)),
            pl.BlockSpec((BLK, D), lambda i: (i, 0)),
        ]
        + [ANY] * n_kv,
        out_specs=(
            pl.BlockSpec((BLK, D), lambda i: (i, 0)),
            pl.BlockSpec((1, 16, BLK), lambda i: (i, 0, 0)),
            pl.BlockSpec((1, SPAN, HQ * BLK), lambda i: (i, 0, 0)),
        ),
        scratch_shapes=[
            pltpu.VMEM((2, SPAN, 2 * KVW), BF16),
            pltpu.VMEM((SPAN, BLK), F32),
            pltpu.VMEM((SPAN, 2 * GRP * BLK), F32),
            pltpu.SemaphoreType.DMA((2,)),
        ],
        compiler_params=params(48, 1),
        cost_estimate=cost(8e9 * blocks, 8e6 * blocks, 2.2e6 * blocks),
        name="attend",
    )(tab, lo, q, *kvs)


def bwd_kernel(n_kv, n_out, n_slots, tab, slots, q_ref, do_ref, mid_ref, rl_ref, p_ref, cos_ref, sin_ref, *refs):
    kvs = refs[:n_kv]
    dq_ref = refs[n_kv]
    outs = refs[n_kv + 1 : n_kv + 1 + n_out]
    win, acc, scores, stage, sem, out_sem = refs[n_kv + 1 + n_out :]
    i = pl.program_id(0)
    slot = next_window(tab, kvs, win, sem)

    @pl.when(i == 0)
    def _():
        def clear(b, _):
            acc[pl.ds(pl.multiple_of(b * BLK, BLK), BLK), :] = jnp.zeros((BLK, 2 * KVW), F32)
            return 0

        lax.fori_loop(0, n_slots, clear, 0)

    def add(lanes, value):
        for j in range(NWB):
            r = pl.ds(pl.multiple_of(slots[i, j] * BLK, BLK), BLK)
            acc[r, lanes : lanes + 128] += value[BLK * j : BLK * j + BLK]

    turned_q = (turned_heads(q_ref[...]) * (HD ** -0.5)).astype(BF16)
    turned_do = turned_heads(do_ref[...])
    turned_o = turned_heads(mid_ref[...])
    scaled, dots = [], []
    for h in range(HQ):
        r = rl_ref[0, h : h + 1, :]
        do_h = turned_do[HD * h : HD * h + HD] * r
        scaled.append(do_h)
        dots.append(jnp.sum(do_h * turned_o[HD * h : HD * h + HD], axis=0, keepdims=True))
    scaled = jnp.concatenate(scaled, axis=0).astype(BF16)
    cos, sin = cos_ref[0], sin_ref[0]
    grads = []
    for k_slab, v_slab, heads in PAIRS:
        keys = win[slot, :, 128 * k_slab : 128 * k_slab + 128]
        vals = win[slot, :, 128 * v_slab : 128 * v_slab + 128]
        count = GRP * len(heads)
        width = BLK * count
        base = BLK * GRP * heads[0]
        q_rows = spread_heads(turned_q, heads, True)
        do_rows = spread_heads(scaled, heads, False)
        scores[:, :width] = dot(vals, do_rows)
        ds = []
        for j in range(count):
            p = p_ref[0, :, base + BLK * j : base + BLK * j + BLK].astype(F32)
            head = GRP * heads[0] + j
            ds.append((p * (scores[:, BLK * j : BLK * j + BLK] - dots[head])).astype(BF16))
        ds = jnp.concatenate(ds, axis=1)
        probs = p_ref[0, :, base : base + width]
        if len(heads) == 2:
            add(128 * k_slab, dot_nt(ds, q_rows))
            add(128 * v_slab, dot_nt(probs, do_rows))
        else:
            add(
                128 * k_slab,
                dot_nt(
                    jnp.concatenate([ds, probs], axis=1),
                    jnp.concatenate([q_rows, do_rows], axis=1),
                ),
            )
        dq = dot(keys.T, ds) * (HD ** -0.5)
        for j in range(count):
            top = HD if j >= GRP else 0
            cols = slice(BLK * j, BLK * j + BLK)
            first = dq[top : top + 32, cols]
            second = dq[top + 32 : top + 64, cols]
            grads.append(first * cos + second * sin)
            grads.append(second * cos - first * sin)
    grads.append(jnp.zeros((64, BLK), F32))
    dq_ref[...] = jnp.concatenate(grads, axis=0).T[:, :D].astype(BF16)

    @pl.when(i == pl.num_programs(0) - 1)
    def _():
        per = 6 * BLK
        total = n_slots // 6
        each = total // n_out
        copies = []
        for t in range(total):
            s = t % 2
            if t >= 2:
                copies[t - 2].wait()
            stage[s] = acc[per * t : per * t + per, :].astype(BF16)
            out = outs[t // each]
            c = pltpu.make_async_copy(
                stage.at[s], out.at[pl.ds(per * (t % each), per)], out_sem.at[s]
            )
            c.start()
            copies.append(c)
        copies[-2].wait()
        copies[-1].wait()


def bwd_call(tab, slots, n_slots, n_out, q, do, mid, rl, p, cos, sin, kvs):
    blocks = q.shape[0] // BLK
    n_kv = len(kvs)
    flat = pl.BlockSpec((BLK, D), lambda i: (i, 0))
    table = pl.BlockSpec((1, 32, BLK), lambda i: (i, 0, 0))
    return pl.pallas_call(
        lambda *refs: bwd_kernel(n_kv, n_out, n_slots, *refs),
        grid=(blocks,),
        out_shape=(jax.ShapeDtypeStruct((q.shape[0], D), BF16),)
        + (jax.ShapeDtypeStruct((n_slots // n_out * BLK, 2 * KVW), BF16),) * n_out,
        in_specs=[
            SMEM,
            SMEM,
            flat,
            flat,
            flat,
            pl.BlockSpec((1, 16, BLK), lambda i: (i, 0, 0)),
            pl.BlockSpec((1, SPAN, HQ * BLK), lambda i: (i, 0, 0)),
            table,
            table,
        ]
        + [ANY] * n_kv,
        out_specs=(flat,) + (ANY,) * n_out,
        scratch_shapes=[
            pltpu.VMEM((2, SPAN, 2 * KVW), BF16),
            pltpu.VMEM((n_slots * BLK, 2 * KVW), F32),
            pltpu.VMEM((SPAN, 2 * GRP * BLK), F32),
            pltpu.VMEM((2, 6 * BLK, 2 * KVW), BF16),
            pltpu.SemaphoreType.DMA((2,)),
            pltpu.SemaphoreType.DMA((2,)),
        ],
        compiler_params=params(58, 1),
        cost_estimate=cost(14e9 * blocks, 8e6 * blocks),
        name="attend_back",
    )(tab, slots, q, do, mid, rl, p, cos, sin, *kvs)


def mid_kernel(
    info, mid_ref, x_ref, cot_ref, gain_ref, w_ref, *refs,
):
    pieces = refs[:10]
    out_ref, gh_ref, gm_ref, go_ref, keep_ref, send_ref = refs[10:16]
    w_out, wbuf, h1, low, acc_o, acc_g, stage, w_sem, out_sem = refs[16:]
    z = info[0]
    units = wbuf.shape[1]
    half = units // 2
    copies = [pltpu.make_async_copy(w_ref.at[1, :, pl.ds(0, 1024)], w_out, w_sem.at[10])]
    at = 0
    for n, piece in enumerate(pieces):
        size = piece.shape[1]
        copies.append(
            pltpu.make_async_copy(piece, wbuf.at[:, pl.ds(at, size), :], w_sem.at[n])
        )
        at += size
    for c in copies:
        c.start()
    copies[0].wait()
    steps = x_ref.shape[0] // ROWS
    gain = gain_ref[...]

    def first(i, _):
        r = pl.ds(pl.multiple_of(i * ROWS, ROWS), ROWS)
        h = x_ref[r, :].astype(F32) + dot(mid_ref[r, :], w_out[:, :D])
        factor = lax.rsqrt(jnp.mean(h * h, axis=-1, keepdims=True) + NORM_EPS)
        h1[r, :] = h
        low[r, :] = (h * factor * gain).astype(BF16)
        acc_o[r, :] = h
        acc_g[r, :] = jnp.zeros((ROWS, D), F32)
        return 0

    lax.fori_loop(0, steps, first, 0)
    for c in copies[1:]:
        c.wait()
    n_chunks = units // UNITS
    half_chunks = n_chunks // 2

    def out_copy(c, slot, ref, start):
        rows = pl.ds(pl.multiple_of((c - start) * UNITS, UNITS), UNITS)
        return pltpu.make_async_copy(stage.at[slot], ref.at[:, rows, :], out_sem.at[slot])

    def chunk(c, _):
        u = pl.ds(pl.multiple_of(c * UNITS, UNITS), UNITS)
        slot = lax.rem(c, 2)
        a = low[...]
        gate = dot_nt(a, wbuf[0, u, :])
        up = dot_nt(a, wbuf[1, u, :])
        grad = dot_nt(cot_ref[...], wbuf[2, u, :])
        sig = lax.logistic(gate)
        swish = gate * sig
        hid = (swish * up).astype(BF16)
        g_gate = (grad * up * sig * (1.0 + gate * (1.0 - sig))).astype(BF16)
        g_up = (grad * swish).astype(BF16)
        acc_o[...] += dot(hid, wbuf[2, u, :])
        acc_g[...] += dot(g_gate, wbuf[0, u, :]) + dot(g_up, wbuf[1, u, :])

        @pl.when(c >= 2)
        def _():
            out_copy(0, slot, keep_ref, 0).wait()

        stage[slot, 0] = dot_tn(g_gate, a).astype(BF16)
        stage[slot, 1] = dot_tn(g_up, a).astype(BF16)
        stage[slot, 2] = dot_tn(hid, cot_ref[...]).astype(BF16)

        @pl.when(c < half_chunks)
        def _():
            out_copy(c, slot, keep_ref, 0).start()

        @pl.when(c >= half_chunks)
        def _():
            out_copy(c, slot, send_ref, half_chunks).start()

        return 0

    lax.fori_loop(0, n_chunks, chunk, 0)
    out_copy(0, 0, keep_ref, 0).wait()
    out_copy(0, 1, keep_ref, 0).wait()

    def last(i, total):
        r = pl.ds(pl.multiple_of(i * ROWS, ROWS), ROWS)
        h = h1[r, :]
        factor = lax.rsqrt(jnp.mean(h * h, axis=-1, keepdims=True) + NORM_EPS)
        normed = h * factor
        g = acc_g[r, :]
        out_ref[r, :] = acc_o[r, :].astype(BF16)
        scaled = g * gain
        back = factor * (scaled - normed * jnp.mean(scaled * normed, axis=-1, keepdims=True))
        full = cot_ref[r, :].astype(F32) + back
        gh_ref[r, :] = full
        res = full.astype(BF16)
        low[r, :] = res
        gm_ref[r, :] = dot_nt(res, w_out[:, :D]).astype(BF16)
        return total + jnp.sum(g * normed, axis=0, keepdims=True)

    gain_grad = lax.fori_loop(0, steps, last, jnp.zeros((1, D), F32))
    product = dot_tn(mid_ref[...], low[...])
    put_shards(z, go_ref, product, gain_grad, 0)


def put_shards(z, ref, product, gain_grad, lead):
    width = product.shape[1]
    first_row = lax.broadcasted_iota(jnp.int32, (ZP - ZR, width), 0) == 0
    for n in range(4):
        s = lax.rem(z - n + 4, 4)
        ref[s, 0:ZR, :] = product[ZR * n : ZR * n + ZR].astype(BF16)
        if gain_grad is None:
            ref[s, ZR:ZP, :] = jnp.zeros((ZP - ZR, width), BF16)
        else:
            part = jnp.concatenate(
                [gain_grad[:, ZR * n : ZR * n + ZR], jnp.zeros((1, width - ZR), F32)], axis=1
            )
            ref[s, ZR:ZP, :] = jnp.where(first_row, part, 0.0).astype(BF16)


def mid_call(info, mid, x, cot, gain, w, pieces):
    t = x.shape[0]
    units = sum(p.shape[1] for p in pieces)
    wide = jax.ShapeDtypeStruct((t, D), BF16)
    half = jax.ShapeDtypeStruct((3, units // 2, D), BF16)
    return pl.pallas_call(
        mid_kernel,
        out_shape=(
            wide,
            jax.ShapeDtypeStruct((t, D), F32),
            wide,
            jax.ShapeDtypeStruct((4, ZP, D), BF16),
            half,
            half,
        ),
        in_specs=[SMEM] + [VMEM] * 4 + [ANY] * 11,
        out_specs=(VMEM,) * 4 + (ANY,) * 2,
        scratch_shapes=[
            pltpu.VMEM((D, 1024), BF16),
            pltpu.VMEM((3, units, D), BF16),
            pltpu.VMEM((t, D), F32),
            pltpu.VMEM((t, D), BF16),
            pltpu.VMEM((t, D), F32),
            pltpu.VMEM((t, D), F32),
            pltpu.VMEM((2, 3, UNITS, D), BF16),
            pltpu.SemaphoreType.DMA((11,)),
            pltpu.SemaphoreType.DMA((2,)),
        ],
        compiler_params=params(60),
        cost_estimate=cost(2 * t * D * (9 * units + 3 * D), 45e6),
        name="feed_forward",
    )(info, mid, x, cot, gain, w, *pieces)


def post_q_kernel(info, a_ref, qg_ref, w_ref, gq_ref, part_ref):
    put_shards(info[0], gq_ref, dot_tn(a_ref[...], qg_ref[...]), None, 0)
    part_ref[...] = dot_nt(qg_ref[...], w_ref[0, :, :D])


def post_q_call(info, a, qg, w):
    t = a.shape[0]
    return pl.pallas_call(
        post_q_kernel,
        out_shape=(
            jax.ShapeDtypeStruct((4, ZP, D), BF16),
            jax.ShapeDtypeStruct((t, D), F32),
        ),
        in_specs=[SMEM] + [VMEM] * 3,
        out_specs=(VMEM,) * 2,
        compiler_params=params(40),
        cost_estimate=cost(4 * t * D * D, 14e6),
        name="query_back",
    )(info, a, qg, w)


def post_kv_kernel(
    info, s0, s1, s2, cos_ref, sin_ref, a_ref, part_ref, w_ref, x_ref, gh_ref, gain_ref,
    keep_ref, send_ref, ig_ref, kg, vg,
):
    z, core = info[0], info[1]
    first_half, low_head = lane_masks(ROWS)
    steps = x_ref.shape[0] // ROWS
    gain = gain_ref[...]

    def body(i, total):
        r = pl.ds(pl.multiple_of(i * ROWS, ROWS), ROWS)

        def slab(j):
            c = slice(128 * j, 128 * j + 128)
            return s0[r, c].astype(F32) + s1[r, c].astype(F32) + s2[r, c].astype(F32)

        cos, sin = cos_ref[r, :], -sin_ref[r, :]
        mixed = slab(2)
        k4 = jnp.where(low_head, 0.0, rope_slab(pltpu.roll(mixed, 64, 1), cos, sin, first_half))
        k_low = jnp.concatenate(
            [k4, rope_slab(slab(0), cos, sin, first_half), rope_slab(slab(1), cos, sin, first_half)],
            axis=1,
        ).astype(BF16)
        v_low = jnp.concatenate(
            [jnp.where(low_head, 0.0, mixed), slab(3), slab(4)], axis=1
        ).astype(BF16)
        kg[r, :] = k_low
        vg[r, :] = v_low
        g = (
            part_ref[r, :]
            + dot_nt(k_low, w_ref[0, :, 896:1280])
            + dot_nt(v_low, w_ref[1, :, 896:1280])
        )
        x = x_ref[r, :].astype(F32)
        factor = lax.rsqrt(jnp.mean(x * x, axis=-1, keepdims=True) + NORM_EPS)
        normed = x * factor
        scaled = g * gain
        back = factor * (scaled - normed * jnp.mean(scaled * normed, axis=-1, keepdims=True))
        ig_ref[r, :] = (gh_ref[r, :] + back).astype(BF16)
        return total + jnp.sum(g * normed, axis=0, keepdims=True)

    gain_grad = lax.fori_loop(0, steps, body, jnp.zeros((1, D), F32))
    mine = core == 0
    k_side = dot_tn(a_ref[...], kg[...])
    v_side = dot_tn(a_ref[...], vg[...])
    put_shards(z, keep_ref, jnp.where(mine, k_side, v_side), jnp.where(mine, gain_grad, 0.0), 0)
    put_shards(z, send_ref, jnp.where(mine, v_side, k_side), jnp.where(mine, 0.0, gain_grad), 0)


def post_kv_call(info, sums, cos, sin, a, part, w, x, gh, gain):
    t = x.shape[0]
    piece = jax.ShapeDtypeStruct((4, ZP, 384), BF16)
    return pl.pallas_call(
        post_kv_kernel,
        out_shape=(piece, piece, jax.ShapeDtypeStruct((t, D), BF16)),
        in_specs=[SMEM] + [VMEM] * 11,
        out_specs=(VMEM,) * 3,
        scratch_shapes=[pltpu.VMEM((t, 384), BF16), pltpu.VMEM((t, 384), BF16)],
        compiler_params=params(50),
        cost_estimate=cost(8 * t * D * 384, 25e6),
        name="key_value_back",
    )(info, *sums, cos, sin, a, part, w, x, gh, gain)


def z_shift(x, step):
    n = 4
    return lax.ppermute(x, "fsdp", [(i, (i + step) % n) for i in range(n)])


def c_swap(x, bit):
    n = lax.axis_size("ctx")
    return lax.ppermute(x, "ctx", [(i, i ^ bit) for i in range(n)])


def z_gather(mine, axis):
    up, dn = z_shift(mine, 1), z_shift(mine, -1)
    cut = mine.shape[axis] // 2
    t1 = z_shift(lax.slice_in_dim(up, 0, cut, axis=axis), 1)
    t2 = z_shift(lax.slice_in_dim(dn, cut, 2 * cut, axis=axis), -1)
    return up, dn, t1, t2


def z_reduce(s0, s1, s2, s3):
    axis = s0.ndim - 2
    cut = s0.shape[axis] // 2
    r1 = z_shift(lax.slice_in_dim(s2, 0, cut, axis=axis), -1)
    r3 = z_shift(lax.slice_in_dim(s2, cut, 2 * cut, axis=axis), 1)

    def join(left, right):
        return jnp.concatenate([left, right], axis=axis)

    lo1, hi1 = lax.slice_in_dim(s1, 0, cut, axis=axis), lax.slice_in_dim(s1, cut, 2 * cut, axis=axis)
    lo3, hi3 = lax.slice_in_dim(s3, 0, cut, axis=axis), lax.slice_in_dim(s3, cut, 2 * cut, axis=axis)
    f1 = z_shift(join(lo1 + r1, hi1), -1)
    f3 = z_shift(join(lo3, hi3 + r3), 1)
    return s0 + f1 + f3


def chips_sum(x):
    n = lax.axis_size("ctx")
    bits = []
    b = 2
    while b < n:
        bits.append(b)
        b *= 2
    axis = x.ndim - 2
    cut = x.shape[axis] // 2
    left = lax.slice_in_dim(x, 0, cut, axis=axis)
    right = lax.slice_in_dim(x, cut, 2 * cut, axis=axis)
    for b in bits:
        left = left + c_swap(left, b)
    for b in reversed(bits):
        right = right + c_swap(right, b)
    return jnp.concatenate([left, right], axis=axis)


def gather_kv(kv):
    n = lax.axis_size("ctx")
    if n != 8:
        return [lax.all_gather(kv, "ctx", axis=0, tiled=True)]
    cut = kv.shape[0] // 2
    across_x, across_y = c_swap(kv, 2), c_swap(kv, 4)
    far_lo = c_swap(across_x[:cut], 4)
    far_hi = c_swap(across_y[cut:], 2)
    chip = [kv, across_x, across_y, far_lo, far_hi]
    return chip + [c_swap(part, 1) for part in chip]


def kv_entry(position, per_dev, me, n):
    if n != 8:
        return position
    owner, within = position // per_dev, position % per_dev
    rel = owner ^ me
    cut = per_dev // 2
    far = (rel // 2) == 3
    late = far & (within >= cut)
    which = (rel % 2) * 5 + rel // 2 + late.astype(jnp.int32)
    return which * 1024 + jnp.where(late, within - cut, within)


def kv_slot(position, per_dev, me):
    owner, within = position // per_dev, position % per_dev
    rel = owner ^ me
    return ((rel % 2) * 4 + rel // 2) * per_dev + within


def return_kv(keep, send):
    rows = keep.shape[0] // 4
    cut = rows // 2
    total = keep + c_swap(send, 1)
    own, to_x, to_y, far = (total[rows * j : rows * j + rows] for j in range(4))
    from_x = c_swap(far[:cut], 2)
    from_y = c_swap(far[cut:], 4)
    to_y = jnp.concatenate([to_y[:cut] + from_x, to_y[cut:]], axis=0)
    to_x = jnp.concatenate([to_x[:cut], to_x[cut:] + from_y], axis=0)
    return own, c_swap(to_x, 2), c_swap(to_y, 4)


def on_device(
    tokens,
    cotangent,
    doc_lengths,
    deal,
    attn_gain,
    w_query,
    w_key,
    w_value,
    w_out,
    mlp_gain,
    w_gate,
    w_up,
    w_down,
):
    me = lax.axis_index("ctx")
    n_ctx = lax.axis_size("ctx")
    z = lax.axis_index("fsdp")
    core = me % 2
    even = core == 0
    info = jnp.stack([z, core]).astype(jnp.int32)
    tok_rows = tokens.shape[1]
    per_dev = tok_rows // BLK
    deal_row = deal[0]
    blocks = deal_row.shape[0]
    group_size = blocks * BLK
    doc_lens = doc_lengths[0]
    seq_count = doc_lens.shape[0]
    length = group_size // seq_count
    x = tokens[0]
    cot = cotangent[0]

    k_last, k_rest = w_key[:, 256:], w_key[:, :256]
    v_last, v_rest = w_value[:, 256:], w_value[:, :256]
    side_a = jnp.concatenate([w_query, k_last, k_rest], axis=1)
    side_b = jnp.concatenate([w_out, v_last, v_rest], axis=1)
    mine_ab = jnp.where(even, side_a, side_b)
    got = z_gather(mine_ab, 1)
    swapped = [c_swap(p, 1) for p in got]
    pieces_ab = [side_a, side_b, *got, *swapped]

    gains = jnp.stack([attn_gain, mlp_gain])
    rel_gains = jnp.stack([gains, z_shift(gains, 1), z_shift(gains, 2), z_shift(gains, 3)])
    rel_of = (z - jnp.arange(4, dtype=jnp.int32)) % 4
    pick = rel_of[:, None] == jnp.arange(4, dtype=jnp.int32)[None, :]
    full_gains = jnp.sum(
        jnp.where(pick[:, :, None, None], rel_gains[None].astype(F32), 0.0), axis=1
    )
    gain_one = full_gains[:, 0].reshape(1, D)
    gain_two = full_gains[:, 1].reshape(1, D)

    block_ids = jnp.arange(blocks, dtype=jnp.int32)
    mine = lax.dynamic_slice_in_dim(deal_row, me * per_dev, per_dev)
    seq_blocks = jnp.maximum(
        mine[:, None] - (NWB - 1) + jnp.arange(NWB, dtype=jnp.int32)[None, :], 0
    )
    position = jnp.sum(
        jnp.where(seq_blocks[:, :, None] == deal_row[None, None, :], block_ids, 0), axis=-1
    )
    tab = kv_entry(position, per_dev, me, n_ctx).astype(jnp.int32)
    doc_ends = (
        jnp.cumsum(doc_lens, axis=1) + (jnp.arange(seq_count, dtype=jnp.int32) * length)[:, None]
    ).reshape(-1)
    doc_starts = doc_ends - doc_lens.reshape(-1)
    q_time = mine[:, None] * BLK + jnp.arange(BLK, dtype=jnp.int32)[None, :]
    begin = jnp.max(jnp.where(q_time[..., None] >= doc_starts, doc_starts, 0), axis=-1)
    lo = jnp.maximum(begin, q_time - (WIN - 1)) - (mine[:, None] * BLK - WIN)
    lo = lo[:, None, :].astype(jnp.int32)
    pos = (q_time - begin).reshape(-1)
    half_dim = HD // 2
    freqs = ROPE_THETA ** (-jnp.arange(half_dim, dtype=F32) * (2.0 / HD))
    angle = pos.astype(F32)[:, None] * freqs[None, :]
    cos_tab, sin_tab = jnp.cos(angle), jnp.sin(angle)
    cos_wide = jnp.tile(cos_tab, (1, 4))
    sin_wide = jnp.tile(jnp.concatenate([-sin_tab, sin_tab], axis=1), (1, 2))
    cos_turn = cos_tab.reshape(per_dev, BLK, half_dim).transpose(0, 2, 1)
    sin_turn = sin_tab.reshape(per_dev, BLK, half_dim).transpose(0, 2, 1)

    attn_in, q_low, kv_low, w_ab = pre_call(info, x, gain_one, cos_wide, sin_wide, pieces_ab)

    stacked = jnp.stack([w_gate.T, w_up.T, w_down])
    unit_half = stacked.shape[1] // 2
    ffn_mine = jnp.where(even, stacked[:, :unit_half], stacked[:, unit_half:])
    ffn_other = jnp.where(even, stacked[:, unit_half:], stacked[:, :unit_half])
    up, dn, t1, t2 = z_gather(ffn_mine, 1)
    near = [up, t1, t2, dn]
    pieces_ffn = [ffn_mine, *near, ffn_other, *[c_swap(p, 1) for p in near]]

    kvs = gather_kv(kv_low)
    mid_low, recips, probs = fwd_call(tab, lo, q_low, kvs)
    output, grad_hidden, grad_mid, go, keep, send = mid_call(
        info, mid_low, x, cot, gain_two, w_ab, pieces_ffn
    )

    both = keep + c_swap(send, 1)
    parts = [both[:, unit_half * s : unit_half * s + unit_half] for s in range(4)]
    ffn_sum = chips_sum(z_reduce(*parts))

    if n_ctx == 8:
        slots = kv_slot(position, per_dev, me).astype(jnp.int32)
        q_grad, kv_keep, kv_send = bwd_call(
            tab, slots, blocks, 2, q_low, grad_mid, mid_low, recips, probs, cos_turn, sin_turn, kvs
        )
        sums = return_kv(kv_keep, kv_send)
    else:
        n_slots = per_dev * NWB
        flat_pos = position.reshape(-1)
        order = jnp.arange(n_slots, dtype=jnp.int32)
        slots = jnp.min(
            jnp.where(flat_pos[:, None] == flat_pos[None, :], order[None, :], n_slots), axis=1
        ).reshape(per_dev, NWB)
        q_grad, compact = bwd_call(
            tab, slots, n_slots, 1, q_low, grad_mid, mid_low, recips, probs, cos_turn, sin_turn, kvs
        )
        source = jnp.min(
            jnp.where(block_ids[:, None] == flat_pos[None, :], order[None, :], n_slots), axis=1
        )
        padded = jnp.concatenate(
            [compact.reshape(n_slots, BLK, 2 * KVW), jnp.zeros((1, BLK, 2 * KVW), BF16)], axis=0
        )
        spread = jnp.take(padded, source, axis=0).reshape(group_size, 2 * KVW)
        own = lax.psum_scatter(spread, "ctx", scatter_dimension=0, tiled=True)
        sums = (own, jnp.zeros_like(own), jnp.zeros_like(own))

    gq, part = post_q_call(info, attn_in, q_grad, w_ab)
    both_qo = jnp.where(even, gq, go) + c_swap(jnp.where(even, go, gq), 1)
    qo_sum = chips_sum(z_reduce(*(both_qo[s] for s in range(4))))

    kv_g_keep, kv_g_send, input_grad = post_kv_call(
        info, sums, cos_wide, sin_wide, attn_in, part, w_ab, x, grad_hidden, gain_one
    )
    both_kv = kv_g_keep + c_swap(kv_g_send, 1)
    kv_sum = chips_sum(z_reduce(*(both_kv[s] for s in range(4))))

    ffn_far = c_swap(ffn_sum, 1)
    ffn_full = jnp.where(
        even,
        jnp.concatenate([ffn_sum, ffn_far], axis=1),
        jnp.concatenate([ffn_far, ffn_sum], axis=1),
    ).astype(F32)
    qo_far = c_swap(qo_sum, 1)
    q_final = jnp.where(even, qo_sum, qo_far).astype(F32)
    o_final = jnp.where(even, qo_far, qo_sum).astype(F32)
    kv_far = c_swap(kv_sum, 1)
    k_final = jnp.where(even, kv_sum, kv_far).astype(F32)
    v_final = jnp.where(even, kv_far, kv_sum).astype(F32)

    def heads_back(arr):
        return jnp.concatenate([arr[:ZR, 128:384], arr[:ZR, 64:128]], axis=1)

    return (
        output[None],
        input_grad[None],
        k_final[ZR, :ZR],
        q_final[:ZR],
        heads_back(k_final),
        heads_back(v_final),
        o_final[:ZR],
        o_final[ZR, :ZR],
        ffn_full[0].T,
        ffn_full[1].T,
        ffn_full[2],
    )


def solution(mesh):
    in_specs = (
        P("fsdp", "ctx", None),
        P("fsdp", "ctx", None),
        P("fsdp", None, None),
        P("fsdp", None),
        P("fsdp"),
        P("fsdp", None),
        P("fsdp", None),
        P("fsdp", None),
        P("fsdp", None),
        P("fsdp"),
        P(None, "fsdp"),
        P(None, "fsdp"),
        P("fsdp", None),
    )
    out_specs = (
        P("fsdp", "ctx", None),
        P("fsdp", "ctx", None),
        P("fsdp"),
        P("fsdp", None),
        P("fsdp", None),
        P("fsdp", None),
        P("fsdp", None),
        P("fsdp"),
        P(None, "fsdp"),
        P(None, "fsdp"),
        P("fsdp", None),
    )
    return jax.shard_map(
        on_device, mesh=mesh, in_specs=in_specs, out_specs=out_specs, check_vma=False
    )
```

```python
import jax
import jax.numpy as jnp
from jax import lax
from jax.experimental import pallas as pl
from jax.experimental.pallas import tpu as pltpu
from jax.sharding import PartitionSpec as P

HQ = 15
KVH = 5
HD = 64
BLK = 128
WIN = 1024
D = 960
GRP = HQ // KVH
SPAN = WIN + BLK
NWB = SPAN // BLK
ROWS = 256
ZR = 240
ZP = 256
UNITS = 256
WIDE = 1024
QKV = 1664

NORM_EPS = 1e-05
ROPE_THETA = 100000.0
MASK_FILL = -1e30
F32 = jnp.float32
BF16 = jnp.bfloat16
MIB = 1024 * 1024

VMEM = pl.BlockSpec(memory_space=pltpu.VMEM)
SMEM = pl.BlockSpec(memory_space=pltpu.SMEM)
ANY = pl.BlockSpec(memory_space=pl.ANY)

KV_LANES = 640
PAIRS = (
    (0, 3, (0, 1), True, True),
    (1, 4, (2, 3), True, True),
    (2, 2, (4,), False, True),
)

CORE_UNITS = 320
QUARTER = 160
OUT_ROWS = 64
OUT_AT = 3 * QUARTER
PACKED = OUT_AT + OUT_ROWS
CUT = 3 * PACKED // 2

P_ROWS = 128
Q_ROWS = 48
SEG = 64


def dot(a, b):
    return jnp.dot(a, b, preferred_element_type=F32)


def dot_nt(a, b):
    return lax.dot_general(a, b, (((1,), (1,)), ((), ())), preferred_element_type=F32)


def dot_tn(a, b):
    return lax.dot_general(a, b, (((0,), (0,)), ((), ())), preferred_element_type=F32)


def params(mib, grid_dims=0):
    return pltpu.CompilerParams(
        vmem_limit_bytes=mib * MIB,
        dimension_semantics=("arbitrary",) * grid_dims if grid_dims else None,
    )


def cost(flops, moved, exps=0):
    return pl.CostEstimate(flops=1, bytes_accessed=1, transcendentals=0)


def rope_slab(t, cos, sin_signed, first_half):
    swapped = jnp.where(first_half, pltpu.roll(t, 96, 1), pltpu.roll(t, 32, 1))
    return t * cos + swapped * sin_signed


def lane_masks(rows):
    lane = lax.broadcasted_iota(jnp.int32, (rows, 128), 1)
    return (lane % HD) < HD // 2, lane < HD


def rel_z(z, i):
    return lax.rem(z + 1 + i, 4)


def each(found, act):
    for cond, c in found:
        if cond is None:
            act(c)
        else:
            pl.when(cond)(lambda c=c: act(c))


def start(c):
    c.start()


def wait(c):
    c.wait()


def run_copies(pairs, sems):
    copies = [pltpu.make_async_copy(a, b, sems.at[i]) for i, (a, b) in enumerate(pairs)]
    for c in copies:
        c.start()
    for c in copies:
        c.wait()


def step_call(
    name, body, info, ins, outs, moved, where=None, out_where=None, scratch=(), aliases=None
):
    n_in, n_out = len(ins), len(outs)

    def kernel(info_ref, *refs):
        body(info_ref, refs[:n_in], refs[n_in : n_in + n_out], refs[n_in + n_out :])

    return pl.pallas_call(
        kernel,
        out_shape=tuple(jax.ShapeDtypeStruct(shape, dtype) for shape, dtype in outs),
        in_specs=[SMEM] + list(where or [VMEM] * n_in),
        out_specs=tuple(out_where or [VMEM] * n_out),
        scratch_shapes=list(scratch),
        input_output_aliases=aliases or {},
        compiler_params=params(40),
        cost_estimate=cost(1e6, moved),
        name=name,
    )(info, *ins)


def prep_weights(info, w_gate, w_up, w_down_turned, w_out):
    def body(info, ins, outs, scratch):
        core, parity = info[1], info[4]
        own, packed = outs
        turn = scratch[0]
        row = jnp.minimum(OUT_ROWS * (2 * core + parity), ZR - OUT_ROWS)
        packed[OUT_AT:PACKED, :] = ins[3][pl.ds(pl.multiple_of(row, 16), OUT_ROWS), :]
        base = core * CORE_UNITS
        for n in range(3):
            turn[...] = ins[n][...].T
            own[n] = turn[pl.ds(pl.multiple_of(base, 16), CORE_UNITS), :]
            quarter = pl.ds(pl.multiple_of(base + QUARTER * parity, 16), QUARTER)
            packed[QUARTER * n : QUARTER * n + QUARTER, :] = turn[quarter, :]

    return step_call(
        "prep_weights",
        body,
        info,
        (w_gate, w_up, w_down_turned, w_out),
        (((3, CORE_UNITS, D), BF16), ((PACKED, D), BF16)),
        8e6,
        scratch=(pltpu.VMEM((2 * CORE_UNITS, D), BF16),),
    )


def stack_weights(info, parts, packed):
    def body(info, ins, outs, scratch):
        c = pltpu.make_async_copy(ins[3], outs[1], scratch[0])
        c.start()
        for n in range(3):
            outs[0][n] = ins[n][...]
        c.wait()

    return step_call(
        "stack_weights",
        body,
        info,
        (*parts, packed),
        (((3,) + parts[0].shape, BF16), (packed.shape, BF16)),
        4e6,
        [VMEM] * 3 + [ANY],
        [VMEM, ANY],
        scratch=(pltpu.SemaphoreType.DMA,),
    )


def split_quarters(info, over_z, deps):
    at = CUT - PACKED

    def body(info, ins, outs, scratch):
        src = ins[0]
        z = info[0]
        zs = [rel_z(z, i) for i in range(3)]
        pairs = [
            (src.at[zs[0]], outs[0].at[pl.ds(0, PACKED)]),
            (src.at[zs[1], pl.ds(0, at)], outs[0].at[pl.ds(PACKED, at)]),
            (src.at[zs[1], pl.ds(at, PACKED - at)], outs[1].at[pl.ds(0, PACKED - at)]),
            (src.at[zs[2]], outs[1].at[pl.ds(PACKED - at, PACKED)]),
        ]
        pairs += [(src.at[zs[i], pl.ds(OUT_AT, OUT_ROWS)], outs[2].at[i]) for i in range(3)]
        run_copies(pairs, scratch[0])

    half = (CUT, D)
    return step_call(
        "split_quarters",
        body,
        info,
        (over_z, *deps),
        ((half, BF16), (half, BF16), ((3, OUT_ROWS, D), BF16)),
        8e6,
        [ANY] * (1 + len(deps)),
        [ANY] * 3,
        scratch=(pltpu.SemaphoreType.DMA((7,)),),
    )


def pick_out_rows(info, first_on, second_on, dep):
    def body(info, ins, outs, scratch):
        rows = (OUT_AT, PACKED + OUT_AT - CUT, 2 * PACKED + OUT_AT - CUT)
        pairs = [
            (ins[min(i, 1)].at[pl.ds(row, OUT_ROWS)], outs[0].at[i]) for i, row in enumerate(rows)
        ]
        run_copies(pairs, scratch[0])

    return step_call(
        "pick_out_rows",
        body,
        info,
        (first_on, second_on, dep),
        (((3, OUT_ROWS, D), BF16),),
        1e6,
        [ANY] * 3,
        [ANY],
        scratch=(pltpu.SemaphoreType.DMA((3,)),),
    )[0]


def pre_kernel(info, xt_ref, cos_ref, sin_ref, *refs):
    own, pieces = refs[0], refs[1:9]
    attn_ref, q_ref, kv_ref, w_ref, gains_ref, x_ref, cos_t, sin_t, sems = refs[9:]
    z, me = info[0], info[2]
    found = []

    def add(src, row, size, cond=None):
        view = w_ref.at[pl.ds(pl.multiple_of(row, 16), size)]
        found.append((cond, pltpu.make_async_copy(src, view, sems.at[len(found)])))

    add(own, z * ZR, ZR)
    for rel, piece in enumerate(pieces):
        c = me ^ rel
        for i in range(3):
            base = rel_z(z, i) * ZR
            add(piece.at[i, pl.ds(0, 16)], base + 32 * c, 16, c < 7)
            add(piece.at[i, pl.ds(16, 16)], base + jnp.minimum(32 * c + 16, ZR - 16), 16)
    each(found, start)
    steps = x_ref.shape[0] // ROWS
    cos_t[...] = cos_ref[...].T[0:32]
    sin_t[...] = sin_ref[...].T[32:64]

    def turn(i, _):
        r = pl.ds(pl.multiple_of(i * ROWS, ROWS), ROWS)
        x_ref[r, :] = xt_ref[:, r].T
        return 0

    lax.fori_loop(0, steps, turn, 0)
    each(found, wait)
    gains_ref[...] = w_ref[:, 1536:QKV].astype(F32).T[64:72]
    first_half, low_head = lane_masks(ROWS)

    def body(i, _):
        r = pl.ds(pl.multiple_of(i * ROWS, ROWS), ROWS)
        x = x_ref[r, :].astype(F32)
        factor = lax.rsqrt(jnp.mean(x * x, axis=-1, keepdims=True) + NORM_EPS)
        a = (x * factor * gains_ref[0:1, :]).astype(BF16)
        attn_ref[r, :] = a
        qk = dot(a, w_ref[:, 0:1280])
        vv = dot(a, w_ref[:, 1280:QKV])
        cos, sin = cos_ref[r, :], sin_ref[r, :]
        slabs = [
            rope_slab(qk[:, 128 * j : 128 * j + 128], cos, sin, first_half) for j in range(10)
        ]
        for j in range(7):
            q_ref[r, 128 * j : 128 * j + 128] = slabs[j].astype(BF16)
        q_ref[r, 896:960] = slabs[7][:, :64].astype(BF16)
        mixed = jnp.where(low_head, vv[:, 256:384], slabs[7])
        for j, part in enumerate((slabs[8], slabs[9], mixed, vv[:, 0:128], vv[:, 128:256])):
            kv_ref[r, 128 * j : 128 * j + 128] = part.astype(BF16)
        return 0

    lax.fori_loop(0, steps, body, 0)


def pre_call(info, xt, cos, sin, pieces):
    t = xt.shape[1]
    return pl.pallas_call(
        pre_kernel,
        out_shape=(
            jax.ShapeDtypeStruct((t, D), BF16),
            jax.ShapeDtypeStruct((t, D), BF16),
            jax.ShapeDtypeStruct((t, KV_LANES), BF16),
            jax.ShapeDtypeStruct((D, QKV), BF16),
            jax.ShapeDtypeStruct((8, D), F32),
            jax.ShapeDtypeStruct((t, D), BF16),
            jax.ShapeDtypeStruct((32, t), F32),
            jax.ShapeDtypeStruct((32, t), F32),
        ),
        in_specs=[SMEM] + [VMEM] * 3 + [ANY] * 9,
        out_specs=(VMEM,) * 8,
        scratch_shapes=[pltpu.SemaphoreType.DMA((49,))],
        compiler_params=params(40),
        cost_estimate=cost(2 * t * D * QKV, 13e6),
        name="pre",
    )(info, xt, cos, sin, *pieces)


def start_window(tab, kvs, win, sem, blk, slot):
    def body(j, _):
        entry = tab[blk, j]
        which = entry // 1024
        idx = lax.rem(entry, 1024)
        dst = win.at[slot, pl.ds(pl.multiple_of(j * BLK, BLK), BLK)]
        for n, ref in enumerate(kvs):
            @pl.when(which == n)
            def _():
                src = ref.at[pl.ds(pl.multiple_of(idx * BLK, BLK), BLK)]
                pltpu.make_async_copy(src, dst, sem.at[slot]).start()
        return 0

    lax.fori_loop(0, NWB, body, 0)


def next_window(tab, kvs, win, sem, first=0):
    i = pl.program_id(0)
    slot = lax.rem(i, 2)

    @pl.when(i == 0)
    def _():
        start_window(tab, kvs, win, sem, i + first, slot)

    @pl.when(i + 1 < pl.num_programs(0))
    def _():
        start_window(tab, kvs, win, sem, i + first + 1, 1 - slot)

    pltpu.make_async_copy(win.at[slot], win.at[slot], sem.at[slot]).wait()
    return slot


def turned(flat):
    rows = flat.astype(F32)
    extra = -rows.shape[1] % 128
    if extra:
        rows = jnp.concatenate([rows, jnp.zeros((rows.shape[0], extra), F32)], axis=1)
    return rows.T


def unturned(parts):
    rows = sum(p.shape[0] for p in parts)
    extra = -rows % 128
    if extra:
        parts = parts + [jnp.zeros((extra, parts[0].shape[1]), F32)]
    return jnp.concatenate(parts, axis=0).T[:, :rows].astype(BF16)


def spread_heads(rows, count, low):
    width = GRP * BLK
    sides = [jnp.concatenate(rows[GRP * n : GRP * n + GRP], axis=1) for n in range(count)]
    empty = jnp.zeros((HD, width), rows[0].dtype)
    if count == 2:
        return jnp.concatenate(
            [jnp.concatenate([sides[0], empty], axis=1), jnp.concatenate([empty, sides[1]], axis=1)],
            axis=0,
        )
    return jnp.concatenate([sides[0], empty] if low else [empty, sides[0]], axis=0)


def head_half(j, kv_heads, low):
    upper = j >= GRP if len(kv_heads) == 2 else not low
    return HD if upper else 0


def fwd_kernel(n_kv, tab, lo_ref, q_ref, *refs):
    kvs = refs[:n_kv]
    mid_ref, rl_ref, p_ref, win, bias, scores, sem = refs[n_kv:]
    slot = next_window(tab, kvs, win, sem)
    row = lax.broadcasted_iota(jnp.int32, (SPAN, BLK), 0)
    lane = lax.broadcasted_iota(jnp.int32, (SPAN, BLK), 1)
    allowed = (row >= lo_ref[0]) & (row <= lane + WIN)
    bias[...] = jnp.where(allowed, 0.0, MASK_FILL)
    q_all = (turned(q_ref[...]) * (HD ** -0.5)).astype(BF16)
    outs, recips = [], []
    at = 0
    for k_slab, v_slab, kv_heads, k_low, v_low in PAIRS:
        keys = win[slot, :, 128 * k_slab : 128 * k_slab + 128]
        vals = win[slot, :, 128 * v_slab : 128 * v_slab + 128]
        count = GRP * len(kv_heads)
        width = BLK * count
        base = BLK * at
        q_rows = [q_all[HD * (at + j) : HD * (at + j) + HD] for j in range(count)]
        scores[:, :width] = dot(keys, spread_heads(q_rows, len(kv_heads), k_low))
        for j in range(count):
            s = scores[:, BLK * j : BLK * j + BLK] + bias[...]
            top = jnp.max(s, axis=0, keepdims=True)
            p_ref[0, :, base + BLK * j : base + BLK * j + BLK] = jnp.exp(s - top).astype(BF16)
        lhs = jnp.concatenate([vals.T, jnp.ones((16, SPAN), BF16)], axis=0)
        product = dot(lhs, p_ref[0, :, base : base + width])
        recip = 1.0 / product[128:129, :]
        for j in range(count):
            cols = slice(BLK * j, BLK * j + BLK)
            half = head_half(j, kv_heads, v_low)
            outs.append(product[half : half + HD, cols] * recip[:, cols])
            recips.append(recip[:, cols])
        at += count
    mid_ref[...] = unturned(outs)
    recips.append(jnp.zeros((16 - len(recips), BLK), F32))
    rl_ref[0] = jnp.concatenate(recips, axis=0)


def fwd_call(tab, lo, q, kvs):
    blocks = q.shape[0] // BLK
    n_kv = len(kvs)
    lanes, heads = D, HQ
    return pl.pallas_call(
        lambda *refs: fwd_kernel(n_kv, *refs),
        grid=(blocks,),
        out_shape=(
            jax.ShapeDtypeStruct((q.shape[0], lanes), BF16),
            jax.ShapeDtypeStruct((blocks, 16, BLK), F32),
            jax.ShapeDtypeStruct((blocks, SPAN, heads * BLK), BF16),
        ),
        in_specs=[
            SMEM,
            pl.BlockSpec((1, 1, BLK), lambda i: (i, 0, 0)),
            pl.BlockSpec((BLK, lanes), lambda i: (i, 0)),
        ]
        + [ANY] * n_kv,
        out_specs=(
            pl.BlockSpec((BLK, lanes), lambda i: (i, 0)),
            pl.BlockSpec((1, 16, BLK), lambda i: (i, 0, 0)),
            pl.BlockSpec((1, SPAN, heads * BLK), lambda i: (i, 0, 0)),
        ),
        scratch_shapes=[
            pltpu.VMEM((2, SPAN, KV_LANES), BF16),
            pltpu.VMEM((SPAN, BLK), F32),
            pltpu.VMEM((SPAN, 2 * GRP * BLK), F32),
            pltpu.SemaphoreType.DMA((2,)),
        ],
        compiler_params=params(48, 1),
        cost_estimate=cost(0.5e9 * heads * blocks, 0.5e6 * heads * blocks, 0.15e6 * heads * blocks),
        name="attend",
    )(tab, lo, q, *kvs)


def bwd_kernel(
    n_kv, n_dep, first, prev, out_units, n_slots, tab, slots, q_ref, do_ref, mid_ref, rl_ref, p_ref, cos_ref, sin_ref, *refs
):
    kvs = refs[:n_kv]
    n_out = len(out_units)
    refs = refs[n_kv + n_dep :]
    earlier = refs[:n_out] if prev else ()
    refs = refs[len(earlier) :]
    dq_ref = refs[0]
    outs = refs[1 : 1 + n_out]
    win, acc, scores, stage, stage_in, sem, out_sem, in_sem = refs[1 + n_out :]
    i = pl.program_id(0)
    blk = i + first
    slot = next_window(tab, kvs, win, sem, first)
    lanes = acc.shape[1]

    @pl.when(i == 0)
    def _():
        def clear(b, _):
            acc[pl.ds(pl.multiple_of(b * BLK, BLK), BLK), :] = jnp.zeros((BLK, lanes), F32)
            return 0

        lax.fori_loop(0, n_slots, clear, 0)

    def add(slab, value):
        for j in range(NWB):
            r = pl.ds(pl.multiple_of(slots[blk, j] * BLK, BLK), BLK)
            acc[r, 128 * slab : 128 * slab + 128] += value[BLK * j : BLK * j + BLK]

    q_all = (turned(q_ref[...]) * (HD ** -0.5)).astype(BF16)
    do_all = turned(do_ref[...])
    o_all = turned(mid_ref[...])
    cos, sin = cos_ref[...], sin_ref[...]
    grads = []
    at = 0
    for k_slab, v_slab, kv_heads, k_low, v_low in PAIRS:
        keys = win[slot, :, 128 * k_slab : 128 * k_slab + 128]
        vals = win[slot, :, 128 * v_slab : 128 * v_slab + 128]
        count = GRP * len(kv_heads)
        width = BLK * count
        base = BLK * at
        q_rows, do_rows, dots = [], [], []
        for j in range(count):
            r = slice(HD * (at + j), HD * (at + j) + HD)
            q_rows.append(q_all[r])
            scaled = do_all[r] * rl_ref[0, at + j : at + j + 1, :]
            dots.append(jnp.sum(scaled * o_all[r], axis=0, keepdims=True))
            do_rows.append(scaled.astype(BF16))
        q_wide = spread_heads(q_rows, len(kv_heads), k_low)
        do_wide = spread_heads(do_rows, len(kv_heads), v_low)
        scores[:, :width] = dot(vals, do_wide)
        ds = []
        for j in range(count):
            p = p_ref[0, :, base + BLK * j : base + BLK * j + BLK].astype(F32)
            ds.append((p * (scores[:, BLK * j : BLK * j + BLK] - dots[j])).astype(BF16))
        ds = jnp.concatenate(ds, axis=1)
        probs = p_ref[0, :, base : base + width]
        if len(kv_heads) == 2:
            add(k_slab, dot_nt(ds, q_wide))
            add(v_slab, dot_nt(probs, do_wide))
        else:
            add(
                k_slab,
                dot_nt(
                    jnp.concatenate([ds, probs], axis=1),
                    jnp.concatenate([q_wide, do_wide], axis=1),
                ),
            )
        dq = dot(keys.T, ds) * (HD ** -0.5)
        for j in range(count):
            top = head_half(j, kv_heads, k_low)
            cols = slice(BLK * j, BLK * j + BLK)
            first = dq[top : top + 32, cols]
            second = dq[top + 32 : top + 64, cols]
            grads.append(first * cos + second * sin)
            grads.append(second * cos - first * sin)
        at += count
    dq_ref[...] = unturned(grads)

    @pl.when(i == pl.num_programs(0) - 1)
    def _():
        per = 6 * BLK
        places = [(n, u) for n, units in enumerate(out_units) for u in range(units)]
        copies, loads = [], []

        def load(t):
            if prev and t < len(places):
                n, u = places[t]
                c = pltpu.make_async_copy(
                    earlier[n].at[pl.ds(per * u, per)], stage_in.at[t % 2], in_sem.at[t % 2]
                )
                c.start()
                loads.append(c)

        load(0)
        load(1)
        for t, (n, u) in enumerate(places):
            s = t % 2
            if t >= 2:
                copies[t - 2].wait()
            value = acc[per * t : per * t + per, :]
            if prev:
                loads[t].wait()
                value = value + stage_in[s].astype(F32)
            stage[s] = value.astype(BF16)
            load(t + 2)
            c = pltpu.make_async_copy(stage.at[s], outs[n].at[pl.ds(per * u, per)], out_sem.at[s])
            c.start()
            copies.append(c)
        copies[-2].wait()
        copies[-1].wait()


def bwd_call(first, blocks, earlier, deps, tab, slots, out_units, q, do, mid, rl, p, cos, sin, kvs):
    n_kv = len(kvs)
    lanes, heads, width = D, HQ, KV_LANES
    n_slots = 6 * sum(out_units)
    flat = pl.BlockSpec((BLK, lanes), lambda i: (i + first, 0))
    table = pl.BlockSpec((32, BLK), lambda i: (0, i + first))
    prev = bool(earlier)
    return pl.pallas_call(
        lambda *refs: bwd_kernel(n_kv, len(deps), first, prev, out_units, n_slots, *refs),
        grid=(blocks,),
        out_shape=(jax.ShapeDtypeStruct((blocks * BLK, lanes), BF16),)
        + tuple(jax.ShapeDtypeStruct((6 * BLK * u, width), BF16) for u in out_units),
        in_specs=[
            SMEM,
            SMEM,
            flat,
            flat,
            flat,
            pl.BlockSpec((1, 16, BLK), lambda i: (i + first, 0, 0)),
            pl.BlockSpec((1, SPAN, heads * BLK), lambda i: (i + first, 0, 0)),
            table,
            table,
        ]
        + [ANY] * (n_kv + len(deps) + len(earlier)),
        out_specs=(pl.BlockSpec((BLK, lanes), lambda i: (i, 0)),) + (ANY,) * len(out_units),
        scratch_shapes=[
            pltpu.VMEM((2, SPAN, width), BF16),
            pltpu.VMEM((n_slots * BLK, width), F32),
            pltpu.VMEM((SPAN, 2 * GRP * BLK), F32),
            pltpu.VMEM((2, 6 * BLK, width), BF16),
            pltpu.VMEM((2, 6 * BLK, width), BF16),
            pltpu.SemaphoreType.DMA((2,)),
            pltpu.SemaphoreType.DMA((2,)),
            pltpu.SemaphoreType.DMA((2,)),
        ],
        compiler_params=params(60, 1),
        cost_estimate=cost(0.5e9 * heads * blocks, 0.5e6 * heads * blocks),
        name=f"attend_back_{first}",
    )(tab, slots, q, do, mid, rl, p, cos, sin, *kvs, *deps, *earlier)


def pro_kernel(info, mid_ref, x_ref, gain_ref, own, *refs):
    here, there = refs[0:4], refs[4:6]
    h1_ref, low_ref, w_ref, sems = refs[7:]
    z, core, parity = info[0], info[1], info[4]
    found = []

    def bring(src, row, size, cond=None):
        dst = w_ref.at[pl.ds(pl.multiple_of(row, 16), size)]
        found.append((cond, pltpu.make_async_copy(src, dst, sems.at[len(found)])))

    bring(own, z * ZR, ZR)
    for n, (side, par) in enumerate(
        ((core, parity), (core, 1 - parity), (1 - core, parity), (1 - core, 1 - parity))
    ):
        qd = 2 * side + par
        for i in range(3):
            if n < 2:
                a = PACKED * i + OUT_AT
                src = here[2 * n + (a >= CUT)]
                a -= CUT if a >= CUT else 0
                view = lambda at, size, src=src, a=a: src.at[pl.ds(a + at, size)]
            else:
                view = lambda at, size, src=there[n - 2], i=i: src.at[i, pl.ds(at, size)]
            base = rel_z(z, i) * ZR + jnp.minimum(OUT_ROWS * qd, ZR - OUT_ROWS)
            bring(view(0, 16), base, 16, qd < 3)
            bring(view(16, OUT_ROWS - 16), base + 16, OUT_ROWS - 16)
    each(found, start)
    gain = gain_ref[1:2, :]
    each(found, wait)

    def body(i, _):
        r = pl.ds(pl.multiple_of(i * ROWS, ROWS), ROWS)
        h = x_ref[r, :].astype(F32) + dot(mid_ref[r, :], w_ref[...])
        factor = lax.rsqrt(jnp.mean(h * h, axis=-1, keepdims=True) + NORM_EPS)
        h1_ref[r, :] = h
        low_ref[r, 0:D] = (h * factor * gain).astype(BF16)
        low_ref[r, D:WIDE] = jnp.zeros((ROWS, WIDE - D), BF16)
        return 0

    lax.fori_loop(0, x_ref.shape[0] // ROWS, body, 0)


def pro_call(info, mid, x, gains, own, here, there, dep):
    t = x.shape[0]
    return pl.pallas_call(
        pro_kernel,
        out_shape=(
            jax.ShapeDtypeStruct((t, D), F32),
            jax.ShapeDtypeStruct((t, WIDE), BF16),
            jax.ShapeDtypeStruct((D, D), BF16),
        ),
        in_specs=[SMEM] + [VMEM] * 3 + [ANY] * 8,
        out_specs=(VMEM,) * 3,
        scratch_shapes=[pltpu.SemaphoreType.DMA((25,))],
        compiler_params=params(40),
        cost_estimate=cost(2 * t * D * D, 12e6),
        name="out_projection",
    )(info, mid, x, gains, own, *here, *there, dep)


def ffn_kernel(info, a0, a1, c0, c1, own, *refs):
    here = refs[:4]
    acc_outs, p_ref, q_refs = refs[4:8], refs[8], refs[9:13]
    (
        wbuf, a_all, c_all, c_turn, hid_s, gg_s, gu_s, stage, acc_o, acc_g, send_o, send_g,
        io_sem, w_sem, out_sem, acc_sem,
    ) = refs[13:]
    z, chip, parity = info[0], info[3], info[4]
    t = a0.shape[0]
    units = wbuf.shape[1]
    ins = [
        pltpu.make_async_copy(a0, a_all.at[pl.ds(0, t)], io_sem.at[0]),
        pltpu.make_async_copy(a1, a_all.at[pl.ds(t, t)], io_sem.at[1]),
        pltpu.make_async_copy(c0, c_turn.at[0], io_sem.at[2]),
        pltpu.make_async_copy(c1, c_turn.at[1], io_sem.at[3]),
    ]
    copies = [pltpu.make_async_copy(own, wbuf.at[:, pl.ds(0, CORE_UNITS)], w_sem.at[0])]
    for n_par, par in enumerate((parity, 1 - parity)):
        for i in range(3):
            for n in range(3):
                a0_row = PACKED * i + QUARTER * n
                for ref, p0, p1 in ((here[2 * n_par], 0, CUT), (here[2 * n_par + 1], CUT, 2 * CUT)):
                    a, b = max(p0, a0_row), min(p1, a0_row + QUARTER)
                    if a < b:
                        row = CORE_UNITS * (i + 1) + QUARTER * par + (a - a0_row)
                        dst = wbuf.at[n, pl.ds(pl.multiple_of(row, 16), b - a)]
                        copies.append(
                            pltpu.make_async_copy(
                                ref.at[pl.ds(a - p0, b - a)], dst, w_sem.at[len(copies)]
                            )
                        )
    for c in ins[2:] + ins[:2] + copies:
        c.start()
    for h in range(2):
        ins[2 + h].wait()
        c_all[t * h : t * h + t, :] = c_turn[h].T
    for c in ins[:2] + copies:
        c.wait()

    def forward(c, _):
        u = pl.ds(pl.multiple_of(c * UNITS, UNITS), UNITS)
        for h in range(2 * t // ROWS):
            r = slice(ROWS * h, ROWS * h + ROWS)
            gate = dot_nt(a_all[r, 0:D], wbuf[0, u, :])
            up = dot_nt(a_all[r, 0:D], wbuf[1, u, :])
            grad = dot_nt(c_all[r, :], wbuf[2, u, :])
            sig = lax.logistic(gate)
            swish = gate * sig
            hid_s[r, u] = (swish * up).astype(BF16)
            gg_s[r, u] = (grad * up * (sig * (1.0 + gate * (1.0 - sig)))).astype(BF16)
            gu_s[r, u] = (grad * swish).astype(BF16)
        return 0

    lax.fori_loop(0, units // UNITS, forward, 0)

    def sums(r):
        left = dot(hid_s[r, :], wbuf[2])
        right = dot(gg_s[r, :], wbuf[0]) + dot(gu_s[r, :], wbuf[1])
        return left, right

    def mine(i, _):
        r = pl.ds(pl.multiple_of(i * ROWS, ROWS), ROWS)
        acc_o[r, :], acc_g[r, :] = sums(r)
        return 0

    def others(i, _):
        r = pl.ds(pl.multiple_of(i * ROWS, ROWS), ROWS)
        left, right = sums(pl.ds(pl.multiple_of(t + i * ROWS, ROWS), ROWS))
        for ref, value in ((send_o, left), (send_g, right)):
            ref[r, 0:D] = value.astype(BF16)
            ref[r, D:WIDE] = jnp.zeros((ROWS, WIDE - D), BF16)
        return 0

    lax.fori_loop(0, t // ROWS, others, 0)
    lax.fori_loop(0, t // ROWS, mine, 0)
    acc_copies = [
        pltpu.make_async_copy(src, dst, acc_sem.at[n])
        for n, (src, dst) in enumerate(zip((acc_o, acc_g, send_o, send_g), acc_outs))
    ]
    for c in acc_copies:
        c.start()

    def back_copies(c, slot):
        found = []
        per = CORE_UNITS // SEG
        for n in range(UNITS // SEG):
            j = c * (UNITS // SEG) + n
            within = lax.rem(j, per)
            zz = lax.rem(z + j // per, 4)
            n_p = P_ROWS // SEG
            first = within < n_p
            row = pl.multiple_of(jnp.minimum(within, n_p - 1) * SEG, SEG)
            src = stage.at[slot, :, pl.ds(SEG * n, SEG)]
            dst = p_ref.at[zz, :, pl.ds(row, SEG)]
            found.append((first, pltpu.make_async_copy(src, dst, out_sem.at[slot, 24 + n])))
            piece = 6 * n
            for k in range(per - n_p):
                at = SEG * k
                while at < SEG * k + SEG:
                    owner = at // Q_ROWS
                    size = min(SEG * k + SEG, Q_ROWS * (owner + 1)) - at
                    src = stage.at[slot, :, pl.ds(SEG * n + at - SEG * k, size)]
                    for r in range(4):
                        dst = q_refs[r].at[zz, :, pl.ds(at - Q_ROWS * owner, size)]
                        copy = pltpu.make_async_copy(src, dst, out_sem.at[slot, piece])
                        found.append(((within == n_p + k) & (chip ^ owner == r), copy))
                    at += size
                    piece += 1
        return found

    def backward(c, _):
        u = pl.ds(pl.multiple_of(c * UNITS, UNITS), UNITS)
        slot = lax.rem(c, 2)

        @pl.when(c >= 2)
        def _():
            each(back_copies(c - 2, slot), wait)

        stage[slot, 0] = dot_tn(gg_s[:, u], a_all[:, 0:D]).astype(BF16)
        stage[slot, 1] = dot_tn(gu_s[:, u], a_all[:, 0:D]).astype(BF16)
        stage[slot, 2] = dot_tn(hid_s[:, u], c_all[...]).astype(BF16)
        each(back_copies(c, slot), start)
        return 0

    n_chunks = units // UNITS
    lax.fori_loop(0, n_chunks, backward, 0)
    for c in (n_chunks - 2, n_chunks - 1):
        each(back_copies(jnp.int32(c), c % 2), wait)
    for c in acc_copies:
        c.wait()


def ffn_call(info, a0, a1, c0, c1, own, here):
    t = a0.shape[0]
    units = 4 * CORE_UNITS
    return pl.pallas_call(
        ffn_kernel,
        out_shape=(
            jax.ShapeDtypeStruct((t, D), F32),
            jax.ShapeDtypeStruct((t, D), F32),
            jax.ShapeDtypeStruct((t, WIDE), BF16),
            jax.ShapeDtypeStruct((t, WIDE), BF16),
            jax.ShapeDtypeStruct((4, 3, P_ROWS, D), BF16),
            *[jax.ShapeDtypeStruct((4, 3, Q_ROWS, D), BF16)] * 4,
        ),
        in_specs=[SMEM] + [ANY] * 9,
        out_specs=(ANY,) * 9,
        scratch_shapes=[
            pltpu.VMEM((3, units, D), BF16),
            pltpu.VMEM((2 * t, WIDE), BF16),
            pltpu.VMEM((2 * t, D), BF16),
            pltpu.VMEM((2, D, t), BF16),
            pltpu.VMEM((2 * t, units), BF16),
            pltpu.VMEM((2 * t, units), BF16),
            pltpu.VMEM((2 * t, units), BF16),
            pltpu.VMEM((2, 3, UNITS, D), BF16),
            pltpu.VMEM((t, D), F32),
            pltpu.VMEM((t, D), F32),
            pltpu.VMEM((t, WIDE), BF16),
            pltpu.VMEM((t, WIDE), BF16),
            pltpu.SemaphoreType.DMA((4,)),
            pltpu.SemaphoreType.DMA((24,)),
            pltpu.SemaphoreType.DMA((2, 28)),
            pltpu.SemaphoreType.DMA((4,)),
        ],
        compiler_params=params(60),
        cost_estimate=cost(2 * 2 * t * D * 9 * units, 40e6),
        name="feed_forward",
    )(info, a0, a1, c0, c1, own, *here)


def put_shards(ref, product, gain_grad):
    extra = ref.shape[-1] - product.shape[1]
    if extra:
        product = jnp.concatenate([product, jnp.zeros((product.shape[0], extra), F32)], axis=1)
    width = product.shape[1]
    first_row = lax.broadcasted_iota(jnp.int32, (ZP - ZR, width), 0) == 0
    for n in range(4):
        ref[n, 0:ZR, :] = product[ZR * n : ZR * n + ZR].astype(BF16)
        if gain_grad is None:
            ref[n, ZR:ZP, :] = jnp.zeros((ZP - ZR, width), BF16)
        else:
            part = jnp.concatenate(
                [gain_grad[:, ZR * n : ZR * n + ZR], jnp.zeros((1, width - ZR), F32)], axis=1
            )
            ref[n, ZR:ZP, :] = jnp.where(first_row, part, 0.0).astype(BF16)


def epi_kernel(info, h1_ref, acc_g, got_ref, ct_ref, gain_ref, w_ref, mid_ref, gh_ref, gm_ref, go_ref, acc, total):
    i = pl.program_id(0)

    @pl.when(i == 0)
    def _():
        acc[...] = jnp.zeros((D, D), F32)
        total[...] = jnp.zeros((8, D), F32)

    h = h1_ref[...]
    factor = lax.rsqrt(jnp.mean(h * h, axis=-1, keepdims=True) + NORM_EPS)
    normed = h * factor
    g = acc_g[...] + got_ref[:, 0:D].astype(F32)
    scaled = g * gain_ref[1:2, :]
    back = factor * (scaled - normed * jnp.mean(scaled * normed, axis=-1, keepdims=True))
    full = ct_ref[...].T.astype(F32) + back
    gh_ref[...] = full
    res = full.astype(BF16)
    gm_ref[...] = dot_nt(res, w_ref[...]).astype(BF16)
    total[0:1, :] += jnp.sum(g * normed, axis=0, keepdims=True)
    acc[...] += dot_tn(mid_ref[...], res)

    @pl.when(i == pl.num_programs(0) - 1)
    def _():
        put_shards(go_ref, acc[...], total[0:1, :])


def epi_call(info, h1, acc_g, got, cot_t, gains, w_out, mid):
    t = h1.shape[0]
    rows = pl.BlockSpec((ROWS, D), lambda i: (i, 0))
    return pl.pallas_call(
        epi_kernel,
        grid=(t // ROWS,),
        out_shape=(
            jax.ShapeDtypeStruct((t, D), F32),
            jax.ShapeDtypeStruct((t, D), BF16),
            jax.ShapeDtypeStruct((4, ZP, WIDE), BF16),
        ),
        in_specs=[
            SMEM,
            rows,
            rows,
            pl.BlockSpec((ROWS, WIDE), lambda i: (i, 0)),
            pl.BlockSpec((D, ROWS), lambda i: (0, i)),
            VMEM,
            VMEM,
            rows,
        ],
        out_specs=(rows, rows, pl.BlockSpec((4, ZP, WIDE), lambda i: (0, 0, 0))),
        scratch_shapes=[pltpu.VMEM((D, D), F32), pltpu.VMEM((8, D), F32)],
        compiler_params=params(48, 1),
        cost_estimate=cost(4 * t * D * D, 20e6),
        name="feed_forward_norm_back",
    )(info, h1, acc_g, got, cot_t, gains, w_out, mid)


def post_q_kernel(info, a_ref, g_ref, w_ref, go_ref, _, keep_ref, send_ref, part_ref):
    core = info[1]
    g = g_ref[...]
    product = dot_tn(a_ref[...], g)

    @pl.when(core == 0)
    def _():
        put_shards(keep_ref, product, None)
        send_ref[...] = go_ref[...]

    @pl.when(core == 1)
    def _():
        put_shards(send_ref, product, None)
        keep_ref[...] = go_ref[...]

    part_ref[...] = dot_nt(g, w_ref[:, :D])


def post_q_call(info, a, g, w, go, dep):
    t = a.shape[0]
    return pl.pallas_call(
        post_q_kernel,
        out_shape=(
            jax.ShapeDtypeStruct((4, ZP, 1024), BF16),
            jax.ShapeDtypeStruct((4, ZP, 1024), BF16),
            jax.ShapeDtypeStruct((t, D), F32),
        ),
        in_specs=[SMEM] + [VMEM] * 4 + [ANY],
        out_specs=(VMEM,) * 3,
        compiler_params=params(40),
        cost_estimate=cost(4 * t * D * D, 12e6),
        name="query_back",
    )(info, a, g, w, go, dep)


def post_kv_kernel(
    info, s0, s1, s2, cos_ref, sin_ref, a_ref, part_ref, w_ref, x_ref, gh_ref, gain_ref,
    keep_ref, send_ref, ig_ref, kg, vg,
):
    core = info[1]
    first_half, low_head = lane_masks(ROWS)
    steps = x_ref.shape[0] // ROWS
    gain = gain_ref[0:1, :]

    def body(i, total):
        r = pl.ds(pl.multiple_of(i * ROWS, ROWS), ROWS)

        def slab(j):
            c = slice(128 * j, 128 * j + 128)
            return s0[r, c].astype(F32) + s1[r, c].astype(F32) + s2[r, c].astype(F32)

        cos, sin = cos_ref[r, :], -sin_ref[r, :]
        mixed = slab(2)
        k4 = jnp.where(low_head, 0.0, rope_slab(mixed, cos, sin, first_half))
        k01 = rope_slab(slab(0), cos, sin, first_half)
        k23 = rope_slab(slab(1), cos, sin, first_half)
        k_low = jnp.concatenate([k4, k01, k23], axis=1).astype(BF16)
        v4 = jnp.where(low_head, mixed, 0.0)
        v_low = jnp.concatenate([slab(3), slab(4), v4], axis=1).astype(BF16)
        kg[r, :] = k_low
        vg[r, :] = v_low
        g = (
            part_ref[r, :]
            + dot_nt(k_low, w_ref[:, 896:1280])
            + dot_nt(v_low[:, 0:320], w_ref[:, 1280:1600])
        )
        x = x_ref[r, :].astype(F32)
        factor = lax.rsqrt(jnp.mean(x * x, axis=-1, keepdims=True) + NORM_EPS)
        normed = x * factor
        scaled = g * gain
        back = factor * (scaled - normed * jnp.mean(scaled * normed, axis=-1, keepdims=True))
        ig_ref[:, r] = (gh_ref[r, :] + back).astype(BF16).T
        return total + jnp.sum(g * normed, axis=0, keepdims=True)

    gain_grad = lax.fori_loop(0, steps, body, jnp.zeros((1, D), F32))
    mine = core == 0
    k_side = dot_tn(a_ref[...], kg[...])
    v_side = dot_tn(a_ref[...], vg[...])
    put_shards(keep_ref, jnp.where(mine, k_side, v_side), jnp.where(mine, gain_grad, 0.0))
    put_shards(send_ref, jnp.where(mine, v_side, k_side), jnp.where(mine, 0.0, gain_grad))


def post_kv_call(info, sums, cos, sin, a, part, w, x, gh, gain, deps):
    t = x.shape[0]
    n_deps = len(deps)
    piece = jax.ShapeDtypeStruct((4, ZP, 384), BF16)
    return pl.pallas_call(
        lambda *refs: post_kv_kernel(*refs[:12], *refs[12 + n_deps :]),
        out_shape=(piece, piece, jax.ShapeDtypeStruct((D, t), BF16)),
        in_specs=[SMEM] + [VMEM] * 11 + [ANY] * n_deps,
        out_specs=(VMEM,) * 3,
        scratch_shapes=[pltpu.VMEM((t, 384), BF16), pltpu.VMEM((t, 384), BF16)],
        compiler_params=params(50),
        cost_estimate=cost(8 * t * D * 384, 25e6),
        name="key_value_back",
    )(info, *sums, cos, sin, a, part, w, x, gh, gain, *deps)


def finish_ffn_kernel(info, pm_ref, po_ref, qm_ref, qo_ref, gate_ref, up_ref, down_ref, rows):
    core, chip = info[1], info[3]
    for n, out in enumerate((gate_ref, up_ref, down_ref)):
        for p_ref, q_ref, side in ((pm_ref, qm_ref, core), (po_ref, qo_ref, 1 - core)):
            base = side * CORE_UNITS
            rows[pl.ds(pl.multiple_of(base, 16), P_ROWS), :] = p_ref[n].astype(F32)
            for r in range(4):
                row = base + P_ROWS + Q_ROWS * (chip ^ r)
                rows[pl.ds(pl.multiple_of(row, 16), Q_ROWS), :] = q_ref[r, n].astype(F32)
        out[...] = rows[...].T


def finish_ffn_call(info, pm, po, qm, qo):
    out = jax.ShapeDtypeStruct((D, 2 * CORE_UNITS), F32)
    return pl.pallas_call(
        finish_ffn_kernel,
        out_shape=(out,) * 3,
        in_specs=[SMEM] + [VMEM] * 4,
        out_specs=(VMEM,) * 3,
        scratch_shapes=[pltpu.VMEM((2 * CORE_UNITS, D), F32)],
        compiler_params=params(32),
        cost_estimate=cost(1e6, 12e6),
        name="finish_feed_forward",
    )(info, pm, po, qm, qo)


def finish_rest_kernel(info, qm_ref, qo_ref, km_ref, ko_ref, wq_ref, wo_ref, wk_ref, wv_ref, gains_ref):
    def emit(q_ref, o_ref, k_ref, v_ref):
        wq_ref[...] = q_ref[0:ZR, 0:D].astype(F32)
        wo_ref[...] = o_ref[0:ZR, 0:D].astype(F32)
        k = k_ref[...].astype(F32).T
        wk_ref[...] = jnp.concatenate([k[128:384], k[64:128]], axis=0)[:, 0:ZR]
        wv_ref[...] = v_ref[...].astype(F32).T[0:320, 0:ZR]
        gains_ref[0:1, :] = k_ref[ZR:ZP, :].astype(F32)[0:1, 0:256]
        gains_ref[1:2, :] = o_ref[ZR:ZP, :].astype(F32)[0:1, 0:256]

    @pl.when(info[1] == 0)
    def _():
        emit(qm_ref, qo_ref, km_ref, ko_ref)

    @pl.when(info[1] == 1)
    def _():
        emit(qo_ref, qm_ref, ko_ref, km_ref)


def finish_rest_call(info, qm, qo, km, ko):
    return pl.pallas_call(
        finish_rest_kernel,
        out_shape=(
            jax.ShapeDtypeStruct((ZR, D), F32),
            jax.ShapeDtypeStruct((ZR, D), F32),
            jax.ShapeDtypeStruct((320, ZR), F32),
            jax.ShapeDtypeStruct((320, ZR), F32),
            jax.ShapeDtypeStruct((2, 256), F32),
        ),
        in_specs=[SMEM] + [VMEM] * 4,
        out_specs=(VMEM,) * 5,
        compiler_params=params(32),
        cost_estimate=cost(1e6, 4e6),
        name="finish_rest",
    )(info, qm, qo, km, ko)


def sum_chips(info, terms, passed, dep):
    n_terms = len(terms)

    def body(info, ins, outs, scratch):
        z = info[0]
        for n in range(4):
            zz = lax.rem(z + n, 4)
            outs[n][...] = sum(ins[k][zz].astype(F32) for k in range(n_terms)).astype(BF16)

    return step_call(
        "sum_chips",
        body,
        info,
        (*terms, *passed, dep),
        (((3, Q_ROWS, D), BF16),) * 4 + tuple((p.shape, p.dtype) for p in passed),
        8e6,
        [VMEM] * n_terms + [ANY] * (len(passed) + 1),
        [VMEM] * 4 + [ANY] * len(passed),
        aliases={1 + n_terms + n: 4 + n for n in range(len(passed))},
    )


def join_near(info, keep, recv, from_x, from_y, dep):
    rows = keep.shape[0] // 3
    cut = rows // 2

    def body(info, ins, outs, scratch):
        keep, recv, from_x, from_y, _ = ins
        outs[0][...] = keep[0:rows, :] + recv[0:rows, :]
        for n, (lo, hi) in ((1, (None, from_y)), (2, (from_x, None))):
            for h, extra in enumerate((lo, hi)):
                r = slice(rows * n + cut * h, rows * n + cut * h + cut)
                value = keep[r, :].astype(F32) + recv[r, :].astype(F32)
                if extra is not None:
                    value = value + extra[...].astype(F32)
                outs[n][cut * h : cut * h + cut, :] = value.astype(BF16)

    out = ((rows, KV_LANES), BF16)
    return step_call(
        "join_near",
        body,
        info,
        (keep, recv, from_x, from_y, dep),
        (out,) * 3,
        10e6,
        [VMEM] * 4 + [ANY],
    )


def join_projections(info, keep, recv, h1, acc_o, got_o, dep):
    t = h1.shape[0]

    def body(info, ins, outs, scratch):
        outs[0][...] = ins[0][...] + ins[1][...]
        for i in range(t // ROWS):
            r = slice(ROWS * i, ROWS * i + ROWS)
            value = ins[2][r, :] + ins[3][r, :] + ins[4][r, 0:D].astype(F32)
            outs[1][:, r] = value.astype(BF16).T

    return step_call(
        "join_projections",
        body,
        info,
        (keep, recv, h1, acc_o, got_o, dep),
        ((keep.shape, BF16), ((D, t), BF16)),
        14e6,
        [VMEM] * 5 + [ANY],
    )


def halve_rows(info, whole, dep, axis):
    cut = whole.shape[axis] // 2
    shape = whole.shape[:axis] + (cut,) + whole.shape[axis + 1 :]
    at = (slice(None),) * axis

    def body(info, ins, outs, scratch):
        for n in range(2):
            outs[n][...] = ins[0][at + (slice(cut * n, cut * n + cut),)]

    return step_call(
        "halve_rows", body, info, (whole, dep), ((shape, BF16),) * 2, 2e6, [VMEM, ANY]
    )


def join_pairs(info, name, pairs, deps):
    flat = [a for pair in pairs for a in pair]

    def body(info, ins, outs, scratch):
        at = 0
        for n, pair in enumerate(pairs):
            terms = [ins[at + k][...].astype(F32) for k in range(len(pair))]
            at += len(pair)
            outs[n][...] = sum(terms).astype(BF16)

    return step_call(
        name,
        body,
        info,
        (*flat, *deps),
        tuple((pair[0].shape, BF16) for pair in pairs),
        4e6,
        [VMEM] * len(flat) + [ANY] * len(deps),
    )


def cut_for_chips(info, keep, recv, deps):
    rows = ZP // 4

    def body(info, ins, outs, scratch):
        chip = info[3]
        for r in range(4):
            at = pl.ds(pl.multiple_of((chip ^ r) * rows, 16), rows)
            outs[r][...] = ins[0][:, at, :] + ins[1][:, at, :]

    piece = ((4, rows, keep.shape[2]), BF16)
    return step_call(
        "cut_for_chips", body, info, (keep, recv, *deps), (piece,) * 4, 3e6, [VMEM] * 2 + [ANY] * len(deps)
    )


def cut_for_z(info, terms, whole):
    shape = terms[0].shape[1:]
    cut = whole.shape[0] // 2

    def body(info, ins, outs, scratch):
        z = info[0]
        for n in range(4):
            zz = lax.rem(z + n, 4)
            outs[n][...] = sum(ins[k][zz].astype(F32) for k in range(4)).astype(BF16)
        for n in range(2):
            outs[4 + n][...] = ins[4][cut * n : cut * n + cut, :]

    half = ((cut, whole.shape[1]), BF16)
    return step_call(
        "cut_for_z", body, info, (*terms, whole), ((shape, BF16),) * 4 + (half,) * 2, 3e6
    )


def place_chips(info, pieces, pairs):
    rows, width = pieces[0].shape
    cut = pairs[0][0].shape[0]

    def body(info, ins, outs, scratch):
        chip = info[3]
        for r in range(4):
            outs[0][pl.ds(pl.multiple_of((chip ^ r) * rows, 16), rows), :] = ins[r][...]
        for n in range(2):
            outs[1][cut * n : cut * n + cut, :] = ins[4 + 2 * n][...] + ins[5 + 2 * n][...]

    return step_call(
        "place_chips",
        body,
        info,
        (*pieces, *pairs[0], *pairs[1]),
        (((4 * rows, width), BF16), ((2 * cut, pairs[0][0].shape[1]), BF16)),
        2e6,
    )


def rows_after(x, start, size, tok, axis=0):
    return lax.dynamic_slice_in_dim(x, start + tok, size, axis=axis)


def z_shift(x, step):
    n = 4
    return lax.ppermute(x, "fsdp", [(i, (i + step) % n) for i in range(n)])


def c_swap(x, bit):
    n = lax.axis_size("ctx")
    return lax.ppermute(x, "ctx", [(i, i ^ bit) for i in range(n)])


def bits_from(b):
    bits = []
    while b < lax.axis_size("ctx"):
        bits.append(b)
        b *= 2
    return bits


def chip_near(kv):
    if lax.axis_size("ctx") != 8:
        return ()
    return c_swap(kv, 2), c_swap(kv, 4)


def chip_far(kv, near):
    if not near:
        return [lax.all_gather(kv, "ctx", axis=0, tiled=True)]
    cut = kv.shape[0] // 2
    across_x, across_y = near
    far_lo = c_swap(across_x[:cut], 4)
    far_hi = c_swap(across_y[cut:], 2)
    chip = [kv, across_x, across_y, far_lo, far_hi]
    return chip + [c_swap(part, 1) for part in chip]


def kv_entry(position, per_dev, me, n):
    if n != 8:
        return position
    owner, within = position // per_dev, position % per_dev
    rel = owner ^ me
    cut = per_dev // 2
    far = (rel // 2) == 3
    late = far & (within >= cut)
    which = (rel % 2) * 5 + rel // 2 + late.astype(jnp.int32)
    return which * 1024 + jnp.where(late, within - cut, within)


def kv_slot(position, per_dev, me):
    owner, within = position // per_dev, position % per_dev
    rel = owner ^ me
    return ((rel % 2) * 4 + rel // 2) * per_dev + within


def on_device(
    tokens,
    cotangent,
    doc_lengths,
    deal,
    attn_gain,
    w_query,
    w_key,
    w_value,
    w_out,
    mlp_gain,
    w_gate,
    w_up,
    w_down,
):
    me = lax.axis_index("ctx")
    n_ctx = lax.axis_size("ctx")
    z = lax.axis_index("fsdp")
    core = me % 2
    near_me = me % 8
    chip = near_me // 2
    parity = (chip + chip // 2) % 2
    info = jnp.stack([z, core, near_me, chip, parity]).astype(jnp.int32)
    tok_rows = tokens.shape[1]
    per_dev = tok_rows // BLK
    deal_row = deal[0]
    blocks = deal_row.shape[0]
    group_size = blocks * BLK
    doc_lens = doc_lengths[0]
    seq_count = doc_lens.shape[0]
    length = group_size // seq_count
    x_turned = tokens[0].T
    cot_turned = cotangent[0].T

    gains_wide = jnp.concatenate(
        [attn_gain[:, None], mlp_gain[:, None], jnp.zeros((ZR, QKV - 1602), BF16)], axis=1
    )
    w_parts = [w_query, w_key[:, 256:], w_key[:, :256], w_value, gains_wide]
    start = jnp.minimum(32 * near_me, ZR - 32)
    w_mine = jnp.concatenate(
        [lax.dynamic_slice_in_dim(w, start, 32, axis=0) for w in w_parts], axis=1
    )
    w_z = [z_shift(w_mine, -1), z_shift(w_mine, 2), z_shift(w_mine, 1)]
    own_half, packed = prep_weights(info, w_gate, w_up, w_down.T, w_out)
    w_got, packed = stack_weights(info, w_z, packed)
    over_z = lax.all_gather(packed, "fsdp", axis=0, tiled=False)
    cot_there = c_swap(cot_turned, 1)
    w_chips = [w_got, c_swap(w_got, 2), c_swap(w_got, 4), c_swap(w_got, 6)]
    w_pieces = [jnp.concatenate(w_parts, axis=1)]
    for piece in w_chips:
        w_pieces += [piece, c_swap(piece, 1)]

    block_ids = jnp.arange(blocks, dtype=jnp.int32)
    mine = lax.dynamic_slice_in_dim(deal_row, me * per_dev, per_dev)
    seq_blocks = jnp.maximum(
        mine[:, None] - (NWB - 1) + jnp.arange(NWB, dtype=jnp.int32)[None, :], 0
    )
    position = jnp.sum(
        jnp.where(seq_blocks[:, :, None] == deal_row[None, None, :], block_ids, 0), axis=-1
    )
    tab = kv_entry(position, per_dev, me, n_ctx).astype(jnp.int32)
    doc_ends = (
        jnp.cumsum(doc_lens, axis=1) + (jnp.arange(seq_count, dtype=jnp.int32) * length)[:, None]
    ).reshape(-1)
    doc_starts = doc_ends - doc_lens.reshape(-1)
    q_time = mine[:, None] * BLK + jnp.arange(BLK, dtype=jnp.int32)[None, :]
    begin = jnp.max(jnp.where(q_time[..., None] >= doc_starts, doc_starts, 0), axis=-1)
    lo = jnp.maximum(begin, q_time - (WIN - 1)) - (mine[:, None] * BLK - WIN)
    lo = lo[:, None, :].astype(jnp.int32)
    pos = (q_time - begin).reshape(-1)
    half_dim = HD // 2
    freqs = ROPE_THETA ** (-jnp.arange(half_dim, dtype=F32) * (2.0 / HD))
    angle = pos.astype(F32)[:, None] * freqs[None, :]
    cos_tab, sin_tab = jnp.cos(angle), jnp.sin(angle)
    cos_wide = jnp.tile(cos_tab, (1, 4))
    sin_wide = jnp.tile(jnp.concatenate([-sin_tab, sin_tab], axis=1), (1, 2))

    attn_in, q_low, kv_low, w_all, gains, x, cos_turn, sin_turn = pre_call(
        info, x_turned, cos_wide, sin_wide, w_pieces
    )
    kvs = chip_far(kv_low, chip_near(kv_low))

    first, second, out_here = split_quarters(info, over_z, kvs[3:5] if n_ctx == 8 else kvs)
    first_on, second_on = c_swap(first, 2), c_swap(second, 4)
    mid_low, recips, probs = fwd_call(tab, lo, q_low, kvs)
    out_there = [
        c_swap(out_here, 1),
        c_swap(pick_out_rows(info, first_on, second_on, mid_low), 1),
    ]
    here = (first, second, first_on, second_on)
    h1, mlp_in, w_out_all = pro_call(
        info, mid_low, x, gains, w_out, here, out_there, cot_there
    )
    acc_o, acc_g, send_o, send_g, p_both, *q_both = ffn_call(
        info, mlp_in, c_swap(mlp_in, 1), cot_turned, cot_there, own_half, here
    )
    p_sum = lax.psum_scatter(p_both, "fsdp", scatter_dimension=0, tiled=True)[0]
    q_got = [c_swap(q_both[r], 2 * r) for r in range(1, 4)]
    grad_hidden, grad_mid, go = epi_call(
        info, h1, acc_g, c_swap(send_g, 1), cot_turned, gains, w_out_all, mid_low
    )
    got_o = c_swap(send_o, 1)

    if n_ctx == 8:
        out_units = (3, 1, 3, 1)
        slots = kv_slot(position, per_dev, me).astype(jnp.int32)
    else:
        out_units = (NWB,)
        n_slots = per_dev * NWB
        flat_pos = position.reshape(-1)
        order = jnp.arange(n_slots, dtype=jnp.int32)
        slots = jnp.min(
            jnp.where(flat_pos[:, None] == flat_pos[None, :], order[None, :], n_slots), axis=1
        ).reshape(per_dev, NWB)
        source = jnp.min(
            jnp.where(block_ids[:, None] == flat_pos[None, :], order[None, :], n_slots), axis=1
        )

    def own_rows(parts):
        width = parts[0].shape[1]
        padded = jnp.concatenate(
            [parts[0].reshape(n_slots, BLK, width), jnp.zeros((1, BLK, width), BF16)], axis=0
        )
        spread = jnp.take(padded, source, axis=0).reshape(group_size, width)
        own = lax.psum_scatter(spread, "ctx", scatter_dimension=0, tiled=True)
        return own, (own, jnp.zeros_like(own), jnp.zeros_like(own))

    back_args = (
        tab, slots, out_units, q_low, grad_mid, mid_low, recips, probs, cos_turn, sin_turn, kvs
    )
    dq, *kv_parts = bwd_call(0, per_dev, (), (), *back_args)
    q_terms = (q_both[0], *q_got)
    if n_ctx == 8:
        keep_near, keep_far, send_near, send_far = kv_parts
        *q_parts, send_near, send_far = sum_chips(info, q_terms, (send_near, send_far), dq)
        recv_far, recv_near = c_swap(send_far, 1), c_swap(send_near, 1)
        cut = keep_far.shape[0] // 2
        far_lo = keep_far[:cut] + recv_far[:cut]
        far_hi = keep_far[cut:] + recv_far[cut:]
        from_x, from_y = c_swap(far_lo, 2), c_swap(far_hi, 4)
        far = far_lo
    else:
        q_parts = sum_chips(info, q_terms, (), dq)
        ready, sums = own_rows(kv_parts)
        far = ready
    q_z = [z_shift(q_parts[step], step) for step in (1, 2, 3)]
    qo_keep, qo_send, part = post_q_call(info, attn_in, dq, w_all, go, far)
    qo_recv = c_swap(qo_send, 1)
    qo_both, output = join_projections(info, qo_keep, qo_recv, h1, acc_o, got_o, far)
    if n_ctx == 8:
        own, to_x, to_y = join_near(info, keep_near, recv_near, from_x, from_y, qo_both)
        sums = (own, c_swap(to_x, 2), c_swap(to_y, 4))
        ready = to_x
    qo_sum = lax.psum_scatter(qo_both, "fsdp", scatter_dimension=0, tiled=True)[0]

    p_l, p_r = halve_rows(info, p_sum, ready, 1)
    p_l, p_r, q_mine = join_pairs(
        info,
        "join_chips",
        ((p_l, c_swap(p_l, 2)), (p_r, c_swap(p_r, 4)), (q_parts[0], *q_z)),
        sums[1:],
    )
    p_got = c_swap(p_l, 4), c_swap(p_r, 2)
    for b in bits_from(8):
        q_mine = q_mine + c_swap(q_mine, b)
    q_all = [q_mine, c_swap(q_mine, 2), c_swap(q_mine, 4), c_swap(q_mine, 6)]
    kv_keep, kv_send, input_grad = post_kv_call(
        info, sums, cos_wide, sin_wide, attn_in, part, w_all, x, grad_hidden, gains, (p_l, q_mine)
    )
    kv_pieces = cut_for_chips(info, kv_keep, c_swap(kv_send, 1), ())
    kv_pieces = [kv_pieces[0]] + [c_swap(kv_pieces[r], 2 * r) for r in range(1, 4)]
    p_l, p_r = join_pairs(
        info, "join_chips", ((p_l, p_got[0]), (p_r, p_got[1])), (kv_pieces[0], *q_all[1:])
    )
    p_sum = jnp.concatenate([p_l, p_r], axis=1)
    for b in bits_from(8):
        p_sum = p_sum + c_swap(p_sum, b)
    q_all = jnp.stack(q_all)
    *kv_z, qo_l, qo_r = cut_for_z(info, kv_pieces, qo_sum)
    kv_terms = [kv_z[0]] + [z_shift(kv_z[step], step) for step in (1, 2, 3)]
    kv_mine, qo_l, qo_r = join_pairs(
        info, "join_z", (kv_terms, (qo_l, c_swap(qo_l, 2)), (qo_r, c_swap(qo_r, 4))), ()
    )
    for b in bits_from(8):
        kv_mine = kv_mine + c_swap(kv_mine, b)
    kv_all = [kv_mine] + [c_swap(kv_mine, 2 * r) for r in range(1, 4)]
    kv_sum, qo_sum = place_chips(
        info, kv_all, ((qo_l, c_swap(qo_l, 4)), (qo_r, c_swap(qo_r, 2)))
    )
    for b in bits_from(8):
        qo_sum = qo_sum + c_swap(qo_sum, b)

    gate_grad, up_grad, down_grad = finish_ffn_call(
        info, p_sum, c_swap(p_sum, 1), q_all, c_swap(q_all, 1)
    )
    query_grad, out_grad, key_grad, value_grad, gain_grads = finish_rest_call(
        info, qo_sum, c_swap(qo_sum, 1), kv_sum, c_swap(kv_sum, 1)
    )

    return (
        output.T[None],
        input_grad.T[None],
        gain_grads[0, :ZR],
        query_grad,
        key_grad.T,
        value_grad.T,
        out_grad,
        gain_grads[1, :ZR],
        gate_grad,
        up_grad,
        down_grad.T,
    )


def solution(mesh):
    in_specs = (
        P("fsdp", "ctx", None),
        P("fsdp", "ctx", None),
        P("fsdp", None, None),
        P("fsdp", None),
        P("fsdp"),
        P("fsdp", None),
        P("fsdp", None),
        P("fsdp", None),
        P("fsdp", None),
        P("fsdp"),
        P(None, "fsdp"),
        P(None, "fsdp"),
        P("fsdp", None),
    )
    out_specs = (
        P("fsdp", "ctx", None),
        P("fsdp", "ctx", None),
        P("fsdp"),
        P("fsdp", None),
        P("fsdp", None),
        P("fsdp", None),
        P("fsdp", None),
        P("fsdp"),
        P(None, "fsdp"),
        P(None, "fsdp"),
        P("fsdp", None),
    )
    return jax.shard_map(
        on_device, mesh=mesh, in_specs=in_specs, out_specs=out_specs, check_vma=False
    )
```

```python
import jax
import jax.numpy as jnp
from jax import lax
from jax.experimental import pallas as pl
from jax.experimental.pallas import tpu as pltpu
from jax.sharding import PartitionSpec as P

HQ = 15
KVH = 5
HD = 64
BLK = 128
WIN = 1024
D = 960
GRP = HQ // KVH
SPAN = WIN + BLK
NWB = SPAN // BLK
ROWS = 256
ZR = 240
ZP = 256
UNITS = 256
WIDE = 1024
QKV = 1664

NORM_EPS = 1e-05
ROPE_THETA = 100000.0
MASK_FILL = -1e30
F32 = jnp.float32
BF16 = jnp.bfloat16
MIB = 1024 * 1024

VMEM = pl.BlockSpec(memory_space=pltpu.VMEM)
SMEM = pl.BlockSpec(memory_space=pltpu.SMEM)
ANY = pl.BlockSpec(memory_space=pl.ANY)

KV_LANES = 640
PAIRS = (
    (0, 3, (0, 1), True, True),
    (1, 4, (2, 3), True, True),
    (2, 2, (4,), False, True),
)

CORE_UNITS = 320
QUARTER = 160
OUT_ROWS = 128
PACKED = 3 * QUARTER
CUT = 3 * PACKED // 2

P_ROWS = 128
Q_ROWS = 48
SEG = 64


def dot(a, b):
    return jnp.dot(a, b, preferred_element_type=F32)


def dot_nt(a, b):
    return lax.dot_general(a, b, (((1,), (1,)), ((), ())), preferred_element_type=F32)


def dot_tn(a, b):
    return lax.dot_general(a, b, (((0,), (0,)), ((), ())), preferred_element_type=F32)


def params(mib, grid_dims=0):
    return pltpu.CompilerParams(
        vmem_limit_bytes=mib * MIB,
        dimension_semantics=("arbitrary",) * grid_dims if grid_dims else None,
    )


def cost(micros):
    return pl.CostEstimate(flops=int(3.5e8 * micros), bytes_accessed=1, transcendentals=0)


def rope_slab(t, cos, sin_signed, first_half):
    swapped = jnp.where(first_half, pltpu.roll(t, 96, 1), pltpu.roll(t, 32, 1))
    return t * cos + swapped * sin_signed


def wide_tables(cos, sin):
    return (
        jnp.concatenate([cos] * 4, axis=0).T,
        jnp.concatenate([-sin, sin, -sin, sin], axis=0).T,
    )


def lane_masks(rows):
    lane = lax.broadcasted_iota(jnp.int32, (rows, 128), 1)
    return (lane % HD) < HD // 2, lane < HD


def rel_z(z, i):
    return lax.rem(z + 1 + i, 4)


def each(found, act):
    for cond, c in found:
        if cond is None:
            act(c)
        else:
            pl.when(cond)(lambda c=c: act(c))


def start(c):
    c.start()


def wait(c):
    c.wait()


def run_copies(pairs, sems):
    copies = [pltpu.make_async_copy(a, b, sems.at[i]) for i, (a, b) in enumerate(pairs)]
    for c in copies:
        c.start()
    for c in copies:
        c.wait()


MICROS = {
    "stack_two": 1,
    "meet": 1,
    "prep_weights": 5,
    "stack_weights": 2,
    "split_quarters": 5,
    "pick_out_rows": 3,
    "sum_chips": 4,
    "join_cores": 5,
    "key_value_weights_back": 11,
    "join_near": 4,
    "join_projections": 7,
    "add_pairs": 3,
    "stack_pairs": 2,
    "halve_rows": 2,
    "join_feed_forward": 3,
    "finish_feed_forward": 6,
    "finish_rest": 4,
}


def whole(shape):
    return pl.BlockSpec(shape, lambda i: (0,) * len(shape))


def step_call(
    name, body, info, ins, outs, far=(), scratch=(), behind=(), passed=()
):
    n_in, n_out, n_behind, n_passed = len(ins), len(outs), len(behind), len(passed)

    def kernel(info_ref, *refs):
        after = refs[n_in + n_behind + n_passed :]
        body(info_ref, refs[:n_in], after[:n_out], after[n_out + n_passed :])

    return pl.pallas_call(
        kernel,
        grid=(1,),
        out_shape=tuple(jax.ShapeDtypeStruct(shape, dtype) for shape, dtype in outs)
        + tuple(jax.ShapeDtypeStruct(p.shape, p.dtype) for p in passed),
        in_specs=[SMEM]
        + [ANY if n in far else whole(x.shape) for n, x in enumerate(ins)]
        + [ANY] * (n_behind + n_passed),
        out_specs=tuple(whole(shape) for shape, _ in outs) + (ANY,) * n_passed,
        scratch_shapes=list(scratch),
        input_output_aliases={1 + n_in + n_behind + n: n_out + n for n in range(n_passed)},
        compiler_params=params(60, 1),
        cost_estimate=cost(MICROS[name]),
        name=name,
    )(info, *ins, *behind, *passed)


def meet(info, passed, behind=()):
    return step_call("meet", lambda *refs: None, info, (), (), behind=behind, passed=passed)


def prep_weights(info, w_gate, w_up, w_down_turned):
    def body(info, ins, outs, scratch):
        core, parity = info[1], info[4]
        turn, given, sems = scratch
        base = core * CORE_UNITS
        copies = [pltpu.make_async_copy(ins[n], given.at[n], sems.at[n]) for n in range(3)]
        for c in copies:
            c.start()
        for n in range(3):
            copies[n].wait()
            turn[...] = given[n].T
            outs[0][n] = turn[pl.ds(pl.multiple_of(base, 16), CORE_UNITS), :]
            quarter = pl.ds(pl.multiple_of(base + QUARTER * parity, 16), QUARTER)
            outs[1][QUARTER * n : QUARTER * n + QUARTER, :] = turn[quarter, :]

    weights = (w_gate, w_up, w_down_turned)
    return step_call(
        "prep_weights",
        body,
        info,
        weights,
        (((3, CORE_UNITS, D), BF16), ((PACKED, D), BF16)),
        far=range(3),
        scratch=(
            pltpu.VMEM((2 * CORE_UNITS, D), BF16),
            pltpu.VMEM((3,) + w_gate.shape, BF16),
            pltpu.SemaphoreType.DMA((3,)),
        ),
    )


def stack_weights(info, parts, behind, passed):
    def body(info, ins, outs, scratch):
        for n in range(3):
            outs[0][n] = ins[n][...]

    out = ((3,) + parts[0].shape, BF16)
    return step_call("stack_weights", body, info, parts, (out,), behind=behind, passed=passed)


def split_quarters(info, over_z, deps):
    at = CUT - PACKED

    def body(info, ins, outs, scratch):
        src = ins[0]
        z = info[0]
        zs = [rel_z(z, i) for i in range(3)]
        pairs = [
            (src.at[zs[0]], outs[0].at[pl.ds(0, PACKED)]),
            (src.at[zs[1], pl.ds(0, at)], outs[0].at[pl.ds(PACKED, at)]),
            (src.at[zs[1], pl.ds(at, PACKED - at)], outs[1].at[pl.ds(0, PACKED - at)]),
            (src.at[zs[2]], outs[1].at[pl.ds(PACKED - at, PACKED)]),
        ]
        run_copies(pairs, scratch[0])

    half = (CUT, D)
    return step_call(
        "split_quarters",
        body,
        info,
        (over_z, *deps),
        ((half, BF16), (half, BF16)),
        range(1 + len(deps)),
        scratch=(pltpu.SemaphoreType.DMA((4,)),),
    )


def pre_kernel(info, xt_ref, cos_ref, sin_ref, *refs):
    own, pieces = refs[0], refs[1:9]
    attn_ref, attn_up, attn_lo, q_ref, kv_ref, x_ref, gains_ref, wq_out, wkv_out = refs[9:18]
    w_ref, sems, out_sems = refs[18:]
    step = pl.program_id(0)
    z, me = info[0], info[2]
    outs = [
        pltpu.make_async_copy(w_ref.at[:, pl.ds(0, WIDE)], wq_out, out_sems.at[0]),
        pltpu.make_async_copy(w_ref.at[:, pl.ds(896, QKV - 896)], wkv_out, out_sems.at[1]),
    ]

    def pieces_do(act):
        found = []

        def add(src, row, size, cond=None):
            view = w_ref.at[pl.ds(pl.multiple_of(row, 16), size)]
            found.append((cond, pltpu.make_async_copy(src, view, sems.at[len(found)])))

        add(own, z * ZR, ZR)
        for rel, piece in enumerate(pieces):
            c = me ^ rel
            for i in range(3):
                base = rel_z(z, i) * ZR
                add(piece.at[i, pl.ds(0, 16)], base + 32 * c, 16, c < 7)
                add(piece.at[i, pl.ds(16, 16)], base + jnp.minimum(32 * c + 16, ZR - 16), 16)
        each(found, act)

    @pl.when(step == 0)
    def _():
        pieces_do(start)

    first_half, low_head = lane_masks(ROWS)
    cos, sin = wide_tables(cos_ref[...], sin_ref[...])
    x_low = xt_ref[...].T
    x_ref[...] = x_low
    x = x_low.astype(F32)
    factor = lax.rsqrt(jnp.mean(x * x, axis=-1, keepdims=True) + NORM_EPS)

    @pl.when(step == 0)
    def _():
        pieces_do(wait)
        for c in outs:
            c.start()
        gains_ref[...] = w_ref[:, 1536:QKV].astype(F32).T[64:72]

    a = (x * factor * gains_ref[0:1, :]).astype(BF16)
    attn_ref[...] = a
    turned_a = a.T
    attn_up[...] = turned_a[0 : D // 2]
    attn_lo[...] = turned_a[D // 2 :]
    qk = dot(a, w_ref[:, 0:1280])
    vv = dot(a, w_ref[:, 1280:QKV])
    slabs = [rope_slab(qk[:, 128 * j : 128 * j + 128], cos, sin, first_half) for j in range(10)]
    for j in range(7):
        q_ref[:, 128 * j : 128 * j + 128] = slabs[j].astype(BF16)
    q_ref[:, 896:960] = slabs[7][:, :64].astype(BF16)
    mixed = jnp.where(low_head, vv[:, 256:384], slabs[7])
    for j, part in enumerate((slabs[8], slabs[9], mixed, vv[:, 0:128], vv[:, 128:256])):
        kv_ref[:, 128 * j : 128 * j + 128] = part.astype(BF16)

    @pl.when(step == pl.num_programs(0) - 1)
    def _():
        for c in outs:
            c.wait()


def by_rows(width):
    return pl.BlockSpec((ROWS, width), lambda i: (i, 0))


def by_lanes(height):
    return pl.BlockSpec((height, ROWS), lambda i: (0, i))


def pre_call(info, xt, cos, sin, pieces):
    t = xt.shape[1]
    return pl.pallas_call(
        pre_kernel,
        grid=(t // ROWS,),
        out_shape=(
            jax.ShapeDtypeStruct((t, D), BF16),
            jax.ShapeDtypeStruct((D // 2, t), BF16),
            jax.ShapeDtypeStruct((D // 2, t), BF16),
            jax.ShapeDtypeStruct((t, D), BF16),
            jax.ShapeDtypeStruct((t, KV_LANES), BF16),
            jax.ShapeDtypeStruct((t, D), BF16),
            jax.ShapeDtypeStruct((8, D), F32),
            jax.ShapeDtypeStruct((D, WIDE), BF16),
            jax.ShapeDtypeStruct((D, QKV - 896), BF16),
        ),
        in_specs=[SMEM, by_lanes(D), by_lanes(32), by_lanes(32)] + [ANY] * 9,
        out_specs=(
            by_rows(D), by_lanes(D // 2), by_lanes(D // 2), by_rows(D), by_rows(KV_LANES), by_rows(D), whole((8, D)),
            ANY, ANY,
        ),
        scratch_shapes=[
            pltpu.VMEM((D, QKV), BF16),
            pltpu.SemaphoreType.DMA((49,)),
            pltpu.SemaphoreType.DMA((2,)),
        ],
        compiler_params=params(60, 1),
        cost_estimate=cost(12),
        name="pre",
    )(info, xt, cos, sin, *pieces)


def start_window(tab, kvs, win, sem, blk, slot):
    def body(j, _):
        entry = tab[blk, j]
        which = entry // 1024
        idx = lax.rem(entry, 1024)
        dst = win.at[slot, pl.ds(pl.multiple_of(j * BLK, BLK), BLK)]
        for n, ref in enumerate(kvs):
            @pl.when(which == n)
            def _():
                src = ref.at[pl.ds(pl.multiple_of(idx * BLK, BLK), BLK)]
                pltpu.make_async_copy(src, dst, sem.at[slot]).start()
        return 0

    lax.fori_loop(0, NWB, body, 0)


def next_window(tab, kvs, win, sem, first=0):
    i = pl.program_id(0)
    slot = lax.rem(i, 2)

    @pl.when(i == 0)
    def _():
        start_window(tab, kvs, win, sem, i + first, slot)

    @pl.when(i + 1 < pl.num_programs(0))
    def _():
        start_window(tab, kvs, win, sem, i + first + 1, 1 - slot)

    pltpu.make_async_copy(win.at[slot], win.at[slot], sem.at[slot]).wait()
    return slot


def turned(flat):
    rows = flat.astype(F32)
    extra = -rows.shape[1] % 128
    if extra:
        rows = jnp.concatenate([rows, jnp.zeros((rows.shape[0], extra), F32)], axis=1)
    return rows.T


def unturned(parts):
    rows = sum(p.shape[0] for p in parts)
    extra = -rows % 128
    if extra:
        parts = parts + [jnp.zeros((extra, parts[0].shape[1]), F32)]
    return jnp.concatenate(parts, axis=0).T[:, :rows].astype(BF16)


def spread_heads(rows, count, low):
    width = GRP * BLK
    sides = [jnp.concatenate(rows[GRP * n : GRP * n + GRP], axis=1) for n in range(count)]
    empty = jnp.zeros((HD, width), rows[0].dtype)
    if count == 2:
        return jnp.concatenate(
            [jnp.concatenate([sides[0], empty], axis=1), jnp.concatenate([empty, sides[1]], axis=1)],
            axis=0,
        )
    return jnp.concatenate([sides[0], empty] if low else [empty, sides[0]], axis=0)


def head_half(j, kv_heads, low):
    upper = j >= GRP if len(kv_heads) == 2 else not low
    return HD if upper else 0


def fwd_kernel(n_kv, tab, lo_ref, q_ref, *refs):
    kvs = refs[:n_kv]
    mid_ref, rl_ref, p_ref, win, bias, scores, sem = refs[n_kv:]
    slot = next_window(tab, kvs, win, sem)
    row = lax.broadcasted_iota(jnp.int32, (SPAN, BLK), 0)
    lane = lax.broadcasted_iota(jnp.int32, (SPAN, BLK), 1)
    allowed = (row >= lo_ref[0]) & (row <= lane + WIN)
    bias[...] = jnp.where(allowed, 0.0, MASK_FILL)
    q_all = (turned(q_ref[...]) * (HD ** -0.5)).astype(BF16)
    outs, recips = [], []
    at = 0
    for k_slab, v_slab, kv_heads, k_low, v_low in PAIRS:
        keys = win[slot, :, 128 * k_slab : 128 * k_slab + 128]
        vals = win[slot, :, 128 * v_slab : 128 * v_slab + 128]
        count = GRP * len(kv_heads)
        width = BLK * count
        base = BLK * at
        q_rows = [q_all[HD * (at + j) : HD * (at + j) + HD] for j in range(count)]
        scores[:, :width] = dot(keys, spread_heads(q_rows, len(kv_heads), k_low))
        for j in range(count):
            s = scores[:, BLK * j : BLK * j + BLK] + bias[...]
            top = jnp.max(s, axis=0, keepdims=True)
            p_ref[0, :, base + BLK * j : base + BLK * j + BLK] = jnp.exp(s - top).astype(BF16)
        lhs = jnp.concatenate([vals.T, jnp.ones((16, SPAN), BF16)], axis=0)
        product = dot(lhs, p_ref[0, :, base : base + width])
        recip = 1.0 / product[128:129, :]
        for j in range(count):
            cols = slice(BLK * j, BLK * j + BLK)
            half = head_half(j, kv_heads, v_low)
            outs.append(product[half : half + HD, cols] * recip[:, cols])
            recips.append(recip[:, cols])
        at += count
    mid_ref[...] = unturned(outs)
    recips.append(jnp.zeros((16 - len(recips), BLK), F32))
    rl_ref[0] = jnp.concatenate(recips, axis=0)


def fwd_call(tab, lo, q, kvs):
    blocks = q.shape[0] // BLK
    n_kv = len(kvs)
    lanes, heads = D, HQ
    return pl.pallas_call(
        lambda *refs: fwd_kernel(n_kv, *refs),
        grid=(blocks,),
        out_shape=(
            jax.ShapeDtypeStruct((q.shape[0], lanes), BF16),
            jax.ShapeDtypeStruct((blocks, 16, BLK), F32),
            jax.ShapeDtypeStruct((blocks, SPAN, heads * BLK), BF16),
        ),
        in_specs=[
            SMEM,
            pl.BlockSpec((1, 1, BLK), lambda i: (i, 0, 0)),
            pl.BlockSpec((BLK, lanes), lambda i: (i, 0)),
        ]
        + [ANY] * n_kv,
        out_specs=(
            pl.BlockSpec((BLK, lanes), lambda i: (i, 0)),
            pl.BlockSpec((1, 16, BLK), lambda i: (i, 0, 0)),
            pl.BlockSpec((1, SPAN, heads * BLK), lambda i: (i, 0, 0)),
        ),
        scratch_shapes=[
            pltpu.VMEM((2, SPAN, KV_LANES), BF16),
            pltpu.VMEM((SPAN, BLK), F32),
            pltpu.VMEM((SPAN, 2 * GRP * BLK), F32),
            pltpu.SemaphoreType.DMA((2,)),
        ],
        compiler_params=params(60, 1),
        cost_estimate=cost(32),
        name="attend",
    )(tab, lo, q, *kvs)


def bwd_kernel(
    n_kv, n_dep, first, prev, out_units, n_slots, tab, slots, q_ref, do_ref, mid_ref, rl_ref, p_ref, cos_ref, sin_ref, *refs
):
    kvs = refs[:n_kv]
    n_out = len(out_units)
    refs = refs[n_kv + n_dep :]
    earlier = refs[:n_out] if prev else ()
    refs = refs[len(earlier) :]
    dq_ref = refs[0]
    outs = refs[1 : 1 + n_out]
    win, acc, scores, stage, stage_in, sem, out_sem, in_sem = refs[1 + n_out :]
    i = pl.program_id(0)
    blk = i + first
    slot = next_window(tab, kvs, win, sem, first)
    lanes = acc.shape[1]

    @pl.when(i == 0)
    def _():
        def clear(b, _):
            acc[pl.ds(pl.multiple_of(b * BLK, BLK), BLK), :] = jnp.zeros((BLK, lanes), F32)
            return 0

        lax.fori_loop(0, n_slots, clear, 0)

    def add(slab, value):
        for j in range(NWB):
            r = pl.ds(pl.multiple_of(slots[blk, j] * BLK, BLK), BLK)
            acc[r, 128 * slab : 128 * slab + 128] += value[BLK * j : BLK * j + BLK]

    q_all = (turned(q_ref[...]) * (HD ** -0.5)).astype(BF16)
    do_all = turned(do_ref[...])
    o_all = turned(mid_ref[...])
    cos, sin = cos_ref[...], sin_ref[...]
    grads = []
    at = 0
    for k_slab, v_slab, kv_heads, k_low, v_low in PAIRS:
        keys = win[slot, :, 128 * k_slab : 128 * k_slab + 128]
        vals = win[slot, :, 128 * v_slab : 128 * v_slab + 128]
        count = GRP * len(kv_heads)
        width = BLK * count
        base = BLK * at
        q_rows, do_rows, dots = [], [], []
        for j in range(count):
            r = slice(HD * (at + j), HD * (at + j) + HD)
            q_rows.append(q_all[r])
            scaled = do_all[r] * rl_ref[0, at + j : at + j + 1, :]
            dots.append(jnp.sum(scaled * o_all[r], axis=0, keepdims=True))
            do_rows.append(scaled.astype(BF16))
        q_wide = spread_heads(q_rows, len(kv_heads), k_low)
        do_wide = spread_heads(do_rows, len(kv_heads), v_low)
        scores[:, :width] = dot(vals, do_wide)
        ds = []
        for j in range(count):
            p = p_ref[0, :, base + BLK * j : base + BLK * j + BLK].astype(F32)
            ds.append((p * (scores[:, BLK * j : BLK * j + BLK] - dots[j])).astype(BF16))
        ds = jnp.concatenate(ds, axis=1)
        probs = p_ref[0, :, base : base + width]
        if len(kv_heads) == 2:
            add(k_slab, dot_nt(ds, q_wide))
            add(v_slab, dot_nt(probs, do_wide))
        else:
            add(
                k_slab,
                dot_nt(
                    jnp.concatenate([ds, probs], axis=1),
                    jnp.concatenate([q_wide, do_wide], axis=1),
                ),
            )
        dq = dot(keys.T, ds) * (HD ** -0.5)
        for j in range(count):
            top = head_half(j, kv_heads, k_low)
            cols = slice(BLK * j, BLK * j + BLK)
            first = dq[top : top + 32, cols]
            second = dq[top + 32 : top + 64, cols]
            grads.append(first * cos + second * sin)
            grads.append(second * cos - first * sin)
        at += count
    dq_ref[...] = unturned(grads)

    @pl.when(i == pl.num_programs(0) - 1)
    def _():
        per = 6 * BLK
        places = [(n, u) for n, units in enumerate(out_units) for u in range(units)]
        copies, loads = [], []

        def load(t):
            if prev and t < len(places):
                n, u = places[t]
                c = pltpu.make_async_copy(
                    earlier[n].at[pl.ds(per * u, per)], stage_in.at[t % 2], in_sem.at[t % 2]
                )
                c.start()
                loads.append(c)

        load(0)
        load(1)
        for t, (n, u) in enumerate(places):
            s = t % 2
            if t >= 2:
                copies[t - 2].wait()
            value = acc[per * t : per * t + per, :]
            if prev:
                loads[t].wait()
                value = value + stage_in[s].astype(F32)
            stage[s] = value.astype(BF16)
            load(t + 2)
            c = pltpu.make_async_copy(stage.at[s], outs[n].at[pl.ds(per * u, per)], out_sem.at[s])
            c.start()
            copies.append(c)
        copies[-2].wait()
        copies[-1].wait()


def bwd_call(first, blocks, earlier, deps, tab, slots, out_units, q, do, mid, rl, p, cos, sin, kvs):
    n_kv = len(kvs)
    lanes, heads, width = D, HQ, KV_LANES
    n_slots = 6 * sum(out_units)
    flat = pl.BlockSpec((BLK, lanes), lambda i: (i + first, 0))
    table = pl.BlockSpec((32, BLK), lambda i: (0, i + first))
    prev = bool(earlier)
    return pl.pallas_call(
        lambda *refs: bwd_kernel(n_kv, len(deps), first, prev, out_units, n_slots, *refs),
        grid=(blocks,),
        out_shape=(jax.ShapeDtypeStruct((blocks * BLK, lanes), BF16),)
        + tuple(jax.ShapeDtypeStruct((6 * BLK * u, width), BF16) for u in out_units),
        in_specs=[
            SMEM,
            SMEM,
            flat,
            flat,
            flat,
            pl.BlockSpec((1, 16, BLK), lambda i: (i + first, 0, 0)),
            pl.BlockSpec((1, SPAN, heads * BLK), lambda i: (i + first, 0, 0)),
            table,
            table,
        ]
        + [ANY] * (n_kv + len(deps) + len(earlier)),
        out_specs=(pl.BlockSpec((BLK, lanes), lambda i: (i, 0)),) + (ANY,) * len(out_units),
        scratch_shapes=[
            pltpu.VMEM((2, SPAN, width), BF16),
            pltpu.VMEM((n_slots * BLK, width), F32),
            pltpu.VMEM((SPAN, 2 * GRP * BLK), F32),
            pltpu.VMEM((2, 6 * BLK, width), BF16),
            pltpu.VMEM((2, 6 * BLK, width), BF16),
            pltpu.SemaphoreType.DMA((2,)),
            pltpu.SemaphoreType.DMA((2,)),
            pltpu.SemaphoreType.DMA((2,)),
        ],
        compiler_params=params(60, 1),
        cost_estimate=cost(10000),
        name=f"attend_back_{first}",
    )(tab, slots, q, do, mid, rl, p, cos, sin, *kvs, *deps, *earlier)


def pro_kernel(info, mid_ref, x_ref, gain_ref, own, *refs):
    here, there = refs[0:3], refs[3:6]
    h1_ref, low_ref, w_out, _, _, w_ref, sems, out_sem = refs[9:]
    z, core = info[0], info[1]
    step = pl.program_id(0)
    out_copy = pltpu.make_async_copy(w_ref, w_out, out_sem)
    found = []

    def bring(src, row, size):
        dst = w_ref.at[pl.ds(pl.multiple_of(row, 16), size)]
        found.append((None, pltpu.make_async_copy(src, dst, sems.at[len(found)])))

    bring(own, z * ZR, ZR)
    skip = 16 * (1 - core)
    for i in range(3):
        base = rel_z(z, i) * ZR
        bring(here[i], base + (ZR - OUT_ROWS) * core, OUT_ROWS)
        bring(
            there[i].at[pl.ds(pl.multiple_of(skip, 16), OUT_ROWS - 16)],
            base + (ZR - OUT_ROWS) * (1 - core) + skip,
            OUT_ROWS - 16,
        )

    @pl.when(step == 0)
    def _():
        each(found, start)
        each(found, wait)
        out_copy.start()

    h = x_ref[...].astype(F32) + dot(mid_ref[...], w_ref[...])
    factor = lax.rsqrt(jnp.mean(h * h, axis=-1, keepdims=True) + NORM_EPS)
    h1_ref[...] = h
    low_ref[:, 0:D] = (h * factor * gain_ref[1:2, :]).astype(BF16)
    low_ref[:, D:WIDE] = jnp.zeros((ROWS, WIDE - D), BF16)

    @pl.when(step == pl.num_programs(0) - 1)
    def _():
        out_copy.wait()


def pro_call(info, mid, x, gains, own, here, there, dep, passed):
    t = x.shape[0]
    return pl.pallas_call(
        pro_kernel,
        grid=(t // ROWS,),
        out_shape=(
            jax.ShapeDtypeStruct((t, D), F32),
            jax.ShapeDtypeStruct((t, WIDE), BF16),
            jax.ShapeDtypeStruct((D, D), BF16),
            *[jax.ShapeDtypeStruct(p.shape, p.dtype) for p in passed],
        ),
        in_specs=[SMEM, by_rows(D), by_rows(D), whole((8, D))] + [ANY] * 10,
        out_specs=(by_rows(D), by_rows(WIDE), ANY, ANY, ANY),
        input_output_aliases={12: 3, 13: 4},
        scratch_shapes=[
            pltpu.VMEM((D, D), BF16),
            pltpu.SemaphoreType.DMA((7,)),
            pltpu.SemaphoreType.DMA,
        ],
        compiler_params=params(60, 1),
        cost_estimate=cost(7),
        name="out_projection",
    )(info, mid, x, gains, own, *here, *there, dep, *passed)


def ffn_kernel(info, a0, a1, c0, c1, own, *refs):
    here = refs[:4]
    acc_outs, p_ref, q_refs = refs[4:9], refs[9], refs[10:14]
    (
        wbuf, a_all, c_all, c_turn, hid_s, gg_s, gu_s, stage, acc_o, acc_g, send_o, send_lo, send_hi,
        io_sem, w_sem, out_sem, acc_sem,
    ) = refs[14:]
    z, chip, parity = info[0], info[3], info[4]
    t = a0.shape[0]
    units = wbuf.shape[1]
    ins = [
        pltpu.make_async_copy(a0, a_all.at[pl.ds(0, t)], io_sem.at[0]),
        pltpu.make_async_copy(a1, a_all.at[pl.ds(t, t)], io_sem.at[1]),
        pltpu.make_async_copy(c0, c_turn.at[0], io_sem.at[2]),
        pltpu.make_async_copy(c1, c_turn.at[1], io_sem.at[3]),
    ]
    copies = [pltpu.make_async_copy(own, wbuf.at[:, pl.ds(0, CORE_UNITS)], w_sem.at[0])]
    for n_par, par in enumerate((parity, 1 - parity)):
        for i in range(3):
            for n in range(3):
                a0_row = PACKED * i + QUARTER * n
                for ref, p0, p1 in ((here[2 * n_par], 0, CUT), (here[2 * n_par + 1], CUT, 2 * CUT)):
                    a, b = max(p0, a0_row), min(p1, a0_row + QUARTER)
                    if a < b:
                        row = CORE_UNITS * (i + 1) + QUARTER * par + (a - a0_row)
                        dst = wbuf.at[n, pl.ds(pl.multiple_of(row, 16), b - a)]
                        copies.append(
                            pltpu.make_async_copy(
                                ref.at[pl.ds(a - p0, b - a)], dst, w_sem.at[len(copies)]
                            )
                        )
    for c in ins[2:] + ins[:2] + copies:
        c.start()
    for h in range(2):
        ins[2 + h].wait()
        c_all[t * h : t * h + t, :] = c_turn[h].T
    for c in ins[:2] + copies:
        c.wait()

    def forward(c, _):
        u = pl.ds(pl.multiple_of(c * UNITS, UNITS), UNITS)
        for h in range(2 * t // ROWS):
            r = slice(ROWS * h, ROWS * h + ROWS)
            gate = dot_nt(a_all[r, 0:D], wbuf[0, u, :])
            up = dot_nt(a_all[r, 0:D], wbuf[1, u, :])
            grad = dot_nt(c_all[r, :], wbuf[2, u, :])
            sig = lax.logistic(gate)
            swish = gate * sig
            hid_s[r, u] = (swish * up).astype(BF16)
            gg_s[r, u] = (grad * up * (sig * (1.0 + gate * (1.0 - sig)))).astype(BF16)
            gu_s[r, u] = (grad * swish).astype(BF16)
        return 0

    lax.fori_loop(0, units // UNITS, forward, 0)

    def sums(r):
        left = dot(hid_s[r, :], wbuf[2])
        right = dot(gg_s[r, :], wbuf[0]) + dot(gu_s[r, :], wbuf[1])
        return left, right

    def mine(i, _):
        r = pl.ds(pl.multiple_of(i * ROWS, ROWS), ROWS)
        acc_o[r, :], acc_g[r, :] = sums(r)
        return 0

    def others(i, _):
        r = pl.ds(pl.multiple_of(i * ROWS, ROWS), ROWS)
        left, right = sums(pl.ds(pl.multiple_of(t + i * ROWS, ROWS), ROWS))
        empty = jnp.zeros((ROWS, WIDE - D), BF16)
        send_o[r, 0:D] = left.astype(BF16)
        send_o[r, D:WIDE] = empty
        half = WIDE // 2
        send_lo[r, :] = right[:, 0:half].astype(BF16)
        send_hi[r, 0 : D - half] = right[:, half:D].astype(BF16)
        send_hi[r, D - half : half] = empty
        return 0

    lax.fori_loop(0, t // ROWS, others, 0)
    lax.fori_loop(0, t // ROWS, mine, 0)
    acc_copies = [
        pltpu.make_async_copy(src, dst, acc_sem.at[n])
        for n, (src, dst) in enumerate(zip((acc_o, acc_g, send_o, send_lo, send_hi), acc_outs))
    ]
    for c in acc_copies:
        c.start()

    def back_copies(c, slot):
        found = []
        per = CORE_UNITS // SEG
        for n in range(UNITS // SEG):
            j = c * (UNITS // SEG) + n
            within = lax.rem(j, per)
            zz = lax.rem(z + j // per, 4)
            n_p = P_ROWS // SEG
            first = within < n_p
            row = pl.multiple_of(jnp.minimum(within, n_p - 1) * SEG, SEG)
            src = stage.at[slot, :, pl.ds(SEG * n, SEG)]
            dst = p_ref.at[zz, :, pl.ds(row, SEG)]
            found.append((first, pltpu.make_async_copy(src, dst, out_sem.at[slot, 24 + n])))
            piece = 6 * n
            for k in range(per - n_p):
                at = SEG * k
                while at < SEG * k + SEG:
                    owner = at // Q_ROWS
                    size = min(SEG * k + SEG, Q_ROWS * (owner + 1)) - at
                    src = stage.at[slot, :, pl.ds(SEG * n + at - SEG * k, size)]
                    for r in range(4):
                        dst = q_refs[r].at[zz, :, pl.ds(at - Q_ROWS * owner, size)]
                        copy = pltpu.make_async_copy(src, dst, out_sem.at[slot, piece])
                        found.append(((within == n_p + k) & (chip ^ owner == r), copy))
                    at += size
                    piece += 1
        return found

    def backward(c, _):
        u = pl.ds(pl.multiple_of(c * UNITS, UNITS), UNITS)
        slot = lax.rem(c, 2)

        @pl.when(c >= 2)
        def _():
            each(back_copies(c - 2, slot), wait)

        stage[slot, 0] = dot_tn(gg_s[:, u], a_all[:, 0:D]).astype(BF16)
        stage[slot, 1] = dot_tn(gu_s[:, u], a_all[:, 0:D]).astype(BF16)
        stage[slot, 2] = dot_tn(hid_s[:, u], c_all[...]).astype(BF16)
        each(back_copies(c, slot), start)
        return 0

    n_chunks = units // UNITS
    lax.fori_loop(0, n_chunks, backward, 0)
    for c in (n_chunks - 2, n_chunks - 1):
        each(back_copies(jnp.int32(c), c % 2), wait)
    for c in acc_copies:
        c.wait()


def ffn_call(info, a0, a1, c0, c1, own, here):
    t = a0.shape[0]
    units = 4 * CORE_UNITS
    return pl.pallas_call(
        ffn_kernel,
        out_shape=(
            jax.ShapeDtypeStruct((t, D), F32),
            jax.ShapeDtypeStruct((t, D), F32),
            jax.ShapeDtypeStruct((t, WIDE), BF16),
            jax.ShapeDtypeStruct((t, WIDE // 2), BF16),
            jax.ShapeDtypeStruct((t, WIDE // 2), BF16),
            jax.ShapeDtypeStruct((4, 3, P_ROWS, D), BF16),
            *[jax.ShapeDtypeStruct((4, 3, Q_ROWS, D), BF16)] * 4,
        ),
        in_specs=[SMEM] + [ANY] * 9,
        out_specs=(ANY,) * 10,
        scratch_shapes=[
            pltpu.VMEM((3, units, D), BF16),
            pltpu.VMEM((2 * t, WIDE), BF16),
            pltpu.VMEM((2 * t, D), BF16),
            pltpu.VMEM((2, D, t), BF16),
            pltpu.VMEM((2 * t, units), BF16),
            pltpu.VMEM((2 * t, units), BF16),
            pltpu.VMEM((2 * t, units), BF16),
            pltpu.VMEM((2, 3, UNITS, D), BF16),
            pltpu.VMEM((t, D), F32),
            pltpu.VMEM((t, D), F32),
            pltpu.VMEM((t, WIDE), BF16),
            pltpu.VMEM((t, WIDE // 2), BF16),
            pltpu.VMEM((t, WIDE // 2), BF16),
            pltpu.SemaphoreType.DMA((4,)),
            pltpu.SemaphoreType.DMA((24,)),
            pltpu.SemaphoreType.DMA((2, 28)),
            pltpu.SemaphoreType.DMA((5,)),
        ],
        compiler_params=params(60),
        cost_estimate=cost(50),
        name="feed_forward",
    )(info, a0, a1, c0, c1, own, *here)


def put_shards(ref, product, gain_grad):
    extra = ref.shape[-1] - product.shape[1]
    if extra:
        product = jnp.concatenate([product, jnp.zeros((product.shape[0], extra), F32)], axis=1)
    width = product.shape[1]
    first_row = lax.broadcasted_iota(jnp.int32, (ZP - ZR, width), 0) == 0
    for n in range(4):
        ref[n, 0:ZR, :] = product[ZR * n : ZR * n + ZR].astype(BF16)
        if gain_grad is None:
            ref[n, ZR:ZP, :] = jnp.zeros((ZP - ZR, width), BF16)
        else:
            part = jnp.concatenate(
                [gain_grad[:, ZR * n : ZR * n + ZR], jnp.zeros((1, width - ZR), F32)], axis=1
            )
            ref[n, ZR:ZP, :] = jnp.where(first_row, part, 0.0).astype(BF16)


def put_halves(core, keep_ref, send_ref, product, gain_grad):
    extra = jnp.zeros((product.shape[0], WIDE - product.shape[1]), F32)
    wide = jnp.concatenate([product, extra], axis=1)
    half = WIDE // 2
    for side, (first, second) in enumerate(((keep_ref, send_ref), (send_ref, keep_ref))):
        @pl.when(core == side)
        def _():
            put_shards(first, wide[:, :half], gain_grad)
            put_shards(second, wide[:, half:], None)


def epi_kernel(
    info, h1_ref, acc_g, got_lo, got_hi, ct_ref, gain_ref, w_ref, mid_ref, *refs
):
    gh_ref, gm_ref, keep_ref, send_ref, acc, total = refs
    i = pl.program_id(0)

    @pl.when(i == 0)
    def _():
        acc[...] = jnp.zeros((D, D), F32)
        total[...] = jnp.zeros((8, D), F32)

    h = h1_ref[...]
    factor = lax.rsqrt(jnp.mean(h * h, axis=-1, keepdims=True) + NORM_EPS)
    normed = h * factor
    got = jnp.concatenate([got_lo[...], got_hi[...]], axis=1)
    g = acc_g[...] + got[:, 0:D].astype(F32)
    scaled = g * gain_ref[1:2, :]
    back = factor * (scaled - normed * jnp.mean(scaled * normed, axis=-1, keepdims=True))
    full = ct_ref[...].T.astype(F32) + back
    gh_ref[...] = full
    res = full.astype(BF16)
    gm_ref[...] = dot_nt(res, w_ref[...]).astype(BF16)
    total[0:1, :] += jnp.sum(g * normed, axis=0, keepdims=True)
    acc[...] += dot_tn(mid_ref[...], res)

    @pl.when(i == pl.num_programs(0) - 1)
    def _():
        put_halves(info[1], keep_ref, send_ref, acc[...], total[0:1, :])


def epi_call(info, h1, acc_g, got_lo, got_hi, cot_t, gains, w_out, mid):
    t = h1.shape[0]
    rows = pl.BlockSpec((ROWS, D), lambda i: (i, 0))
    return pl.pallas_call(
        epi_kernel,
        grid=(t // ROWS,),
        out_shape=(
            jax.ShapeDtypeStruct((t, D), F32),
            jax.ShapeDtypeStruct((t, D), BF16),
            jax.ShapeDtypeStruct((4, ZP, WIDE // 2), BF16),
            jax.ShapeDtypeStruct((4, ZP, WIDE // 2), BF16),
        ),
        in_specs=[
            SMEM,
            rows,
            rows,
            by_rows(WIDE // 2),
            by_rows(WIDE // 2),
            by_lanes(D),
            whole((8, D)),
            whole((D, D)),
            rows,
        ],
        out_specs=(rows, rows) + (whole((4, ZP, WIDE // 2)),) * 2,
        scratch_shapes=[pltpu.VMEM((D, D), F32), pltpu.VMEM((8, D), F32)],
        compiler_params=params(60, 1),
        cost_estimate=cost(12),
        name="feed_forward_norm_back",
    )(info, h1, acc_g, got_lo, got_hi, cot_t, gains, w_out, mid)


def post_q_kernel(info, a_ref, g_ref, w_ref, _, keep_ref, send_ref, part_ref, acc):
    step = pl.program_id(0)

    @pl.when(step == 0)
    def _():
        acc[...] = jnp.zeros((D, D), F32)

    g = g_ref[...]
    part_ref[...] = dot_nt(g, w_ref[:, 0:D])
    acc[...] += dot_tn(a_ref[...], g)

    @pl.when(step == pl.num_programs(0) - 1)
    def _():
        put_halves(info[1], keep_ref, send_ref, acc[...], None)


def post_q_call(info, a, g, w, dep):
    t = a.shape[0]
    piece = (4, ZP, WIDE // 2)
    return pl.pallas_call(
        post_q_kernel,
        grid=(t // ROWS,),
        out_shape=(
            jax.ShapeDtypeStruct(piece, BF16),
            jax.ShapeDtypeStruct(piece, BF16),
            jax.ShapeDtypeStruct((t, D), F32),
        ),
        in_specs=[SMEM, by_rows(D), by_rows(D), whole(w.shape), ANY],
        out_specs=(whole(piece), whole(piece), by_rows(D)),
        scratch_shapes=[pltpu.VMEM((D, D), F32)],
        compiler_params=params(60, 1),
        cost_estimate=cost(8),
        name="query_back",
    )(info, a, g, w, dep)


def turn_back(slab, cos, sin, first_half, low_head):
    mixed = slab(2)
    k4 = jnp.where(low_head, 0.0, rope_slab(mixed, cos, sin, first_half))
    k01 = rope_slab(slab(0), cos, sin, first_half)
    k23 = rope_slab(slab(1), cos, sin, first_half)
    v4 = jnp.where(low_head, mixed, 0.0)
    return jnp.concatenate([k4, k01, k23, slab(3), slab(4), v4], axis=1).astype(BF16)


def kv_weights_back(info, cos, sin, turned, totals, dep):
    t = turned[0].shape[1]
    half = t // 2
    piece = ((4, ZP, 384), BF16)
    n_all = len(totals)

    def body(info, ins, outs, scratch):
        cos_ref, sin_ref = ins[0], ins[1]
        a_refs, g_refs = ins[2 : 2 + len(turned)], ins[2 + len(turned) :]
        first_half, low_head = lane_masks(ROWS)
        low, acc = scratch
        for c in range(n_all if n_all < 4 else 4):
            for i in range(t // ROWS):
                at = ROWS * i

                def slab(j):
                    lanes = slice(128 * j, 128 * j + 128)
                    if c < 3:
                        return g_refs[c][at : at + ROWS, lanes].astype(F32)
                    if at + ROWS <= half:
                        return g_refs[3][at : at + ROWS, lanes].astype(F32)
                    if at >= half:
                        return g_refs[4][at - half : at - half + ROWS, lanes].astype(F32)
                    parts = [g_refs[3][at:half, lanes], g_refs[4][0 : at + ROWS - half, lanes]]
                    return jnp.concatenate([p.astype(F32) for p in parts], axis=0)

                r = slice(t * c + at, t * c + at + ROWS)
                cos, sin = wide_tables(cos_ref[:, r], -sin_ref[:, r])
                low[at : at + ROWS, :] = turn_back(slab, cos, sin, first_half, low_head)
            for n, rows in enumerate((slice(0, D // 2), slice(D // 2, D))):
                value = dot(a_refs[2 * c + n][...], low[...])
                if c == 0:
                    acc[rows, :] = value
                else:
                    acc[rows, :] += value
        for core, (k_out, v_out) in enumerate(((outs[0], outs[1]), (outs[1], outs[0]))):
            @pl.when(info[1] == core)
            def _():
                put_shards(k_out, acc[:, 0:384], None)
                put_shards(v_out, acc[:, 384:768], None)

    return step_call(
        "key_value_weights_back",
        body,
        info,
        (cos, sin, *turned, *totals),
        (piece, piece),
        scratch=(pltpu.VMEM((t, 768), BF16), pltpu.VMEM((D, 768), F32)),
        behind=(dep,),
    )


def post_kv_kernel(
    info, s0, s1, s2, cos_ref, sin_ref, part_ref, w_ref, x_ref, gh_ref, gain_ref, ig_ref,
):
    first_half, low_head = lane_masks(ROWS)

    def slab(j):
        c = slice(128 * j, 128 * j + 128)
        return s0[:, c].astype(F32) + s1[:, c].astype(F32) + s2[:, c].astype(F32)

    cos, sin = wide_tables(cos_ref[...], -sin_ref[...])
    low = turn_back(slab, cos, sin, first_half, low_head)
    g = (
        part_ref[...]
        + dot_nt(low[:, 0:384], w_ref[:, 0:384])
        + dot_nt(low[:, 384:704], w_ref[:, 384:704])
    )
    x = x_ref[...].astype(F32)
    factor = lax.rsqrt(jnp.mean(x * x, axis=-1, keepdims=True) + NORM_EPS)
    normed = x * factor
    scaled = g * gain_ref[0:1, :]
    back = factor * (scaled - normed * jnp.mean(scaled * normed, axis=-1, keepdims=True))
    ig_ref[...] = (gh_ref[...] + back).astype(BF16).T


def post_kv_call(info, sums, cos, sin, part, w, x, gh, gain, dep):
    t = x.shape[0]
    return pl.pallas_call(
        lambda *refs: post_kv_kernel(*refs[:11], refs[12]),
        grid=(t // ROWS,),
        out_shape=jax.ShapeDtypeStruct((D, t), BF16),
        in_specs=[SMEM]
        + [by_rows(KV_LANES)] * 3
        + [by_lanes(32)] * 2
        + [by_rows(D), whole(w.shape)]
        + [by_rows(D)] * 2
        + [whole((8, D)), ANY],
        out_specs=by_lanes(D),
        compiler_params=params(60, 1),
        cost_estimate=cost(8),
        name="key_value_back",
    )(info, *sums, cos, sin, part, w, x, gh, gain, dep)


def finish_ffn(info, mine, other, dep):
    out = ((D, 2 * CORE_UNITS), F32)

    def body(info, ins, outs, scratch):
        rows = scratch[0]
        for n in range(3):
            for ref, side in ((ins[0], info[1]), (ins[1], 1 - info[1])):
                at = pl.multiple_of(side * CORE_UNITS, 16)
                rows[pl.ds(at, CORE_UNITS), :] = ref[n].astype(F32)
            outs[n][...] = rows[...].T

    return step_call(
        "finish_feed_forward",
        body,
        info,
        (mine, other),
        (out,) * 3,
        scratch=(pltpu.VMEM((2 * CORE_UNITS, D), F32),),
        behind=(dep,),
    )


def finish_rest(info, mine, other, w_own):
    half = WIDE // 2

    def body(info, ins, outs, scratch):
        wq_ref, wo_ref, wk_ref, wv_ref, one_ref, two_ref = outs

        def emit(first, second):
            def both(at):
                lanes = slice(at, at + half)
                return jnp.concatenate([first[0:ZR, lanes], second[0:ZR, lanes]], axis=1)

            wo_ref[...] = both(0).astype(F32)[:, 0:D]
            query = both(half).astype(F32)[:, 0:D]
            wq_ref[...] = query
            k = first[:, WIDE : WIDE + 384].astype(F32)
            v = second[:, WIDE : WIDE + 384].astype(F32)
            k_t = k.T
            wk_ref[...] = jnp.concatenate([k_t[128:384], k_t[64:128]], axis=0)[:, 0:ZR]
            wv_ref[...] = v.T[0:320, 0:ZR]
            w = ins[2][...].astype(F32)
            total = jnp.sum(query * w[:, 0:D], axis=1, keepdims=True)
            total += jnp.sum(k[0:ZR, 128:384] * w[:, 1024:1280], axis=1, keepdims=True)
            total += jnp.sum(k[0:ZR, 64:128] * w[:, 960:1024], axis=1, keepdims=True)
            total += jnp.sum(v[0:ZR, 0:320] * w[:, 1280:1600], axis=1, keepdims=True)
            total = total / w[:, 1600:1601]
            one_ref[...] = jnp.broadcast_to(total, (ZR, 128)).T[0:1, :]
            two_ref[...] = first[ZR:ZP, :].astype(F32)[0:1, 0:ZR]

        for core, refs in enumerate(((ins[0], ins[1]), (ins[1], ins[0]))):
            @pl.when(info[1] == core)
            def _():
                emit(*refs)

    outs = (((ZR, D), F32), ((ZR, D), F32), ((320, ZR), F32), ((320, ZR), F32), ((1, ZR), F32), ((1, ZR), F32))
    return step_call("finish_rest", body, info, (mine, other, w_own), outs)


def sum_chips(info, terms, over_z, passed, behind):
    n_terms = len(terms)
    cut = P_ROWS // 2

    def body(info, ins, outs, scratch):
        for zz in range(4):
            outs[0][zz] = sum(ins[k][zz].astype(F32) for k in range(n_terms)).astype(BF16)
        for n in range(2):
            outs[1 + n][...] = ins[n_terms][0, :, cut * n : cut * n + cut, :]

    outs = ((terms[0].shape, BF16),) + (((3, cut, D), BF16),) * 2
    return step_call(
        "sum_chips", body, info, (*terms, over_z), outs, behind=behind, passed=passed
    )


def join_cores(info, keep_near, recv_near, keep_far, recv_far, pairs):
    rows = keep_far.shape[0]
    cut = rows // 2

    def body(info, ins, outs, scratch):
        for n in range(3):
            r = slice(rows * n, rows * n + rows)
            outs[n][...] = ins[0][r, :] + ins[1][r, :]
        for n in range(2):
            r = slice(cut * n, cut * n + cut)
            outs[3 + n][...] = ins[2][r, :] + ins[3][r, :]
        for n in range(len(pairs)):
            outs[5 + n][...] = ins[4 + 2 * n][...] + ins[5 + 2 * n][...]

    outs = (((rows, KV_LANES), BF16),) * 3 + (((cut, KV_LANES), BF16),) * 2
    outs += tuple((a.shape, BF16) for a, _ in pairs)
    flat = [a for pair in pairs for a in pair]
    return step_call(
        "join_cores", body, info, (keep_near, recv_near, keep_far, recv_far, *flat), outs
    )


def join_near(info, to_x, to_y, from_x, from_y, pairs, passed):
    cut = from_x.shape[0]
    rows = pairs[0][0].shape[1]

    def body(info, ins, outs, scratch):
        to_x, to_y, from_x, from_y = ins[:4]
        outs[0][0:cut, :] = to_x[0:cut, :]
        outs[0][cut : 2 * cut, :] = to_x[cut : 2 * cut, :] + from_y[...]
        outs[1][0:cut, :] = to_y[0:cut, :] + from_x[...]
        outs[1][cut : 2 * cut, :] = to_y[cut : 2 * cut, :]
        for n in range(2):
            outs[2][:, rows * n : rows * n + rows, :] = ins[4 + 2 * n][...] + ins[5 + 2 * n][...]

    flat = [a for pair in pairs for a in pair]
    return step_call(
        "join_near",
        body,
        info,
        (to_x, to_y, from_x, from_y, *flat),
        ((to_x.shape, BF16),) * 2 + (((3, P_ROWS, D), BF16),),
        passed=passed,
    )


def join_projections(info, q_pair, kv_pair, h1, acc_o, got_o, dep):
    t = h1.shape[0]
    half = WIDE // 2

    def body(info, ins, outs, scratch):
        outs[0][:, :, 0:half] = ins[0][...] + ins[1][...]
        outs[0][:, :, half : half + 384] = ins[2][...] + ins[3][...]
        for i in range(t // ROWS):
            r = slice(ROWS * i, ROWS * i + ROWS)
            value = ins[4][r, :] + ins[5][r, :] + ins[6][r, 0:D].astype(F32)
            outs[1][:, r] = value.astype(BF16).T

    return step_call(
        "join_projections",
        body,
        info,
        (*q_pair, *kv_pair, h1, acc_o, got_o),
        (((4, ZP, half + 384), BF16), ((D, t), BF16)),
        behind=(dep,),
    )


def halve_rows(info, left, right, behind):
    rows = left.shape[1] // 2
    lanes = left.shape[2], right.shape[2]

    def body(info, ins, outs, scratch):
        for n in range(2):
            r = slice(rows * n, rows * n + rows)
            outs[n][:, 0 : lanes[0]] = ins[0][0, r, :]
            outs[n][:, lanes[0] : sum(lanes)] = ins[1][0, r, :]

    outs = (((rows, sum(lanes)), BF16),) * 2
    return step_call("halve_rows", body, info, (left, right), outs, behind=behind)


def add_pairs(info, pairs, behind=()):
    def body(info, ins, outs, scratch):
        for n in range(len(pairs)):
            outs[n][...] = ins[2 * n][...] + ins[2 * n + 1][...]

    flat = [a for pair in pairs for a in pair]
    outs = tuple((a.shape, BF16) for a, _ in pairs)
    return step_call("add_pairs", body, info, flat, outs, behind=behind)


def stack_two(info, first, second, behind):
    def body(info, ins, outs, scratch):
        for n in range(2):
            outs[0][n] = ins[n][...]

    out = ((2,) + first.shape, BF16)
    return step_call("stack_two", body, info, (first, second), (out,), behind=behind)[0]


def stack_pairs(info, pairs, dep):
    rows = pairs[0][0].shape[0]

    def body(info, ins, outs, scratch):
        for n in range(2):
            outs[0][rows * n : rows * n + rows, :] = ins[2 * n][...] + ins[2 * n + 1][...]

    flat = [a for pair in pairs for a in pair]
    shape = (2 * rows,) + pairs[0][0].shape[1:]
    return step_call("stack_pairs", body, info, flat, ((shape, BF16),), behind=(dep,))[0]


def join_ffn(info, first, near, far, dep):
    def body(info, ins, outs, scratch):
        chip = info[3]
        out = outs[0]
        out[:, 0:P_ROWS, :] = ins[0][...]
        for r in range(4):
            at = pl.multiple_of(P_ROWS + Q_ROWS * (chip ^ r), 16)
            out[:, pl.ds(at, Q_ROWS), :] = ins[1 + r // 2][r % 2]

    return step_call(
        "join_feed_forward",
        body,
        info,
        (first, near, far),
        (((3, CORE_UNITS, D), BF16),),
        behind=(dep,),
    )[0]


def rows_after(x, start, size, tok, axis=0):
    return lax.dynamic_slice_in_dim(x, start + tok, size, axis=axis)


def z_shift(x, step):
    n = 4
    return lax.ppermute(x, "fsdp", [(i, (i + step) % n) for i in range(n)])


def c_swap(x, bit):
    n = lax.axis_size("ctx")
    return lax.ppermute(x, "ctx", [(i, i ^ bit) for i in range(n)])


def bits_from(b):
    bits = []
    while b < lax.axis_size("ctx"):
        bits.append(b)
        b *= 2
    return bits


def chip_near(kv):
    if lax.axis_size("ctx") != 8:
        return ()
    return c_swap(kv, 2), c_swap(kv, 4)


def chip_far(kv, near):
    if not near:
        return [lax.all_gather(kv, "ctx", axis=0, tiled=True)]
    cut = kv.shape[0] // 2
    across_x, across_y = near
    far_lo = c_swap(across_x[:cut], 4)
    far_hi = c_swap(across_y[cut:], 2)
    chip = [kv, across_x, across_y, far_lo, far_hi]
    return chip + [c_swap(part, 1) for part in chip]


def kv_entry(position, per_dev, me, n):
    if n != 8:
        return position
    owner, within = position // per_dev, position % per_dev
    rel = owner ^ me
    cut = per_dev // 2
    far = (rel // 2) == 3
    late = far & (within >= cut)
    which = (rel % 2) * 5 + rel // 2 + late.astype(jnp.int32)
    return which * 1024 + jnp.where(late, within - cut, within)


def kv_slot(position, per_dev, me):
    owner, within = position // per_dev, position % per_dev
    rel = owner ^ me
    return ((rel % 2) * 4 + rel // 2) * per_dev + within


def on_device(
    tokens,
    cotangent,
    doc_lengths,
    deal,
    attn_gain,
    w_query,
    w_key,
    w_value,
    w_out,
    mlp_gain,
    w_gate,
    w_up,
    w_down,
):
    me = lax.axis_index("ctx")
    n_ctx = lax.axis_size("ctx")
    z = lax.axis_index("fsdp")
    core = me % 2
    near_me = me % 8
    chip = near_me // 2
    parity = (chip + chip // 2) % 2
    info = jnp.stack([z, core, near_me, chip, parity]).astype(jnp.int32)
    tok_rows = tokens.shape[1]
    per_dev = tok_rows // BLK
    deal_row = deal[0]
    blocks = deal_row.shape[0]
    group_size = blocks * BLK
    doc_lens = doc_lengths[0]
    seq_count = doc_lens.shape[0]
    length = group_size // seq_count
    x_turned = tokens[0].T
    cot_turned = cotangent[0].T

    block_ids = jnp.arange(blocks, dtype=jnp.int32)
    mine = lax.dynamic_slice_in_dim(deal_row, me * per_dev, per_dev)
    seq_blocks = jnp.maximum(
        mine[:, None] - (NWB - 1) + jnp.arange(NWB, dtype=jnp.int32)[None, :], 0
    )
    position = jnp.sum(
        jnp.where(seq_blocks[:, :, None] == deal_row[None, None, :], block_ids, 0), axis=-1
    )
    tab = kv_entry(position, per_dev, me, n_ctx).astype(jnp.int32)
    doc_ends = (
        jnp.cumsum(doc_lens, axis=1) + (jnp.arange(seq_count, dtype=jnp.int32) * length)[:, None]
    ).reshape(-1)
    doc_starts = doc_ends - doc_lens.reshape(-1)
    q_time = mine[:, None] * BLK + jnp.arange(BLK, dtype=jnp.int32)[None, :]
    begin = jnp.max(jnp.where(q_time[..., None] >= doc_starts, doc_starts, 0), axis=-1)
    lo = jnp.maximum(begin, q_time - (WIN - 1)) - (mine[:, None] * BLK - WIN)
    lo = lo[:, None, :].astype(jnp.int32)
    n_chips = 4 if n_ctx == 8 else 1
    owners = jnp.stack([me ^ (2 * r) for r in range(n_chips)])
    theirs = jnp.sum(
        jnp.where(
            block_ids == (owners[:, None] * per_dev + jnp.arange(per_dev, dtype=jnp.int32))[..., None],
            deal_row,
            0,
        ),
        axis=-1,
    )
    their_time = theirs[:, :, None] * BLK + jnp.arange(BLK, dtype=jnp.int32)
    their_begin = jnp.max(jnp.where(their_time[..., None] >= doc_starts, doc_starts, 0), axis=-1)
    pos = (their_time - their_begin).reshape(-1)
    half_dim = HD // 2
    freqs = ROPE_THETA ** (-jnp.arange(half_dim, dtype=F32) * (2.0 / HD))
    angle = freqs[:, None] * pos.astype(F32)[None, :]
    cos_turn, sin_turn = jnp.cos(angle), jnp.sin(angle)

    gains_wide = jnp.concatenate(
        [attn_gain[:, None], mlp_gain[:, None], jnp.zeros((ZR, QKV - 1602), BF16)], axis=1
    )
    w_parts = [w_query, w_key[:, 256:], w_key[:, :256], w_value, gains_wide]
    start = jnp.minimum(32 * near_me, ZR - 32)
    w_mine = jnp.concatenate(
        [lax.dynamic_slice_in_dim(w, start, 32, axis=0) for w in w_parts], axis=1
    )
    w_z = [z_shift(w_mine, -1), z_shift(w_mine, 2), z_shift(w_mine, 1)]
    own_half, packed = prep_weights(info, w_gate, w_up, w_down.T)
    w_got, packed = stack_weights(info, w_z, (cos_turn, sin_turn), (packed,))
    over_z = lax.all_gather(packed, "fsdp", axis=0, tiled=False)
    cot_there = c_swap(cot_turned, 1)
    w_chips = [w_got, c_swap(w_got, 2), c_swap(w_got, 4), c_swap(w_got, 6)]
    w_pieces = [jnp.concatenate(w_parts, axis=1)]
    for piece in w_chips:
        w_pieces += [piece, c_swap(piece, 1)]

    attn_in, attn_up, attn_lo, q_low, kv_low, x, gains, w_q, w_kv = pre_call(
        info, x_turned, cos_turn, sin_turn, w_pieces
    )
    kvs = chip_far(kv_low, chip_near(kv_low))

    first, second = split_quarters(info, over_z, kvs[3:5] if n_ctx == 8 else kvs)
    first_on, second_on = c_swap(first, 2), c_swap(second, 4)
    out_mine = lax.dynamic_slice_in_dim(w_out, (ZR - OUT_ROWS) * core, OUT_ROWS, axis=0)
    out_mine = meet(info, (out_mine,), (first,))[0]
    out_here = [z_shift(out_mine, -1), z_shift(out_mine, 2), z_shift(out_mine, 1)]
    mid_low, recips, probs = fwd_call(tab, lo, q_low, kvs)
    *out_here, first_on, second_on = meet(info, (*out_here, first_on, second_on), (mid_low,))
    out_there = [c_swap(p, 1) for p in out_here]
    here = (first, second, first_on, second_on)
    h1, mlp_in, w_out_all, attn_up, attn_lo = pro_call(
        info, mid_low, x, gains, w_out, out_here, out_there, cot_there, (attn_up, attn_lo)
    )
    acc_o, acc_g, send_o, send_lo, send_hi, p_both, *q_both = ffn_call(
        info, mlp_in, c_swap(mlp_in, 1), cot_turned, cot_there, own_half, here
    )
    p_sum = lax.psum_scatter(p_both, "fsdp", scatter_dimension=0, tiled=True)
    q_got = [c_swap(q_both[r], 2 * r) for r in range(1, 4)]
    got_o = c_swap(send_o, 1)
    attn_turned = [attn_up, attn_lo]
    a_x = [c_swap(a, 2) for a in attn_turned]
    a_y = [c_swap(a, 4) for a in attn_turned]
    send_lo, send_hi, *a_near = meet(info, (send_lo, send_hi, *a_x, *a_y))
    got_lo, got_hi = c_swap(send_lo, 1), c_swap(send_hi, 1)
    grad_hidden, grad_mid, go_keep, go_send = epi_call(
        info, h1, acc_g, got_lo, got_hi, cot_turned, gains, w_out_all, mid_low
    )
    a_turned = [*attn_turned, *a_near, c_swap(a_near[0], 4), c_swap(a_near[3], 2)]

    if n_ctx == 8:
        out_units = (3, 1, 3, 1)
        slots = kv_slot(position, per_dev, me).astype(jnp.int32)
    else:
        out_units = (NWB,)
        n_slots = per_dev * NWB
        flat_pos = position.reshape(-1)
        order = jnp.arange(n_slots, dtype=jnp.int32)
        slots = jnp.min(
            jnp.where(flat_pos[:, None] == flat_pos[None, :], order[None, :], n_slots), axis=1
        ).reshape(per_dev, NWB)
        source = jnp.min(
            jnp.where(block_ids[:, None] == flat_pos[None, :], order[None, :], n_slots), axis=1
        )

    def own_rows(parts):
        width = parts[0].shape[1]
        padded = jnp.concatenate(
            [parts[0].reshape(n_slots, BLK, width), jnp.zeros((1, BLK, width), BF16)], axis=0
        )
        spread = jnp.take(padded, source, axis=0).reshape(group_size, width)
        own = lax.psum_scatter(spread, "ctx", scatter_dimension=0, tiled=True)
        return own, (own, jnp.zeros_like(own), jnp.zeros_like(own))

    back_args = (
        tab, slots, out_units, q_low, grad_mid, mid_low, recips, probs, cos_turn, sin_turn, kvs
    )
    dq, *kv_parts = bwd_call(0, per_dev, (), (), *back_args)
    q_terms = (q_both[0], *q_got)
    go_pair = (go_keep, c_swap(go_send, 1))
    if n_ctx == 8:
        keep_near, keep_far, send_near, send_far = kv_parts
        q_sum, p_l, p_r, send_near, send_far, a_lo, a_hi = sum_chips(
            info, q_terms, p_sum, (send_near, send_far, *a_turned[6:]), (dq,)
        )
        a_turned[6:] = [a_lo, a_hi]
        own, to_x, to_y, far_lo, far_hi, go_both, p_l, p_r = join_cores(
            info,
            keep_near,
            c_swap(send_near, 1),
            keep_far,
            c_swap(send_far, 1),
            (go_pair, (p_l, c_swap(p_l, 2)), (p_r, c_swap(p_r, 4))),
        )
        totals = (own, to_x, to_y, far_lo, far_hi)
    else:
        q_sum, p_l, p_r = sum_chips(info, q_terms, p_sum, (), (dq,))
        own, sums = own_rows(kv_parts)
        a_turned, totals = a_turned[:2], (own,)
        go_both, p_l, p_r = add_pairs(
            info, (go_pair, (p_l, c_swap(p_l, 2)), (p_r, c_swap(p_r, 4)))
        )
    q_mine = lax.psum_scatter(q_sum, "fsdp", scatter_dimension=0, tiled=True)[0]
    for b in bits_from(8):
        q_mine = q_mine + c_swap(q_mine, b)
    gq_keep, gq_send, part = post_q_call(info, attn_in, dq, w_q, own)
    go_sum = lax.psum_scatter(go_both, "fsdp", scatter_dimension=0, tiled=True)
    gkv_keep, gkv_send = kv_weights_back(info, cos_turn, sin_turn, a_turned, totals, gq_keep)
    p_pairs = ((p_l, c_swap(p_l, 4)), (p_r, c_swap(p_r, 2)))
    if n_ctx == 8:
        to_x, to_y, p_sum, gq_send, gkv_send, q_mine = join_near(
            info,
            to_x,
            to_y,
            c_swap(far_lo, 2),
            c_swap(far_hi, 4),
            p_pairs,
            (gq_send, gkv_send, q_mine),
        )
        sums = (own, c_swap(to_x, 2), c_swap(to_y, 4))
    else:
        p_sum = jnp.concatenate([a + b for a, b in p_pairs], axis=1)
    g_both, output = join_projections(
        info, (gq_keep, c_swap(gq_send, 1)), (gkv_keep, c_swap(gkv_send, 1)), h1, acc_o, got_o, p_sum
    )
    g_sum = lax.psum_scatter(g_both, "fsdp", scatter_dimension=0, tiled=True)
    q_near = stack_two(info, q_mine, c_swap(q_mine, 2), (output,))
    q_far = c_swap(q_near, 4)
    input_grad = post_kv_call(
        info, sums, cos_turn, sin_turn, part, w_kv, x, grad_hidden, gains, q_near
    )
    for b in bits_from(8):
        p_sum = p_sum + c_swap(p_sum, b)
    ffn_sum = join_ffn(info, p_sum, q_near, q_far, input_grad)
    g_l, g_r = halve_rows(info, go_sum, g_sum, (ffn_sum,))
    g_l, g_r = add_pairs(info, ((g_l, c_swap(g_l, 2)), (g_r, c_swap(g_r, 4))))
    gate_grad, up_grad, down_grad = finish_ffn(info, ffn_sum, c_swap(ffn_sum, 1), g_l)
    g_sum = stack_pairs(info, ((g_l, c_swap(g_l, 4)), (g_r, c_swap(g_r, 2))), gate_grad)
    for b in bits_from(8):
        g_sum = g_sum + c_swap(g_sum, b)
    query_grad, out_grad, key_grad, value_grad, gain_one, gain_two = finish_rest(
        info, g_sum, c_swap(g_sum, 1), w_pieces[0]
    )

    return (
        output.T[None],
        input_grad.T[None],
        gain_one.reshape(ZR),
        query_grad,
        key_grad.T,
        value_grad.T,
        out_grad,
        gain_two.reshape(ZR),
        gate_grad,
        up_grad,
        down_grad.T,
    )


def solution(mesh):
    in_specs = (
        P("fsdp", "ctx", None),
        P("fsdp", "ctx", None),
        P("fsdp", None, None),
        P("fsdp", None),
        P("fsdp"),
        P("fsdp", None),
        P("fsdp", None),
        P("fsdp", None),
        P("fsdp", None),
        P("fsdp"),
        P(None, "fsdp"),
        P(None, "fsdp"),
        P("fsdp", None),
    )
    out_specs = (
        P("fsdp", "ctx", None),
        P("fsdp", "ctx", None),
        P("fsdp"),
        P("fsdp", None),
        P("fsdp", None),
        P("fsdp", None),
        P("fsdp", None),
        P("fsdp"),
        P(None, "fsdp"),
        P(None, "fsdp"),
        P("fsdp", None),
    )
    return jax.shard_map(
        on_device, mesh=mesh, in_specs=in_specs, out_specs=out_specs, check_vma=False
    )
```

```python
import jax
import jax.numpy as jnp
from jax import lax
from jax.experimental import pallas as pl
from jax.experimental.pallas import tpu as pltpu
from jax.sharding import PartitionSpec as P

HQ = 15
KVH = 5
HD = 64
BLK = 128
WIN = 1024
D = 960
GRP = HQ // KVH
SPAN = WIN + BLK
NWB = SPAN // BLK
ROWS = 256
ZR = 240
ZP = 256
UNITS = 256
WIDE = 1024
QKV = 1664

NORM_EPS = 1e-05
ROPE_THETA = 100000.0
MASK_FILL = -1e30
F32 = jnp.float32
BF16 = jnp.bfloat16
MIB = 1024 * 1024

VMEM = pl.BlockSpec(memory_space=pltpu.VMEM)
SMEM = pl.BlockSpec(memory_space=pltpu.SMEM)
ANY = pl.BlockSpec(memory_space=pl.ANY)

KV_LANES = 640
PAIRS = (
    (0, 3, (0, 1), True, True),
    (1, 4, (2, 3), True, True),
    (2, 2, (4,), False, True),
)

CORE_UNITS = 320
QUARTER = 160
OUT_ROWS = 128
PACKED = 3 * QUARTER
CUT = 3 * PACKED // 2

P_ROWS = 128
Q_ROWS = 48
SEG = 64


def dot(a, b):
    return jnp.dot(a, b, preferred_element_type=F32)


def dot_nt(a, b):
    return lax.dot_general(a, b, (((1,), (1,)), ((), ())), preferred_element_type=F32)


def dot_tn(a, b):
    return lax.dot_general(a, b, (((0,), (0,)), ((), ())), preferred_element_type=F32)


def params(mib, grid_dims=0):
    return pltpu.CompilerParams(
        vmem_limit_bytes=mib * MIB,
        dimension_semantics=("arbitrary",) * grid_dims if grid_dims else None,
    )


def cost(micros):
    return pl.CostEstimate(flops=int(3.5e8 * micros), bytes_accessed=1, transcendentals=0)


def rope_slab(t, cos, sin_signed, first_half):
    swapped = jnp.where(first_half, pltpu.roll(t, 96, 1), pltpu.roll(t, 32, 1))
    return t * cos + swapped * sin_signed


def wide_tables(cos, sin):
    return (
        jnp.concatenate([cos] * 4, axis=0).T,
        jnp.concatenate([-sin, sin, -sin, sin], axis=0).T,
    )


def lane_masks(rows):
    lane = lax.broadcasted_iota(jnp.int32, (rows, 128), 1)
    return (lane % HD) < HD // 2, lane < HD


def rel_z(z, i):
    return lax.rem(z + 1 + i, 4)


def each(found, act):
    for cond, c in found:
        if cond is None:
            act(c)
        else:
            pl.when(cond)(lambda c=c: act(c))


def start(c):
    c.start()


def wait(c):
    c.wait()


def run_copies(pairs, sems):
    copies = [pltpu.make_async_copy(a, b, sems.at[i]) for i, (a, b) in enumerate(pairs)]
    for c in copies:
        c.start()
    for c in copies:
        c.wait()


MICROS = {
    "stack_two": 1,
    "meet": 1,
    "prep_weights": 5,
    "stack_weights": 2,
    "split_quarters": 5,
    "pick_out_rows": 3,
    "sum_chips": 4,
    "join_cores": 5,
    "key_value_weights_back": 11,
    "join_near": 4,
    "join_projections": 7,
    "add_pairs": 3,
    "stack_pairs": 2,
    "halve_rows": 2,
    "join_feed_forward": 3,
    "finish_feed_forward": 6,
    "finish_rest": 4,
}


def whole(shape):
    return pl.BlockSpec(shape, lambda i: (0,) * len(shape))


def step_call(
    name, body, info, ins, outs, far=(), scratch=(), behind=(), passed=()
):
    n_in, n_out, n_behind, n_passed = len(ins), len(outs), len(behind), len(passed)

    def kernel(info_ref, *refs):
        after = refs[n_in + n_behind + n_passed :]
        body(info_ref, refs[:n_in], after[:n_out], after[n_out + n_passed :])

    return pl.pallas_call(
        kernel,
        grid=(1,),
        out_shape=tuple(jax.ShapeDtypeStruct(shape, dtype) for shape, dtype in outs)
        + tuple(jax.ShapeDtypeStruct(p.shape, p.dtype) for p in passed),
        in_specs=[SMEM]
        + [ANY if n in far else whole(x.shape) for n, x in enumerate(ins)]
        + [ANY] * (n_behind + n_passed),
        out_specs=tuple(whole(shape) for shape, _ in outs) + (ANY,) * n_passed,
        scratch_shapes=list(scratch),
        input_output_aliases={1 + n_in + n_behind + n: n_out + n for n in range(n_passed)},
        compiler_params=params(60, 1),
        cost_estimate=cost(MICROS[name]),
        name=name,
    )(info, *ins, *behind, *passed)


def meet(info, passed, behind=()):
    return step_call("meet", lambda *refs: None, info, (), (), behind=behind, passed=passed)


def prep_weights(info, w_gate, w_up, w_down_turned, w_out):
    def body(info, ins, outs, scratch):
        core, parity = info[1], info[4]
        turn, given, sems = scratch
        base = core * CORE_UNITS
        copies = [pltpu.make_async_copy(ins[n], given.at[n], sems.at[n]) for n in range(3)]
        for c in copies:
            c.start()
        row = pl.multiple_of((ZR - OUT_ROWS) * core, 16)
        outs[2][...] = ins[3][pl.ds(row, OUT_ROWS), :]
        for n in range(3):
            copies[n].wait()
            turn[...] = given[n].T
            outs[0][n] = turn[pl.ds(pl.multiple_of(base, 16), CORE_UNITS), :]
            quarter = pl.ds(pl.multiple_of(base + QUARTER * parity, 16), QUARTER)
            outs[1][QUARTER * n : QUARTER * n + QUARTER, :] = turn[quarter, :]

    return step_call(
        "prep_weights",
        body,
        info,
        (w_gate, w_up, w_down_turned, w_out),
        (((3, CORE_UNITS, D), BF16), ((PACKED, D), BF16), ((OUT_ROWS, D), BF16)),
        far=range(3),
        scratch=(
            pltpu.VMEM((2 * CORE_UNITS, D), BF16),
            pltpu.VMEM((3,) + w_gate.shape, BF16),
            pltpu.SemaphoreType.DMA((3,)),
        ),
    )


def stack_weights(info, parts, behind, passed):
    def body(info, ins, outs, scratch):
        for n in range(3):
            outs[0][n] = ins[n][...]

    out = ((3,) + parts[0].shape, BF16)
    return step_call("stack_weights", body, info, parts, (out,), behind=behind, passed=passed)


def split_quarters(info, over_z, deps):
    at = CUT - PACKED

    def body(info, ins, outs, scratch):
        src = ins[0]
        z = info[0]
        zs = [rel_z(z, i) for i in range(3)]
        pairs = [
            (src.at[zs[0]], outs[0].at[pl.ds(0, PACKED)]),
            (src.at[zs[1], pl.ds(0, at)], outs[0].at[pl.ds(PACKED, at)]),
            (src.at[zs[1], pl.ds(at, PACKED - at)], outs[1].at[pl.ds(0, PACKED - at)]),
            (src.at[zs[2]], outs[1].at[pl.ds(PACKED - at, PACKED)]),
        ]
        run_copies(pairs, scratch[0])

    half = (CUT, D)
    return step_call(
        "split_quarters",
        body,
        info,
        (over_z, *deps),
        ((half, BF16), (half, BF16)),
        range(1 + len(deps)),
        scratch=(pltpu.SemaphoreType.DMA((4,)),),
    )


def pre_kernel(info, xt_ref, cos_ref, sin_ref, *refs):
    own, pieces = refs[0], refs[1:9]
    attn_ref, attn_up, attn_lo, q_ref, kv_ref, x_ref, gains_ref, wq_out, wkv_out = refs[9:18]
    w_ref, sems, out_sems = refs[18:]
    step = pl.program_id(0)
    z, me = info[0], info[2]
    outs = [
        pltpu.make_async_copy(w_ref.at[:, pl.ds(0, WIDE)], wq_out, out_sems.at[0]),
        pltpu.make_async_copy(w_ref.at[:, pl.ds(896, QKV - 896)], wkv_out, out_sems.at[1]),
    ]

    def pieces_do(act):
        found = []

        def add(src, row, size, cond=None):
            view = w_ref.at[pl.ds(pl.multiple_of(row, 16), size)]
            found.append((cond, pltpu.make_async_copy(src, view, sems.at[len(found)])))

        add(own, z * ZR, ZR)
        for rel, piece in enumerate(pieces):
            c = me ^ rel
            for i in range(3):
                base = rel_z(z, i) * ZR
                add(piece.at[i, pl.ds(0, 16)], base + 32 * c, 16, c < 7)
                add(piece.at[i, pl.ds(16, 16)], base + jnp.minimum(32 * c + 16, ZR - 16), 16)
        each(found, act)

    @pl.when(step == 0)
    def _():
        pieces_do(start)

    first_half, low_head = lane_masks(ROWS)
    cos, sin = wide_tables(cos_ref[...], sin_ref[...])
    x_low = xt_ref[...].T
    x_ref[...] = x_low
    x = x_low.astype(F32)
    factor = lax.rsqrt(jnp.mean(x * x, axis=-1, keepdims=True) + NORM_EPS)

    @pl.when(step == 0)
    def _():
        pieces_do(wait)
        for c in outs:
            c.start()
        gains_ref[...] = w_ref[:, 1536:QKV].astype(F32).T[64:72]

    a = (x * factor * gains_ref[0:1, :]).astype(BF16)
    attn_ref[...] = a
    turned_a = a.T
    attn_up[...] = turned_a[0 : D // 2]
    attn_lo[...] = turned_a[D // 2 :]
    qk = dot(a, w_ref[:, 0:1280])
    vv = dot(a, w_ref[:, 1280:QKV])
    slabs = [rope_slab(qk[:, 128 * j : 128 * j + 128], cos, sin, first_half) for j in range(10)]
    for j in range(7):
        q_ref[:, 128 * j : 128 * j + 128] = slabs[j].astype(BF16)
    q_ref[:, 896:960] = slabs[7][:, :64].astype(BF16)
    mixed = jnp.where(low_head, vv[:, 256:384], slabs[7])
    for j, part in enumerate((slabs[8], slabs[9], mixed, vv[:, 0:128], vv[:, 128:256])):
        kv_ref[:, 128 * j : 128 * j + 128] = part.astype(BF16)

    @pl.when(step == pl.num_programs(0) - 1)
    def _():
        for c in outs:
            c.wait()


def by_rows(width):
    return pl.BlockSpec((ROWS, width), lambda i: (i, 0))


def by_lanes(height):
    return pl.BlockSpec((height, ROWS), lambda i: (0, i))


def pre_call(info, xt, cos, sin, pieces):
    t = xt.shape[1]
    return pl.pallas_call(
        pre_kernel,
        grid=(t // ROWS,),
        out_shape=(
            jax.ShapeDtypeStruct((t, D), BF16),
            jax.ShapeDtypeStruct((D // 2, t), BF16),
            jax.ShapeDtypeStruct((D // 2, t), BF16),
            jax.ShapeDtypeStruct((t, D), BF16),
            jax.ShapeDtypeStruct((t, KV_LANES), BF16),
            jax.ShapeDtypeStruct((t, D), BF16),
            jax.ShapeDtypeStruct((8, D), F32),
            jax.ShapeDtypeStruct((D, WIDE), BF16),
            jax.ShapeDtypeStruct((D, QKV - 896), BF16),
        ),
        in_specs=[SMEM, by_lanes(D), by_lanes(32), by_lanes(32)] + [ANY] * 9,
        out_specs=(
            by_rows(D), by_lanes(D // 2), by_lanes(D // 2), by_rows(D), by_rows(KV_LANES), by_rows(D), whole((8, D)),
            ANY, ANY,
        ),
        scratch_shapes=[
            pltpu.VMEM((D, QKV), BF16),
            pltpu.SemaphoreType.DMA((49,)),
            pltpu.SemaphoreType.DMA((2,)),
        ],
        compiler_params=params(60, 1),
        cost_estimate=cost(12),
        name="pre",
    )(info, xt, cos, sin, *pieces)


def start_window(tab, kvs, win, sem, blk, slot):
    def body(j, _):
        entry = tab[blk, j]
        which = entry // 1024
        idx = lax.rem(entry, 1024)
        dst = win.at[slot, pl.ds(pl.multiple_of(j * BLK, BLK), BLK)]
        for n, ref in enumerate(kvs):
            @pl.when(which == n)
            def _():
                src = ref.at[pl.ds(pl.multiple_of(idx * BLK, BLK), BLK)]
                pltpu.make_async_copy(src, dst, sem.at[slot]).start()
        return 0

    lax.fori_loop(0, NWB, body, 0)


def next_window(tab, kvs, win, sem, first=0):
    i = pl.program_id(0)
    slot = lax.rem(i, 2)

    @pl.when(i == 0)
    def _():
        start_window(tab, kvs, win, sem, i + first, slot)

    @pl.when(i + 1 < pl.num_programs(0))
    def _():
        start_window(tab, kvs, win, sem, i + first + 1, 1 - slot)

    pltpu.make_async_copy(win.at[slot], win.at[slot], sem.at[slot]).wait()
    return slot


def turned(flat):
    rows = flat.astype(F32)
    extra = -rows.shape[1] % 128
    if extra:
        rows = jnp.concatenate([rows, jnp.zeros((rows.shape[0], extra), F32)], axis=1)
    return rows.T


def unturned(parts):
    rows = sum(p.shape[0] for p in parts)
    extra = -rows % 128
    if extra:
        parts = parts + [jnp.zeros((extra, parts[0].shape[1]), F32)]
    return jnp.concatenate(parts, axis=0).T[:, :rows].astype(BF16)


def spread_heads(rows, count, low):
    width = GRP * BLK
    sides = [jnp.concatenate(rows[GRP * n : GRP * n + GRP], axis=1) for n in range(count)]
    empty = jnp.zeros((HD, width), rows[0].dtype)
    if count == 2:
        return jnp.concatenate(
            [jnp.concatenate([sides[0], empty], axis=1), jnp.concatenate([empty, sides[1]], axis=1)],
            axis=0,
        )
    return jnp.concatenate([sides[0], empty] if low else [empty, sides[0]], axis=0)


def head_half(j, kv_heads, low):
    upper = j >= GRP if len(kv_heads) == 2 else not low
    return HD if upper else 0


def fwd_kernel(n_kv, tab, lo_ref, q_ref, *refs):
    kvs = refs[:n_kv]
    mid_ref, rl_ref, p_ref, win, bias, scores, sem = refs[n_kv:]
    slot = next_window(tab, kvs, win, sem)
    row = lax.broadcasted_iota(jnp.int32, (SPAN, BLK), 0)
    lane = lax.broadcasted_iota(jnp.int32, (SPAN, BLK), 1)
    allowed = (row >= lo_ref[0]) & (row <= lane + WIN)
    bias[...] = jnp.where(allowed, 0.0, MASK_FILL)
    q_all = (turned(q_ref[...]) * (HD ** -0.5)).astype(BF16)
    outs, recips = [], []
    at = 0
    for k_slab, v_slab, kv_heads, k_low, v_low in PAIRS:
        keys = win[slot, :, 128 * k_slab : 128 * k_slab + 128]
        vals = win[slot, :, 128 * v_slab : 128 * v_slab + 128]
        count = GRP * len(kv_heads)
        width = BLK * count
        base = BLK * at
        q_rows = [q_all[HD * (at + j) : HD * (at + j) + HD] for j in range(count)]
        scores[:, :width] = dot(keys, spread_heads(q_rows, len(kv_heads), k_low))
        for j in range(count):
            s = scores[:, BLK * j : BLK * j + BLK] + bias[...]
            top = jnp.max(s, axis=0, keepdims=True)
            p_ref[0, :, base + BLK * j : base + BLK * j + BLK] = jnp.exp(s - top).astype(BF16)
        lhs = jnp.concatenate([vals.T, jnp.ones((16, SPAN), BF16)], axis=0)
        product = dot(lhs, p_ref[0, :, base : base + width])
        recip = 1.0 / product[128:129, :]
        for j in range(count):
            cols = slice(BLK * j, BLK * j + BLK)
            half = head_half(j, kv_heads, v_low)
            outs.append(product[half : half + HD, cols] * recip[:, cols])
            recips.append(recip[:, cols])
        at += count
    mid_ref[...] = unturned(outs)
    recips.append(jnp.zeros((16 - len(recips), BLK), F32))
    rl_ref[0] = jnp.concatenate(recips, axis=0)


def fwd_call(tab, lo, q, kvs):
    blocks = q.shape[0] // BLK
    n_kv = len(kvs)
    lanes, heads = D, HQ
    return pl.pallas_call(
        lambda *refs: fwd_kernel(n_kv, *refs),
        grid=(blocks,),
        out_shape=(
            jax.ShapeDtypeStruct((q.shape[0], lanes), BF16),
            jax.ShapeDtypeStruct((blocks, 16, BLK), F32),
            jax.ShapeDtypeStruct((blocks, SPAN, heads * BLK), BF16),
        ),
        in_specs=[
            SMEM,
            pl.BlockSpec((1, 1, BLK), lambda i: (i, 0, 0)),
            pl.BlockSpec((BLK, lanes), lambda i: (i, 0)),
        ]
        + [ANY] * n_kv,
        out_specs=(
            pl.BlockSpec((BLK, lanes), lambda i: (i, 0)),
            pl.BlockSpec((1, 16, BLK), lambda i: (i, 0, 0)),
            pl.BlockSpec((1, SPAN, heads * BLK), lambda i: (i, 0, 0)),
        ),
        scratch_shapes=[
            pltpu.VMEM((2, SPAN, KV_LANES), BF16),
            pltpu.VMEM((SPAN, BLK), F32),
            pltpu.VMEM((SPAN, 2 * GRP * BLK), F32),
            pltpu.SemaphoreType.DMA((2,)),
        ],
        compiler_params=params(60, 1),
        cost_estimate=cost(32),
        name="attend",
    )(tab, lo, q, *kvs)


def bwd_kernel(
    n_kv, n_dep, first, prev, out_units, n_slots, tab, slots, q_ref, do_ref, mid_ref, rl_ref, p_ref, cos_ref, sin_ref, *refs
):
    kvs = refs[:n_kv]
    n_out = len(out_units)
    refs = refs[n_kv + n_dep :]
    earlier = refs[:n_out] if prev else ()
    refs = refs[len(earlier) :]
    dq_ref = refs[0]
    outs = refs[1 : 1 + n_out]
    win, acc, scores, stage, stage_in, sem, out_sem, in_sem = refs[1 + n_out :]
    i = pl.program_id(0)
    blk = i + first
    slot = next_window(tab, kvs, win, sem, first)
    lanes = acc.shape[1]

    @pl.when(i == 0)
    def _():
        def clear(b, _):
            acc[pl.ds(pl.multiple_of(b * BLK, BLK), BLK), :] = jnp.zeros((BLK, lanes), F32)
            return 0

        lax.fori_loop(0, n_slots, clear, 0)

    def add(slab, value):
        for j in range(NWB):
            r = pl.ds(pl.multiple_of(slots[blk, j] * BLK, BLK), BLK)
            acc[r, 128 * slab : 128 * slab + 128] += value[BLK * j : BLK * j + BLK]

    q_all = (turned(q_ref[...]) * (HD ** -0.5)).astype(BF16)
    do_all = turned(do_ref[...])
    o_all = turned(mid_ref[...])
    cos, sin = cos_ref[...], sin_ref[...]
    grads = []
    at = 0
    for k_slab, v_slab, kv_heads, k_low, v_low in PAIRS:
        keys = win[slot, :, 128 * k_slab : 128 * k_slab + 128]
        vals = win[slot, :, 128 * v_slab : 128 * v_slab + 128]
        count = GRP * len(kv_heads)
        width = BLK * count
        base = BLK * at
        q_rows, do_rows, dots = [], [], []
        for j in range(count):
            r = slice(HD * (at + j), HD * (at + j) + HD)
            q_rows.append(q_all[r])
            scaled = do_all[r] * rl_ref[0, at + j : at + j + 1, :]
            dots.append(jnp.sum(scaled * o_all[r], axis=0, keepdims=True))
            do_rows.append(scaled.astype(BF16))
        q_wide = spread_heads(q_rows, len(kv_heads), k_low)
        do_wide = spread_heads(do_rows, len(kv_heads), v_low)
        scores[:, :width] = dot(vals, do_wide)
        ds = []
        for j in range(count):
            p = p_ref[0, :, base + BLK * j : base + BLK * j + BLK].astype(F32)
            ds.append((p * (scores[:, BLK * j : BLK * j + BLK] - dots[j])).astype(BF16))
        ds = jnp.concatenate(ds, axis=1)
        probs = p_ref[0, :, base : base + width]
        if len(kv_heads) == 2:
            add(k_slab, dot_nt(ds, q_wide))
            add(v_slab, dot_nt(probs, do_wide))
        else:
            add(
                k_slab,
                dot_nt(
                    jnp.concatenate([ds, probs], axis=1),
                    jnp.concatenate([q_wide, do_wide], axis=1),
                ),
            )
        dq = dot(keys.T, ds) * (HD ** -0.5)
        for j in range(count):
            top = head_half(j, kv_heads, k_low)
            cols = slice(BLK * j, BLK * j + BLK)
            first = dq[top : top + 32, cols]
            second = dq[top + 32 : top + 64, cols]
            grads.append(first * cos + second * sin)
            grads.append(second * cos - first * sin)
        at += count
    dq_ref[...] = unturned(grads)

    @pl.when(i == pl.num_programs(0) - 1)
    def _():
        per = 6 * BLK
        places = [(n, u) for n, units in enumerate(out_units) for u in range(units)]
        copies, loads = [], []

        def load(t):
            if prev and t < len(places):
                n, u = places[t]
                c = pltpu.make_async_copy(
                    earlier[n].at[pl.ds(per * u, per)], stage_in.at[t % 2], in_sem.at[t % 2]
                )
                c.start()
                loads.append(c)

        load(0)
        load(1)
        for t, (n, u) in enumerate(places):
            s = t % 2
            if t >= 2:
                copies[t - 2].wait()
            value = acc[per * t : per * t + per, :]
            if prev:
                loads[t].wait()
                value = value + stage_in[s].astype(F32)
            stage[s] = value.astype(BF16)
            load(t + 2)
            c = pltpu.make_async_copy(stage.at[s], outs[n].at[pl.ds(per * u, per)], out_sem.at[s])
            c.start()
            copies.append(c)
        copies[-2].wait()
        copies[-1].wait()


def bwd_call(first, blocks, earlier, deps, tab, slots, out_units, q, do, mid, rl, p, cos, sin, kvs):
    n_kv = len(kvs)
    lanes, heads, width = D, HQ, KV_LANES
    n_slots = 6 * sum(out_units)
    flat = pl.BlockSpec((BLK, lanes), lambda i: (i + first, 0))
    table = pl.BlockSpec((32, BLK), lambda i: (0, i + first))
    prev = bool(earlier)
    return pl.pallas_call(
        lambda *refs: bwd_kernel(n_kv, len(deps), first, prev, out_units, n_slots, *refs),
        grid=(blocks,),
        out_shape=(jax.ShapeDtypeStruct((blocks * BLK, lanes), BF16),)
        + tuple(jax.ShapeDtypeStruct((6 * BLK * u, width), BF16) for u in out_units),
        in_specs=[
            SMEM,
            SMEM,
            flat,
            flat,
            flat,
            pl.BlockSpec((1, 16, BLK), lambda i: (i + first, 0, 0)),
            pl.BlockSpec((1, SPAN, heads * BLK), lambda i: (i + first, 0, 0)),
            table,
            table,
        ]
        + [ANY] * (n_kv + len(deps) + len(earlier)),
        out_specs=(pl.BlockSpec((BLK, lanes), lambda i: (i, 0)),) + (ANY,) * len(out_units),
        scratch_shapes=[
            pltpu.VMEM((2, SPAN, width), BF16),
            pltpu.VMEM((n_slots * BLK, width), F32),
            pltpu.VMEM((SPAN, 2 * GRP * BLK), F32),
            pltpu.VMEM((2, 6 * BLK, width), BF16),
            pltpu.VMEM((2, 6 * BLK, width), BF16),
            pltpu.SemaphoreType.DMA((2,)),
            pltpu.SemaphoreType.DMA((2,)),
            pltpu.SemaphoreType.DMA((2,)),
        ],
        compiler_params=params(60, 1),
        cost_estimate=cost(10000),
        name=f"attend_back_{first}",
    )(tab, slots, q, do, mid, rl, p, cos, sin, *kvs, *deps, *earlier)


def pro_kernel(info, mid_ref, x_ref, gain_ref, own, *refs):
    here, there = refs[0:3], refs[3:6]
    h1_ref, low_ref, w_out, _, _, w_ref, sems, out_sem = refs[9:]
    z, core = info[0], info[1]
    step = pl.program_id(0)
    out_copy = pltpu.make_async_copy(w_ref, w_out, out_sem)
    found = []

    def bring(src, row, size):
        dst = w_ref.at[pl.ds(pl.multiple_of(row, 16), size)]
        found.append((None, pltpu.make_async_copy(src, dst, sems.at[len(found)])))

    bring(own, z * ZR, ZR)
    skip = 16 * (1 - core)
    for i in range(3):
        base = rel_z(z, i) * ZR
        bring(here[i], base + (ZR - OUT_ROWS) * core, OUT_ROWS)
        bring(
            there[i].at[pl.ds(pl.multiple_of(skip, 16), OUT_ROWS - 16)],
            base + (ZR - OUT_ROWS) * (1 - core) + skip,
            OUT_ROWS - 16,
        )

    @pl.when(step == 0)
    def _():
        each(found, start)
        each(found, wait)
        out_copy.start()

    h = x_ref[...].astype(F32) + dot(mid_ref[...], w_ref[...])
    factor = lax.rsqrt(jnp.mean(h * h, axis=-1, keepdims=True) + NORM_EPS)
    h1_ref[...] = h
    low_ref[:, 0:D] = (h * factor * gain_ref[1:2, :]).astype(BF16)
    low_ref[:, D:WIDE] = jnp.zeros((ROWS, WIDE - D), BF16)

    @pl.when(step == pl.num_programs(0) - 1)
    def _():
        out_copy.wait()


def pro_call(info, mid, x, gains, own, here, there, dep, passed):
    t = x.shape[0]
    return pl.pallas_call(
        pro_kernel,
        grid=(t // ROWS,),
        out_shape=(
            jax.ShapeDtypeStruct((t, D), F32),
            jax.ShapeDtypeStruct((t, WIDE), BF16),
            jax.ShapeDtypeStruct((D, D), BF16),
            *[jax.ShapeDtypeStruct(p.shape, p.dtype) for p in passed],
        ),
        in_specs=[SMEM, by_rows(D), by_rows(D), whole((8, D))] + [ANY] * 10,
        out_specs=(by_rows(D), by_rows(WIDE), ANY, ANY, ANY),
        input_output_aliases={12: 3, 13: 4},
        scratch_shapes=[
            pltpu.VMEM((D, D), BF16),
            pltpu.SemaphoreType.DMA((7,)),
            pltpu.SemaphoreType.DMA,
        ],
        compiler_params=params(60, 1),
        cost_estimate=cost(7),
        name="out_projection",
    )(info, mid, x, gains, own, *here, *there, dep, *passed)


def ffn_kernel(info, a0, a1, c0, c1, own, *refs):
    here = refs[:4]
    acc_outs, p_ref, q_refs = refs[4:9], refs[9], refs[10:14]
    (
        wbuf, a_all, c_all, c_turn, hid_s, gg_s, gu_s, stage, acc_o, acc_g, send_o, send_lo, send_hi,
        io_sem, w_sem, out_sem, acc_sem,
    ) = refs[14:]
    z, chip, parity = info[0], info[3], info[4]
    t = a0.shape[0]
    units = wbuf.shape[1]
    ins = [
        pltpu.make_async_copy(a0, a_all.at[pl.ds(0, t)], io_sem.at[0]),
        pltpu.make_async_copy(a1, a_all.at[pl.ds(t, t)], io_sem.at[1]),
        pltpu.make_async_copy(c0, c_turn.at[0], io_sem.at[2]),
        pltpu.make_async_copy(c1, c_turn.at[1], io_sem.at[3]),
    ]
    copies = [pltpu.make_async_copy(own, wbuf.at[:, pl.ds(0, CORE_UNITS)], w_sem.at[0])]
    for n_par, par in enumerate((parity, 1 - parity)):
        for i in range(3):
            for n in range(3):
                a0_row = PACKED * i + QUARTER * n
                for ref, p0, p1 in ((here[2 * n_par], 0, CUT), (here[2 * n_par + 1], CUT, 2 * CUT)):
                    a, b = max(p0, a0_row), min(p1, a0_row + QUARTER)
                    if a < b:
                        row = CORE_UNITS * (i + 1) + QUARTER * par + (a - a0_row)
                        dst = wbuf.at[n, pl.ds(pl.multiple_of(row, 16), b - a)]
                        copies.append(
                            pltpu.make_async_copy(
                                ref.at[pl.ds(a - p0, b - a)], dst, w_sem.at[len(copies)]
                            )
                        )
    for c in ins[2:] + ins[:2] + copies:
        c.start()
    for h in range(2):
        ins[2 + h].wait()
        c_all[t * h : t * h + t, :] = c_turn[h].T
    for c in ins[:2] + copies[:1]:
        c.wait()

    def forward(c, _):
        @pl.when(c == 1)
        def _():
            for late in copies[1:]:
                late.wait()

        u = pl.ds(pl.multiple_of(c * UNITS, UNITS), UNITS)
        for h in range(2 * t // ROWS):
            r = slice(ROWS * h, ROWS * h + ROWS)
            gate = dot_nt(a_all[r, 0:D], wbuf[0, u, :])
            up = dot_nt(a_all[r, 0:D], wbuf[1, u, :])
            grad = dot_nt(c_all[r, :], wbuf[2, u, :])
            sig = lax.logistic(gate)
            swish = gate * sig
            hid_s[r, u] = (swish * up).astype(BF16)
            gg_s[r, u] = (grad * up * (sig * (1.0 + gate * (1.0 - sig)))).astype(BF16)
            gu_s[r, u] = (grad * swish).astype(BF16)
        return 0

    lax.fori_loop(0, units // UNITS, forward, 0)

    def sums(r):
        left = dot(hid_s[r, :], wbuf[2])
        right = dot(gg_s[r, :], wbuf[0]) + dot(gu_s[r, :], wbuf[1])
        return left, right

    def mine(i, _):
        r = pl.ds(pl.multiple_of(i * ROWS, ROWS), ROWS)
        acc_o[r, :], acc_g[r, :] = sums(r)
        return 0

    def others(i, _):
        r = pl.ds(pl.multiple_of(i * ROWS, ROWS), ROWS)
        left, right = sums(pl.ds(pl.multiple_of(t + i * ROWS, ROWS), ROWS))
        empty = jnp.zeros((ROWS, WIDE - D), BF16)
        send_o[r, 0:D] = left.astype(BF16)
        send_o[r, D:WIDE] = empty
        half = WIDE // 2
        send_lo[r, :] = right[:, 0:half].astype(BF16)
        send_hi[r, 0 : D - half] = right[:, half:D].astype(BF16)
        send_hi[r, D - half : half] = empty
        return 0

    lax.fori_loop(0, t // ROWS, others, 0)
    lax.fori_loop(0, t // ROWS, mine, 0)
    acc_copies = [
        pltpu.make_async_copy(src, dst, acc_sem.at[n])
        for n, (src, dst) in enumerate(zip((acc_o, acc_g, send_o, send_lo, send_hi), acc_outs))
    ]
    for c in acc_copies:
        c.start()

    def back_copies(c, slot):
        found = []
        per = CORE_UNITS // SEG
        for n in range(UNITS // SEG):
            j = c * (UNITS // SEG) + n
            within = lax.rem(j, per)
            zz = lax.rem(z + j // per, 4)
            n_p = P_ROWS // SEG
            first = within < n_p
            row = pl.multiple_of(jnp.minimum(within, n_p - 1) * SEG, SEG)
            src = stage.at[slot, :, pl.ds(SEG * n, SEG)]
            dst = p_ref.at[zz, :, pl.ds(row, SEG)]
            found.append((first, pltpu.make_async_copy(src, dst, out_sem.at[slot, 24 + n])))
            piece = 6 * n
            for k in range(per - n_p):
                at = SEG * k
                while at < SEG * k + SEG:
                    owner = at // Q_ROWS
                    size = min(SEG * k + SEG, Q_ROWS * (owner + 1)) - at
                    src = stage.at[slot, :, pl.ds(SEG * n + at - SEG * k, size)]
                    for r in range(4):
                        dst = q_refs[r].at[zz, :, pl.ds(at - Q_ROWS * owner, size)]
                        copy = pltpu.make_async_copy(src, dst, out_sem.at[slot, piece])
                        found.append(((within == n_p + k) & (chip ^ owner == r), copy))
                    at += size
                    piece += 1
        return found

    def backward(c, _):
        u = pl.ds(pl.multiple_of(c * UNITS, UNITS), UNITS)
        slot = lax.rem(c, 2)

        @pl.when(c >= 2)
        def _():
            each(back_copies(c - 2, slot), wait)

        stage[slot, 0] = dot_tn(gg_s[:, u], a_all[:, 0:D]).astype(BF16)
        stage[slot, 1] = dot_tn(gu_s[:, u], a_all[:, 0:D]).astype(BF16)
        stage[slot, 2] = dot_tn(hid_s[:, u], c_all[...]).astype(BF16)
        each(back_copies(c, slot), start)
        return 0

    n_chunks = units // UNITS
    lax.fori_loop(0, n_chunks, backward, 0)
    for c in (n_chunks - 2, n_chunks - 1):
        each(back_copies(jnp.int32(c), c % 2), wait)
    for c in acc_copies:
        c.wait()


def ffn_call(info, a0, a1, c0, c1, own, here):
    t = a0.shape[0]
    units = 4 * CORE_UNITS
    return pl.pallas_call(
        ffn_kernel,
        out_shape=(
            jax.ShapeDtypeStruct((t, D), F32),
            jax.ShapeDtypeStruct((t, D), F32),
            jax.ShapeDtypeStruct((t, WIDE), BF16),
            jax.ShapeDtypeStruct((t, WIDE // 2), BF16),
            jax.ShapeDtypeStruct((t, WIDE // 2), BF16),
            jax.ShapeDtypeStruct((4, 3, P_ROWS, D), BF16),
            *[jax.ShapeDtypeStruct((4, 3, Q_ROWS, D), BF16)] * 4,
        ),
        in_specs=[SMEM] + [ANY] * 9,
        out_specs=(ANY,) * 10,
        scratch_shapes=[
            pltpu.VMEM((3, units, D), BF16),
            pltpu.VMEM((2 * t, WIDE), BF16),
            pltpu.VMEM((2 * t, D), BF16),
            pltpu.VMEM((2, D, t), BF16),
            pltpu.VMEM((2 * t, units), BF16),
            pltpu.VMEM((2 * t, units), BF16),
            pltpu.VMEM((2 * t, units), BF16),
            pltpu.VMEM((2, 3, UNITS, D), BF16),
            pltpu.VMEM((t, D), F32),
            pltpu.VMEM((t, D), F32),
            pltpu.VMEM((t, WIDE), BF16),
            pltpu.VMEM((t, WIDE // 2), BF16),
            pltpu.VMEM((t, WIDE // 2), BF16),
            pltpu.SemaphoreType.DMA((4,)),
            pltpu.SemaphoreType.DMA((24,)),
            pltpu.SemaphoreType.DMA((2, 28)),
            pltpu.SemaphoreType.DMA((5,)),
        ],
        compiler_params=params(60),
        cost_estimate=cost(50),
        name="feed_forward",
    )(info, a0, a1, c0, c1, own, *here)


def put_shards(ref, product, gain_grad):
    extra = ref.shape[-1] - product.shape[1]
    if extra:
        product = jnp.concatenate([product, jnp.zeros((product.shape[0], extra), F32)], axis=1)
    width = product.shape[1]
    first_row = lax.broadcasted_iota(jnp.int32, (ZP - ZR, width), 0) == 0
    for n in range(4):
        ref[n, 0:ZR, :] = product[ZR * n : ZR * n + ZR].astype(BF16)
        if gain_grad is None:
            ref[n, ZR:ZP, :] = jnp.zeros((ZP - ZR, width), BF16)
        else:
            part = jnp.concatenate(
                [gain_grad[:, ZR * n : ZR * n + ZR], jnp.zeros((1, width - ZR), F32)], axis=1
            )
            ref[n, ZR:ZP, :] = jnp.where(first_row, part, 0.0).astype(BF16)


def put_halves(core, keep_ref, send_ref, product, gain_grad):
    extra = jnp.zeros((product.shape[0], WIDE - product.shape[1]), F32)
    wide = jnp.concatenate([product, extra], axis=1)
    half = WIDE // 2
    for side, (first, second) in enumerate(((keep_ref, send_ref), (send_ref, keep_ref))):
        @pl.when(core == side)
        def _():
            put_shards(first, wide[:, :half], gain_grad)
            put_shards(second, wide[:, half:], None)


def epi_kernel(
    info, h1_ref, acc_g, got_lo, got_hi, ct_ref, gain_ref, w_ref, mid_ref, *refs
):
    gh_ref, gm_ref, keep_ref, send_ref, acc, total = refs
    i = pl.program_id(0)

    @pl.when(i == 0)
    def _():
        acc[...] = jnp.zeros((D, D), F32)
        total[...] = jnp.zeros((8, D), F32)

    h = h1_ref[...]
    factor = lax.rsqrt(jnp.mean(h * h, axis=-1, keepdims=True) + NORM_EPS)
    normed = h * factor
    got = jnp.concatenate([got_lo[...], got_hi[...]], axis=1)
    g = acc_g[...] + got[:, 0:D].astype(F32)
    scaled = g * gain_ref[1:2, :]
    back = factor * (scaled - normed * jnp.mean(scaled * normed, axis=-1, keepdims=True))
    full = ct_ref[...].T.astype(F32) + back
    gh_ref[...] = full
    res = full.astype(BF16)
    gm_ref[...] = dot_nt(res, w_ref[...]).astype(BF16)
    total[0:1, :] += jnp.sum(g * normed, axis=0, keepdims=True)
    acc[...] += dot_tn(mid_ref[...], res)

    @pl.when(i == pl.num_programs(0) - 1)
    def _():
        put_halves(info[1], keep_ref, send_ref, acc[...], total[0:1, :])


def epi_call(info, h1, acc_g, got_lo, got_hi, cot_t, gains, w_out, mid):
    t = h1.shape[0]
    rows = pl.BlockSpec((ROWS, D), lambda i: (i, 0))
    return pl.pallas_call(
        epi_kernel,
        grid=(t // ROWS,),
        out_shape=(
            jax.ShapeDtypeStruct((t, D), F32),
            jax.ShapeDtypeStruct((t, D), BF16),
            jax.ShapeDtypeStruct((4, ZP, WIDE // 2), BF16),
            jax.ShapeDtypeStruct((4, ZP, WIDE // 2), BF16),
        ),
        in_specs=[
            SMEM,
            rows,
            rows,
            by_rows(WIDE // 2),
            by_rows(WIDE // 2),
            by_lanes(D),
            whole((8, D)),
            whole((D, D)),
            rows,
        ],
        out_specs=(rows, rows) + (whole((4, ZP, WIDE // 2)),) * 2,
        scratch_shapes=[pltpu.VMEM((D, D), F32), pltpu.VMEM((8, D), F32)],
        compiler_params=params(60, 1),
        cost_estimate=cost(12),
        name="feed_forward_norm_back",
    )(info, h1, acc_g, got_lo, got_hi, cot_t, gains, w_out, mid)


def post_q_kernel(info, a_ref, g_ref, w_ref, _, keep_ref, send_ref, part_ref, acc):
    step = pl.program_id(0)

    @pl.when(step == 0)
    def _():
        acc[...] = jnp.zeros((D, D), F32)

    g = g_ref[...]
    part_ref[...] = dot_nt(g, w_ref[:, 0:D])
    acc[...] += dot_tn(a_ref[...], g)

    @pl.when(step == pl.num_programs(0) - 1)
    def _():
        put_halves(info[1], keep_ref, send_ref, acc[...], None)


def post_q_call(info, a, g, w, dep):
    t = a.shape[0]
    piece = (4, ZP, WIDE // 2)
    return pl.pallas_call(
        post_q_kernel,
        grid=(t // ROWS,),
        out_shape=(
            jax.ShapeDtypeStruct(piece, BF16),
            jax.ShapeDtypeStruct(piece, BF16),
            jax.ShapeDtypeStruct((t, D), F32),
        ),
        in_specs=[SMEM, by_rows(D), by_rows(D), whole(w.shape), ANY],
        out_specs=(whole(piece), whole(piece), by_rows(D)),
        scratch_shapes=[pltpu.VMEM((D, D), F32)],
        compiler_params=params(60, 1),
        cost_estimate=cost(8),
        name="query_back",
    )(info, a, g, w, dep)


def turn_back(slab, cos, sin, first_half, low_head):
    mixed = slab(2)
    k4 = jnp.where(low_head, 0.0, rope_slab(mixed, cos, sin, first_half))
    k01 = rope_slab(slab(0), cos, sin, first_half)
    k23 = rope_slab(slab(1), cos, sin, first_half)
    v4 = jnp.where(low_head, mixed, 0.0)
    return jnp.concatenate([k4, k01, k23, slab(3), slab(4), v4], axis=1).astype(BF16)


def kv_weights_back(info, cos, sin, turned, totals, dep):
    t = turned[0].shape[1]
    half = t // 2
    piece = ((4, ZP, 384), BF16)
    n_all = len(totals)

    def body(info, ins, outs, scratch):
        cos_ref, sin_ref = ins[0], ins[1]
        a_refs, g_refs = ins[2 : 2 + len(turned)], ins[2 + len(turned) :]
        first_half, low_head = lane_masks(ROWS)
        low, acc = scratch
        for c in range(n_all if n_all < 4 else 4):
            for i in range(t // ROWS):
                at = ROWS * i

                def slab(j):
                    lanes = slice(128 * j, 128 * j + 128)
                    if c < 3:
                        return g_refs[c][at : at + ROWS, lanes].astype(F32)
                    if at + ROWS <= half:
                        return g_refs[3][at : at + ROWS, lanes].astype(F32)
                    if at >= half:
                        return g_refs[4][at - half : at - half + ROWS, lanes].astype(F32)
                    parts = [g_refs[3][at:half, lanes], g_refs[4][0 : at + ROWS - half, lanes]]
                    return jnp.concatenate([p.astype(F32) for p in parts], axis=0)

                r = slice(t * c + at, t * c + at + ROWS)
                cos, sin = wide_tables(cos_ref[:, r], -sin_ref[:, r])
                low[at : at + ROWS, :] = turn_back(slab, cos, sin, first_half, low_head)
            for n, rows in enumerate((slice(0, D // 2), slice(D // 2, D))):
                value = dot(a_refs[2 * c + n][...], low[...])
                if c == 0:
                    acc[rows, :] = value
                else:
                    acc[rows, :] += value
        for core, (k_out, v_out) in enumerate(((outs[0], outs[1]), (outs[1], outs[0]))):
            @pl.when(info[1] == core)
            def _():
                put_shards(k_out, acc[:, 0:384], None)
                put_shards(v_out, acc[:, 384:768], None)

    return step_call(
        "key_value_weights_back",
        body,
        info,
        (cos, sin, *turned, *totals),
        (piece, piece),
        scratch=(pltpu.VMEM((t, 768), BF16), pltpu.VMEM((D, 768), F32)),
        behind=(dep,),
    )


def post_kv_kernel(
    info, s0, s1, s2, cos_ref, sin_ref, part_ref, w_ref, x_ref, gh_ref, gain_ref, ig_ref,
):
    first_half, low_head = lane_masks(ROWS)

    def slab(j):
        c = slice(128 * j, 128 * j + 128)
        return s0[:, c].astype(F32) + s1[:, c].astype(F32) + s2[:, c].astype(F32)

    cos, sin = wide_tables(cos_ref[...], -sin_ref[...])
    low = turn_back(slab, cos, sin, first_half, low_head)
    g = (
        part_ref[...]
        + dot_nt(low[:, 0:384], w_ref[:, 0:384])
        + dot_nt(low[:, 384:704], w_ref[:, 384:704])
    )
    x = x_ref[...].astype(F32)
    factor = lax.rsqrt(jnp.mean(x * x, axis=-1, keepdims=True) + NORM_EPS)
    normed = x * factor
    scaled = g * gain_ref[0:1, :]
    back = factor * (scaled - normed * jnp.mean(scaled * normed, axis=-1, keepdims=True))
    ig_ref[...] = (gh_ref[...] + back).astype(BF16).T


def post_kv_call(info, sums, cos, sin, part, w, x, gh, gain, dep):
    t = x.shape[0]
    return pl.pallas_call(
        lambda *refs: post_kv_kernel(*refs[:11], refs[12]),
        grid=(t // ROWS,),
        out_shape=jax.ShapeDtypeStruct((D, t), BF16),
        in_specs=[SMEM]
        + [by_rows(KV_LANES)] * 3
        + [by_lanes(32)] * 2
        + [by_rows(D), whole(w.shape)]
        + [by_rows(D)] * 2
        + [whole((8, D)), ANY],
        out_specs=by_lanes(D),
        compiler_params=params(60, 1),
        cost_estimate=cost(8),
        name="key_value_back",
    )(info, *sums, cos, sin, part, w, x, gh, gain, dep)


def finish_ffn(info, mine, other, dep):
    out = ((D, 2 * CORE_UNITS), F32)

    def body(info, ins, outs, scratch):
        rows = scratch[0]
        for n in range(3):
            for ref, side in ((ins[0], info[1]), (ins[1], 1 - info[1])):
                at = pl.multiple_of(side * CORE_UNITS, 16)
                rows[pl.ds(at, CORE_UNITS), :] = ref[n].astype(F32)
            outs[n][...] = rows[...].T

    return step_call(
        "finish_feed_forward",
        body,
        info,
        (mine, other),
        (out,) * 3,
        scratch=(pltpu.VMEM((2 * CORE_UNITS, D), F32),),
        behind=(dep,),
    )


def finish_rest(info, mine, other, w_own):
    half = WIDE // 2

    def body(info, ins, outs, scratch):
        wq_ref, wo_ref, wk_ref, wv_ref, one_ref, two_ref = outs

        def emit(first, second):
            def both(at):
                lanes = slice(at, at + half)
                return jnp.concatenate([first[0:ZR, lanes], second[0:ZR, lanes]], axis=1)

            wo_ref[...] = both(0).astype(F32)[:, 0:D]
            query = both(half).astype(F32)[:, 0:D]
            wq_ref[...] = query
            k = first[:, WIDE : WIDE + 384].astype(F32)
            v = second[:, WIDE : WIDE + 384].astype(F32)
            k_t = k.T
            wk_ref[...] = jnp.concatenate([k_t[128:384], k_t[64:128]], axis=0)[:, 0:ZR]
            wv_ref[...] = v.T[0:320, 0:ZR]
            w = ins[2][...].astype(F32)
            total = jnp.sum(query * w[:, 0:D], axis=1, keepdims=True)
            total += jnp.sum(k[0:ZR, 128:384] * w[:, 1024:1280], axis=1, keepdims=True)
            total += jnp.sum(k[0:ZR, 64:128] * w[:, 960:1024], axis=1, keepdims=True)
            total += jnp.sum(v[0:ZR, 0:320] * w[:, 1280:1600], axis=1, keepdims=True)
            total = total / w[:, 1600:1601]
            one_ref[...] = jnp.broadcast_to(total, (ZR, 128)).T[0:1, :]
            two_ref[...] = first[ZR:ZP, :].astype(F32)[0:1, 0:ZR]

        for core, refs in enumerate(((ins[0], ins[1]), (ins[1], ins[0]))):
            @pl.when(info[1] == core)
            def _():
                emit(*refs)

    outs = (((ZR, D), F32), ((ZR, D), F32), ((320, ZR), F32), ((320, ZR), F32), ((1, ZR), F32), ((1, ZR), F32))
    return step_call("finish_rest", body, info, (mine, other, w_own), outs)


def sum_chips(info, terms, over_z, passed, behind):
    n_terms = len(terms)
    cut = P_ROWS // 2

    def body(info, ins, outs, scratch):
        for zz in range(4):
            outs[0][zz] = sum(ins[k][zz].astype(F32) for k in range(n_terms)).astype(BF16)
        for n in range(2):
            outs[1 + n][...] = ins[n_terms][0, :, cut * n : cut * n + cut, :]

    outs = ((terms[0].shape, BF16),) + (((3, cut, D), BF16),) * 2
    return step_call(
        "sum_chips", body, info, (*terms, over_z), outs, behind=behind, passed=passed
    )


def join_cores(info, keep, recv, pairs):
    rows = keep.shape[0] // 4
    cut = rows // 2

    def body(info, ins, outs, scratch):
        for n in range(3):
            r = slice(rows * n, rows * n + rows)
            outs[n][...] = ins[0][r, :] + ins[1][r, :]
        for n in range(2):
            r = slice(3 * rows + cut * n, 3 * rows + cut * n + cut)
            outs[3 + n][...] = ins[0][r, :] + ins[1][r, :]
        for n in range(len(pairs)):
            outs[5 + n][...] = ins[2 + 2 * n][...] + ins[3 + 2 * n][...]

    outs = (((rows, KV_LANES), BF16),) * 3 + (((cut, KV_LANES), BF16),) * 2
    outs += tuple((a.shape, BF16) for a, _ in pairs)
    flat = [a for pair in pairs for a in pair]
    return step_call("join_cores", body, info, (keep, recv, *flat), outs)


def join_near(info, to_x, to_y, from_x, from_y, pairs, passed):
    cut = from_x.shape[0]

    def body(info, ins, outs, scratch):
        to_x, to_y, from_x, from_y = ins[:4]
        outs[0][0:cut, :] = to_x[0:cut, :]
        outs[0][cut : 2 * cut, :] = to_x[cut : 2 * cut, :] + from_y[...]
        outs[1][0:cut, :] = to_y[0:cut, :] + from_x[...]
        outs[1][cut : 2 * cut, :] = to_y[cut : 2 * cut, :]
        for n in range(2):
            outs[2 + n][...] = ins[4 + 2 * n][...] + ins[5 + 2 * n][...]

    flat = [a for pair in pairs for a in pair]
    outs = ((to_x.shape, BF16),) * 2 + tuple((a.shape, BF16) for a, _ in pairs)
    return step_call(
        "join_near", body, info, (to_x, to_y, from_x, from_y, *flat), outs, passed=passed
    )


def join_projections(info, q_pair, kv_pair, h1, acc_o, got_o, dep):
    t = h1.shape[0]
    half = WIDE // 2

    def body(info, ins, outs, scratch):
        outs[0][:, :, 0:half] = ins[0][...] + ins[1][...]
        outs[0][:, :, half : half + 384] = ins[2][...] + ins[3][...]
        for i in range(t // ROWS):
            r = slice(ROWS * i, ROWS * i + ROWS)
            value = ins[4][r, :] + ins[5][r, :] + ins[6][r, 0:D].astype(F32)
            outs[1][:, r] = value.astype(BF16).T

    return step_call(
        "join_projections",
        body,
        info,
        (*q_pair, *kv_pair, h1, acc_o, got_o),
        (((4, ZP, half + 384), BF16), ((D, t), BF16)),
        behind=(dep,),
    )


def halve_rows(info, left, right, behind):
    rows = left.shape[1] // 2
    lanes = left.shape[2], right.shape[2]

    def body(info, ins, outs, scratch):
        for n in range(2):
            r = slice(rows * n, rows * n + rows)
            outs[n][:, 0 : lanes[0]] = ins[0][0, r, :]
            outs[n][:, lanes[0] : sum(lanes)] = ins[1][0, r, :]

    outs = (((rows, sum(lanes)), BF16),) * 2
    return step_call("halve_rows", body, info, (left, right), outs, behind=behind)


def add_pairs(info, pairs, passed=()):
    def body(info, ins, outs, scratch):
        for n in range(len(pairs)):
            outs[n][...] = ins[2 * n][...] + ins[2 * n + 1][...]

    flat = [a for pair in pairs for a in pair]
    outs = tuple((a.shape, BF16) for a, _ in pairs)
    return step_call("add_pairs", body, info, flat, outs, passed=passed)


def stack_two(info, first, second, behind):
    def body(info, ins, outs, scratch):
        for n in range(2):
            outs[0][n] = ins[n][...]

    out = ((2,) + first.shape, BF16)
    return step_call("stack_two", body, info, (first, second), (out,), behind=behind)[0]


def stack_pairs(info, pairs, dep):
    rows = pairs[0][0].shape[0]

    def body(info, ins, outs, scratch):
        for n in range(2):
            outs[0][rows * n : rows * n + rows, :] = ins[2 * n][...] + ins[2 * n + 1][...]

    flat = [a for pair in pairs for a in pair]
    shape = (2 * rows,) + pairs[0][0].shape[1:]
    return step_call("stack_pairs", body, info, flat, ((shape, BF16),), behind=(dep,))[0]


def join_ffn(info, pairs, near, far, dep):
    cut = P_ROWS // 2

    def body(info, ins, outs, scratch):
        chip = info[3]
        out = outs[0]
        for n in range(2):
            out[:, cut * n : cut * n + cut, :] = ins[2 * n][...] + ins[2 * n + 1][...]
        for r in range(4):
            at = pl.multiple_of(P_ROWS + Q_ROWS * (chip ^ r), 16)
            out[:, pl.ds(at, Q_ROWS), :] = ins[4 + r // 2][r % 2]

    flat = [a for pair in pairs for a in pair]
    return step_call(
        "join_feed_forward",
        body,
        info,
        (*flat, near, far),
        (((3, CORE_UNITS, D), BF16),),
        behind=(dep,),
    )[0]


def rows_after(x, start, size, tok, axis=0):
    return lax.dynamic_slice_in_dim(x, start + tok, size, axis=axis)


def z_shift(x, step):
    n = 4
    return lax.ppermute(x, "fsdp", [(i, (i + step) % n) for i in range(n)])


def c_swap(x, bit):
    n = lax.axis_size("ctx")
    return lax.ppermute(x, "ctx", [(i, i ^ bit) for i in range(n)])


def bits_from(b):
    bits = []
    while b < lax.axis_size("ctx"):
        bits.append(b)
        b *= 2
    return bits


def chip_near(kv):
    if lax.axis_size("ctx") != 8:
        return ()
    return c_swap(kv, 2), c_swap(kv, 4)


def chip_far(kv, near):
    if not near:
        return [lax.all_gather(kv, "ctx", axis=0, tiled=True)]
    cut = kv.shape[0] // 2
    across_x, across_y = near
    far_lo = c_swap(across_x[:cut], 4)
    far_hi = c_swap(across_y[cut:], 2)
    chip = [kv, across_x, across_y, far_lo, far_hi]
    return chip + [c_swap(part, 1) for part in chip]


def kv_entry(position, per_dev, me, n):
    if n != 8:
        return position
    owner, within = position // per_dev, position % per_dev
    rel = owner ^ me
    cut = per_dev // 2
    far = (rel // 2) == 3
    late = far & (within >= cut)
    which = (rel % 2) * 5 + rel // 2 + late.astype(jnp.int32)
    return which * 1024 + jnp.where(late, within - cut, within)


def kv_slot(position, per_dev, me):
    owner, within = position // per_dev, position % per_dev
    rel = owner ^ me
    return ((rel % 2) * 4 + rel // 2) * per_dev + within


def on_device(
    tokens,
    cotangent,
    doc_lengths,
    deal,
    attn_gain,
    w_query,
    w_key,
    w_value,
    w_out,
    mlp_gain,
    w_gate,
    w_up,
    w_down,
):
    me = lax.axis_index("ctx")
    n_ctx = lax.axis_size("ctx")
    z = lax.axis_index("fsdp")
    core = me % 2
    near_me = me % 8
    chip = near_me // 2
    parity = (chip + chip // 2) % 2
    info = jnp.stack([z, core, near_me, chip, parity]).astype(jnp.int32)
    tok_rows = tokens.shape[1]
    per_dev = tok_rows // BLK
    deal_row = deal[0]
    blocks = deal_row.shape[0]
    group_size = blocks * BLK
    doc_lens = doc_lengths[0]
    seq_count = doc_lens.shape[0]
    length = group_size // seq_count
    x_turned = tokens[0].T
    cot_turned = cotangent[0].T

    block_ids = jnp.arange(blocks, dtype=jnp.int32)
    mine = lax.dynamic_slice_in_dim(deal_row, me * per_dev, per_dev)
    seq_blocks = jnp.maximum(
        mine[:, None] - (NWB - 1) + jnp.arange(NWB, dtype=jnp.int32)[None, :], 0
    )
    position = jnp.sum(
        jnp.where(seq_blocks[:, :, None] == deal_row[None, None, :], block_ids, 0), axis=-1
    )
    tab = kv_entry(position, per_dev, me, n_ctx).astype(jnp.int32)
    doc_ends = (
        jnp.cumsum(doc_lens, axis=1) + (jnp.arange(seq_count, dtype=jnp.int32) * length)[:, None]
    ).reshape(-1)
    doc_starts = doc_ends - doc_lens.reshape(-1)
    q_time = mine[:, None] * BLK + jnp.arange(BLK, dtype=jnp.int32)[None, :]
    begin = jnp.max(jnp.where(q_time[..., None] >= doc_starts, doc_starts, 0), axis=-1)
    lo = jnp.maximum(begin, q_time - (WIN - 1)) - (mine[:, None] * BLK - WIN)
    lo = lo[:, None, :].astype(jnp.int32)
    n_chips = 4 if n_ctx == 8 else 1
    owners = jnp.stack([me ^ (2 * r) for r in range(n_chips)])
    theirs = jnp.sum(
        jnp.where(
            block_ids == (owners[:, None] * per_dev + jnp.arange(per_dev, dtype=jnp.int32))[..., None],
            deal_row,
            0,
        ),
        axis=-1,
    )
    their_time = theirs[:, :, None] * BLK + jnp.arange(BLK, dtype=jnp.int32)
    their_begin = jnp.max(jnp.where(their_time[..., None] >= doc_starts, doc_starts, 0), axis=-1)
    pos = (their_time - their_begin).reshape(-1)
    half_dim = HD // 2
    freqs = ROPE_THETA ** (-jnp.arange(half_dim, dtype=F32) * (2.0 / HD))
    angle = freqs[:, None] * pos.astype(F32)[None, :]
    cos_turn, sin_turn = jnp.cos(angle), jnp.sin(angle)

    gains_wide = jnp.concatenate(
        [attn_gain[:, None], mlp_gain[:, None], jnp.zeros((ZR, QKV - 1602), BF16)], axis=1
    )
    w_parts = [w_query, w_key[:, 256:], w_key[:, :256], w_value, gains_wide]
    start = jnp.minimum(32 * near_me, ZR - 32)
    w_mine = jnp.concatenate(
        [lax.dynamic_slice_in_dim(w, start, 32, axis=0) for w in w_parts], axis=1
    )
    w_z = [z_shift(w_mine, -1), z_shift(w_mine, 2), z_shift(w_mine, 1)]
    own_half, packed, out_mine = prep_weights(info, w_gate, w_up, w_down.T, w_out)
    w_got, packed = stack_weights(info, w_z, (cos_turn, sin_turn), (packed,))
    over_z = lax.all_gather(packed, "fsdp", axis=0, tiled=False)
    cot_there = c_swap(cot_turned, 1)
    w_chips = [w_got, c_swap(w_got, 2), c_swap(w_got, 4), c_swap(w_got, 6)]
    w_pieces = [jnp.concatenate(w_parts, axis=1)]
    for piece in w_chips:
        w_pieces += [piece, c_swap(piece, 1)]

    attn_in, attn_up, attn_lo, q_low, kv_low, x, gains, w_q, w_kv = pre_call(
        info, x_turned, cos_turn, sin_turn, w_pieces
    )
    kvs = chip_far(kv_low, chip_near(kv_low))

    first, second = split_quarters(info, over_z, (*kvs, cot_there))
    first_on, second_on = c_swap(first, 2), c_swap(second, 4)
    out_mine = meet(info, (out_mine,), (first,))[0]
    out_here = [z_shift(out_mine, -1), z_shift(out_mine, 2), z_shift(out_mine, 1)]
    mid_low, recips, probs = fwd_call(tab, lo, q_low, kvs)
    *out_here, first_on, second_on = meet(info, (*out_here, first_on, second_on), (mid_low,))
    out_there = [c_swap(p, 1) for p in out_here]
    here = (first, second, first_on, second_on)
    h1, mlp_in, w_out_all, attn_up, attn_lo = pro_call(
        info, mid_low, x, gains, w_out, out_here, out_there, cot_there, (attn_up, attn_lo)
    )
    acc_o, acc_g, send_o, send_lo, send_hi, p_both, *q_both = ffn_call(
        info, mlp_in, c_swap(mlp_in, 1), cot_turned, cot_there, own_half, here
    )
    p_sum = lax.psum_scatter(p_both, "fsdp", scatter_dimension=0, tiled=True)
    q_got = [c_swap(q_both[r], 2 * r) for r in range(1, 4)]
    got_o = c_swap(send_o, 1)
    attn_turned = [attn_up, attn_lo]
    a_x = [c_swap(a, 2) for a in attn_turned]
    a_y = [c_swap(a, 4) for a in attn_turned]
    send_lo, send_hi, *a_near = meet(info, (send_lo, send_hi, *a_x, *a_y))
    got_lo, got_hi = c_swap(send_lo, 1), c_swap(send_hi, 1)
    grad_hidden, grad_mid, go_keep, go_send = epi_call(
        info, h1, acc_g, got_lo, got_hi, cot_turned, gains, w_out_all, mid_low
    )
    a_turned = [*attn_turned, *a_near, c_swap(a_near[0], 4), c_swap(a_near[3], 2)]

    if n_ctx == 8:
        out_units = (4, 4)
        slots = kv_slot(position, per_dev, me).astype(jnp.int32)
    else:
        out_units = (NWB,)
        n_slots = per_dev * NWB
        flat_pos = position.reshape(-1)
        order = jnp.arange(n_slots, dtype=jnp.int32)
        slots = jnp.min(
            jnp.where(flat_pos[:, None] == flat_pos[None, :], order[None, :], n_slots), axis=1
        ).reshape(per_dev, NWB)
        source = jnp.min(
            jnp.where(block_ids[:, None] == flat_pos[None, :], order[None, :], n_slots), axis=1
        )

    def own_rows(parts):
        width = parts[0].shape[1]
        padded = jnp.concatenate(
            [parts[0].reshape(n_slots, BLK, width), jnp.zeros((1, BLK, width), BF16)], axis=0
        )
        spread = jnp.take(padded, source, axis=0).reshape(group_size, width)
        own = lax.psum_scatter(spread, "ctx", scatter_dimension=0, tiled=True)
        return own, (own, jnp.zeros_like(own), jnp.zeros_like(own))

    back_args = (
        tab, slots, out_units, q_low, grad_mid, mid_low, recips, probs, cos_turn, sin_turn, kvs
    )
    dq, *kv_parts = bwd_call(0, per_dev, (), (), *back_args)
    q_terms = (q_both[0], *q_got)
    go_pair = (go_keep, c_swap(go_send, 1))
    if n_ctx == 8:
        kv_keep, kv_send = kv_parts
        q_sum, p_l, p_r, kv_send, a_lo, a_hi = sum_chips(
            info, q_terms, p_sum, (kv_send, *a_turned[6:]), (dq,)
        )
        a_turned[6:] = [a_lo, a_hi]
        own, to_x, to_y, far_lo, far_hi, go_both = join_cores(
            info, kv_keep, c_swap(kv_send, 1), (go_pair,)
        )
        totals = (own, to_x, to_y, far_lo, far_hi)
    else:
        q_sum, p_l, p_r = sum_chips(info, q_terms, p_sum, (), (dq,))
        own, sums = own_rows(kv_parts)
        a_turned, totals = a_turned[:2], (own,)
        go_both = add_pairs(info, (go_pair,))[0]
    q_mine = lax.psum_scatter(q_sum, "fsdp", scatter_dimension=0, tiled=True)[0]
    for b in bits_from(8):
        q_mine = q_mine + c_swap(q_mine, b)
    gq_keep, gq_send, part = post_q_call(info, attn_in, dq, w_q, own)
    go_sum = lax.psum_scatter(go_both, "fsdp", scatter_dimension=0, tiled=True)
    gkv_keep, gkv_send = kv_weights_back(info, cos_turn, sin_turn, a_turned, totals, gq_keep)
    p_pairs = ((p_l, c_swap(p_l, 2)), (p_r, c_swap(p_r, 4)))
    if n_ctx == 8:
        to_x, to_y, p_l, p_r, gq_send, gkv_send, q_mine = join_near(
            info,
            to_x,
            to_y,
            c_swap(far_lo, 2),
            c_swap(far_hi, 4),
            p_pairs,
            (gq_send, gkv_send, q_mine),
        )
        sums = (own, c_swap(to_x, 2), c_swap(to_y, 4))
    else:
        p_l, p_r = (a + b for a, b in p_pairs)
    p_pairs = ((p_l, c_swap(p_l, 4)), (p_r, c_swap(p_r, 2)))
    g_both, output = join_projections(
        info, (gq_keep, c_swap(gq_send, 1)), (gkv_keep, c_swap(gkv_send, 1)), h1, acc_o, got_o, p_l
    )
    g_sum = lax.psum_scatter(g_both, "fsdp", scatter_dimension=0, tiled=True)
    q_near = stack_two(info, q_mine, c_swap(q_mine, 2), (output,))
    q_far = c_swap(q_near, 4)
    input_grad = post_kv_call(
        info, sums, cos_turn, sin_turn, part, w_kv, x, grad_hidden, gains, q_near
    )
    for b in bits_from(8):
        p_pairs = tuple((a + c_swap(a, b), g + c_swap(g, b)) for a, g in p_pairs)
    g_l, g_r = halve_rows(info, go_sum, g_sum, (input_grad,))
    ffn_sum = join_ffn(info, p_pairs, q_near, q_far, g_l)
    g_l, g_r, ffn_sum = add_pairs(
        info, ((g_l, c_swap(g_l, 2)), (g_r, c_swap(g_r, 4))), (ffn_sum,)
    )
    gate_grad, up_grad, down_grad = finish_ffn(info, ffn_sum, c_swap(ffn_sum, 1), g_l)
    g_sum = stack_pairs(info, ((g_l, c_swap(g_l, 4)), (g_r, c_swap(g_r, 2))), gate_grad)
    for b in bits_from(8):
        g_sum = g_sum + c_swap(g_sum, b)
    query_grad, out_grad, key_grad, value_grad, gain_one, gain_two = finish_rest(
        info, g_sum, c_swap(g_sum, 1), w_pieces[0]
    )

    return (
        output.T[None],
        input_grad.T[None],
        gain_one.reshape(ZR),
        query_grad,
        key_grad.T,
        value_grad.T,
        out_grad,
        gain_two.reshape(ZR),
        gate_grad,
        up_grad,
        down_grad.T,
    )


def solution(mesh):
    in_specs = (
        P("fsdp", "ctx", None),
        P("fsdp", "ctx", None),
        P("fsdp", None, None),
        P("fsdp", None),
        P("fsdp"),
        P("fsdp", None),
        P("fsdp", None),
        P("fsdp", None),
        P("fsdp", None),
        P("fsdp"),
        P(None, "fsdp"),
        P(None, "fsdp"),
        P("fsdp", None),
    )
    out_specs = (
        P("fsdp", "ctx", None),
        P("fsdp", "ctx", None),
        P("fsdp"),
        P("fsdp", None),
        P("fsdp", None),
        P("fsdp", None),
        P("fsdp", None),
        P("fsdp"),
        P(None, "fsdp"),
        P(None, "fsdp"),
        P("fsdp", None),
    )
    return jax.shard_map(
        on_device, mesh=mesh, in_specs=in_specs, out_specs=out_specs, check_vma=False
    )
```

```python
import jax
import jax.numpy as jnp
from jax import lax
from jax.experimental import pallas as pl
from jax.experimental.pallas import tpu as pltpu
from jax.sharding import PartitionSpec as P

HQ = 15
KVH = 5
HD = 64
BLK = 128
WIN = 1024
D = 960
GRP = HQ // KVH
SPAN = WIN + BLK
NWB = SPAN // BLK
ROWS = 256
ZR = 240
ZP = 256
UNITS = 256
WIDE = 1024
QKV = 1664

NORM_EPS = 1e-05
ROPE_THETA = 100000.0
MASK_FILL = -1e30
F32 = jnp.float32
BF16 = jnp.bfloat16
MIB = 1024 * 1024

VMEM = pl.BlockSpec(memory_space=pltpu.VMEM)
SMEM = pl.BlockSpec(memory_space=pltpu.SMEM)
ANY = pl.BlockSpec(memory_space=pl.ANY)

KV_LANES = 640
PAIRS = (
    (0, 3, (0, 1), True, True),
    (1, 4, (2, 3), True, True),
    (2, 2, (4,), False, True),
)

CORE_UNITS = 320
QUARTER = 160
OUT_ROWS = 128
PACKED = 3 * QUARTER
CUT = 3 * PACKED // 2

P_ROWS = 128
Q_ROWS = 48
SEG = 64


def dot(a, b):
    return jnp.dot(a, b, preferred_element_type=F32)


def dot_nt(a, b):
    return lax.dot_general(a, b, (((1,), (1,)), ((), ())), preferred_element_type=F32)


def dot_tn(a, b):
    return lax.dot_general(a, b, (((0,), (0,)), ((), ())), preferred_element_type=F32)


def params(mib, grid_dims=0):
    return pltpu.CompilerParams(
        vmem_limit_bytes=mib * MIB,
        dimension_semantics=("arbitrary",) * grid_dims if grid_dims else None,
    )


def cost(micros):
    return pl.CostEstimate(flops=int(3.5e8 * micros), bytes_accessed=1, transcendentals=0)


def rope_slab(t, cos, sin_signed, first_half):
    swapped = jnp.where(first_half, pltpu.roll(t, 96, 1), pltpu.roll(t, 32, 1))
    return t * cos + swapped * sin_signed


def wide_tables(cos, sin):
    return (
        jnp.concatenate([cos] * 4, axis=0).T,
        jnp.concatenate([-sin, sin, -sin, sin], axis=0).T,
    )


def lane_masks(rows):
    lane = lax.broadcasted_iota(jnp.int32, (rows, 128), 1)
    return (lane % HD) < HD // 2, lane < HD


def rel_z(z, i):
    return lax.rem(z + 1 + i, 4)


def each(found, act):
    for cond, c in found:
        if cond is None:
            act(c)
        else:
            pl.when(cond)(lambda c=c: act(c))


def start(c):
    c.start()


def wait(c):
    c.wait()


def run_copies(pairs, sems):
    copies = [pltpu.make_async_copy(a, b, sems.at[i]) for i, (a, b) in enumerate(pairs)]
    for c in copies:
        c.start()
    for c in copies:
        c.wait()


MICROS = {
    "stack_two": 1,
    "meet": 1,
    "prep_weights": 5,
    "stack_weights": 2,
    "split_quarters": 5,
    "pick_out_rows": 3,
    "sum_chips": 4,
    "join_cores": 5,
    "key_value_weights_back": 11,
    "join_near": 4,
    "join_projections": 3,
    "join_output": 5,
    "add_pairs": 3,
    "stack_pairs": 2,
    "halve_rows": 2,
    "join_feed_forward": 3,
    "finish_feed_forward": 6,
    "finish_rest": 4,
}


def whole(shape):
    return pl.BlockSpec(shape, lambda i: (0,) * len(shape))


def step_call(
    name, body, info, ins, outs, far=(), scratch=(), behind=(), passed=()
):
    n_in, n_out, n_behind, n_passed = len(ins), len(outs), len(behind), len(passed)

    def kernel(info_ref, *refs):
        after = refs[n_in + n_behind + n_passed :]
        body(info_ref, refs[:n_in], after[:n_out], after[n_out + n_passed :])

    return pl.pallas_call(
        kernel,
        grid=(1,),
        out_shape=tuple(jax.ShapeDtypeStruct(shape, dtype) for shape, dtype in outs)
        + tuple(jax.ShapeDtypeStruct(p.shape, p.dtype) for p in passed),
        in_specs=[SMEM]
        + [ANY if n in far else whole(x.shape) for n, x in enumerate(ins)]
        + [ANY] * (n_behind + n_passed),
        out_specs=tuple(whole(shape) for shape, _ in outs) + (ANY,) * n_passed,
        scratch_shapes=list(scratch),
        input_output_aliases={1 + n_in + n_behind + n: n_out + n for n in range(n_passed)},
        compiler_params=params(60, 1),
        cost_estimate=cost(MICROS[name]),
        name=name,
    )(info, *ins, *behind, *passed)


def meet(info, passed, behind=()):
    return step_call("meet", lambda *refs: None, info, (), (), behind=behind, passed=passed)


def prep_weights(info, w_gate, w_up, w_down_turned, w_out):
    def body(info, ins, outs, scratch):
        core, parity = info[1], info[4]
        turn, given, sems = scratch
        base = core * CORE_UNITS
        copies = [pltpu.make_async_copy(ins[n], given.at[n], sems.at[n]) for n in range(3)]
        for c in copies:
            c.start()
        row = pl.multiple_of((ZR - OUT_ROWS) * core, 16)
        outs[2][...] = ins[3][pl.ds(row, OUT_ROWS), :]
        for n in range(3):
            copies[n].wait()
            turn[...] = given[n].T
            outs[0][n] = turn[pl.ds(pl.multiple_of(base, 16), CORE_UNITS), :]
            quarter = pl.ds(pl.multiple_of(base + QUARTER * parity, 16), QUARTER)
            outs[1][QUARTER * n : QUARTER * n + QUARTER, :] = turn[quarter, :]

    return step_call(
        "prep_weights",
        body,
        info,
        (w_gate, w_up, w_down_turned, w_out),
        (((3, CORE_UNITS, D), BF16), ((PACKED, D), BF16), ((OUT_ROWS, D), BF16)),
        far=range(3),
        scratch=(
            pltpu.VMEM((2 * CORE_UNITS, D), BF16),
            pltpu.VMEM((3,) + w_gate.shape, BF16),
            pltpu.SemaphoreType.DMA((3,)),
        ),
    )


def stack_weights(info, parts, behind, passed):
    def body(info, ins, outs, scratch):
        for n in range(3):
            outs[0][n] = ins[n][...]

    out = ((3,) + parts[0].shape, BF16)
    return step_call("stack_weights", body, info, parts, (out,), behind=behind, passed=passed)


def split_quarters(info, over_z, deps):
    at = CUT - PACKED

    def body(info, ins, outs, scratch):
        src = ins[0]
        z = info[0]
        zs = [rel_z(z, i) for i in range(3)]
        pairs = [
            (src.at[zs[0]], outs[0].at[pl.ds(0, PACKED)]),
            (src.at[zs[1], pl.ds(0, at)], outs[0].at[pl.ds(PACKED, at)]),
            (src.at[zs[1], pl.ds(at, PACKED - at)], outs[1].at[pl.ds(0, PACKED - at)]),
            (src.at[zs[2]], outs[1].at[pl.ds(PACKED - at, PACKED)]),
        ]
        run_copies(pairs, scratch[0])

    half = (CUT, D)
    return step_call(
        "split_quarters",
        body,
        info,
        (over_z, *deps),
        ((half, BF16), (half, BF16)),
        range(1 + len(deps)),
        scratch=(pltpu.SemaphoreType.DMA((4,)),),
    )


def pre_kernel(info, xt_ref, cos_ref, sin_ref, *refs):
    own, pieces = refs[0], refs[1:9]
    attn_ref, attn_up, attn_lo, q_ref, kv_ref, x_ref, gains_ref, wq_out, wkv_out = refs[9:18]
    w_ref, sems, out_sems = refs[18:]
    step = pl.program_id(0)
    z, me = info[0], info[2]
    outs = [
        pltpu.make_async_copy(w_ref.at[:, pl.ds(0, WIDE)], wq_out, out_sems.at[0]),
        pltpu.make_async_copy(w_ref.at[:, pl.ds(896, QKV - 896)], wkv_out, out_sems.at[1]),
    ]

    def pieces_do(act):
        found = []

        def add(src, row, size, cond=None):
            view = w_ref.at[pl.ds(pl.multiple_of(row, 16), size)]
            found.append((cond, pltpu.make_async_copy(src, view, sems.at[len(found)])))

        add(own, z * ZR, ZR)
        for rel, piece in enumerate(pieces):
            c = me ^ rel
            for i in range(3):
                base = rel_z(z, i) * ZR
                add(piece.at[i, pl.ds(0, 16)], base + 32 * c, 16, c < 7)
                add(piece.at[i, pl.ds(16, 16)], base + jnp.minimum(32 * c + 16, ZR - 16), 16)
        each(found, act)

    @pl.when(step == 0)
    def _():
        pieces_do(start)

    first_half, low_head = lane_masks(ROWS)
    cos, sin = wide_tables(cos_ref[...], sin_ref[...])
    x_low = xt_ref[...].T
    x_ref[...] = x_low
    x = x_low.astype(F32)
    factor = lax.rsqrt(jnp.mean(x * x, axis=-1, keepdims=True) + NORM_EPS)

    @pl.when(step == 0)
    def _():
        pieces_do(wait)
        for c in outs:
            c.start()
        gains_ref[...] = w_ref[:, 1536:QKV].astype(F32).T[64:72]

    a = (x * factor * gains_ref[0:1, :]).astype(BF16)
    attn_ref[...] = a
    turned_a = a.T
    attn_up[...] = turned_a[0 : D // 2]
    attn_lo[...] = turned_a[D // 2 :]
    qk = dot(a, w_ref[:, 0:1280])
    vv = dot(a, w_ref[:, 1280:QKV])
    slabs = [rope_slab(qk[:, 128 * j : 128 * j + 128], cos, sin, first_half) for j in range(10)]
    for j in range(7):
        q_ref[:, 128 * j : 128 * j + 128] = slabs[j].astype(BF16)
    q_ref[:, 896:960] = slabs[7][:, :64].astype(BF16)
    mixed = jnp.where(low_head, vv[:, 256:384], slabs[7])
    for j, part in enumerate((slabs[8], slabs[9], mixed, vv[:, 0:128], vv[:, 128:256])):
        kv_ref[:, 128 * j : 128 * j + 128] = part.astype(BF16)

    @pl.when(step == pl.num_programs(0) - 1)
    def _():
        for c in outs:
            c.wait()


def by_rows(width):
    return pl.BlockSpec((ROWS, width), lambda i: (i, 0))


def by_lanes(height):
    return pl.BlockSpec((height, ROWS), lambda i: (0, i))


def pre_call(info, xt, cos, sin, pieces):
    t = xt.shape[1]
    return pl.pallas_call(
        pre_kernel,
        grid=(t // ROWS,),
        out_shape=(
            jax.ShapeDtypeStruct((t, D), BF16),
            jax.ShapeDtypeStruct((D // 2, t), BF16),
            jax.ShapeDtypeStruct((D // 2, t), BF16),
            jax.ShapeDtypeStruct((t, D), BF16),
            jax.ShapeDtypeStruct((t, KV_LANES), BF16),
            jax.ShapeDtypeStruct((t, D), BF16),
            jax.ShapeDtypeStruct((8, D), F32),
            jax.ShapeDtypeStruct((D, WIDE), BF16),
            jax.ShapeDtypeStruct((D, QKV - 896), BF16),
        ),
        in_specs=[SMEM, by_lanes(D), by_lanes(32), by_lanes(32)] + [ANY] * 9,
        out_specs=(
            by_rows(D), by_lanes(D // 2), by_lanes(D // 2), by_rows(D), by_rows(KV_LANES), by_rows(D), whole((8, D)),
            ANY, ANY,
        ),
        scratch_shapes=[
            pltpu.VMEM((D, QKV), BF16),
            pltpu.SemaphoreType.DMA((49,)),
            pltpu.SemaphoreType.DMA((2,)),
        ],
        compiler_params=params(60, 1),
        cost_estimate=cost(12),
        name="pre",
    )(info, xt, cos, sin, *pieces)


def start_window(tab, kvs, win, sem, blk, slot):
    def body(j, _):
        entry = tab[blk, j]
        which = entry // 1024
        idx = lax.rem(entry, 1024)
        dst = win.at[slot, pl.ds(pl.multiple_of(j * BLK, BLK), BLK)]
        for n, ref in enumerate(kvs):
            @pl.when(which == n)
            def _():
                src = ref.at[pl.ds(pl.multiple_of(idx * BLK, BLK), BLK)]
                pltpu.make_async_copy(src, dst, sem.at[slot]).start()
        return 0

    lax.fori_loop(0, NWB, body, 0)


def next_window(tab, kvs, win, sem, first=0):
    i = pl.program_id(0)
    slot = lax.rem(i, 2)

    @pl.when(i == 0)
    def _():
        start_window(tab, kvs, win, sem, i + first, slot)

    @pl.when(i + 1 < pl.num_programs(0))
    def _():
        start_window(tab, kvs, win, sem, i + first + 1, 1 - slot)

    pltpu.make_async_copy(win.at[slot], win.at[slot], sem.at[slot]).wait()
    return slot


def turned(flat):
    rows = flat.astype(F32)
    extra = -rows.shape[1] % 128
    if extra:
        rows = jnp.concatenate([rows, jnp.zeros((rows.shape[0], extra), F32)], axis=1)
    return rows.T


def unturned(parts):
    rows = sum(p.shape[0] for p in parts)
    extra = -rows % 128
    if extra:
        parts = parts + [jnp.zeros((extra, parts[0].shape[1]), F32)]
    return jnp.concatenate(parts, axis=0).T[:, :rows].astype(BF16)


def spread_heads(rows, count, low):
    width = GRP * BLK
    sides = [jnp.concatenate(rows[GRP * n : GRP * n + GRP], axis=1) for n in range(count)]
    empty = jnp.zeros((HD, width), rows[0].dtype)
    if count == 2:
        return jnp.concatenate(
            [jnp.concatenate([sides[0], empty], axis=1), jnp.concatenate([empty, sides[1]], axis=1)],
            axis=0,
        )
    return jnp.concatenate([sides[0], empty] if low else [empty, sides[0]], axis=0)


def head_half(j, kv_heads, low):
    upper = j >= GRP if len(kv_heads) == 2 else not low
    return HD if upper else 0


def fwd_kernel(n_kv, tab, lo_ref, q_ref, *refs):
    kvs = refs[:n_kv]
    mid_ref, rl_ref, p_ref, win, bias, scores, sem = refs[n_kv:]
    slot = next_window(tab, kvs, win, sem)
    row = lax.broadcasted_iota(jnp.int32, (SPAN, BLK), 0)
    lane = lax.broadcasted_iota(jnp.int32, (SPAN, BLK), 1)
    allowed = (row >= lo_ref[0]) & (row <= lane + WIN)
    bias[...] = jnp.where(allowed, 0.0, MASK_FILL)
    q_all = (turned(q_ref[...]) * (HD ** -0.5)).astype(BF16)
    outs, recips = [], []
    at = 0
    for k_slab, v_slab, kv_heads, k_low, v_low in PAIRS:
        keys = win[slot, :, 128 * k_slab : 128 * k_slab + 128]
        vals = win[slot, :, 128 * v_slab : 128 * v_slab + 128]
        count = GRP * len(kv_heads)
        width = BLK * count
        base = BLK * at
        q_rows = [q_all[HD * (at + j) : HD * (at + j) + HD] for j in range(count)]
        scores[:, :width] = dot(keys, spread_heads(q_rows, len(kv_heads), k_low))
        for j in range(count):
            s = scores[:, BLK * j : BLK * j + BLK] + bias[...]
            top = jnp.max(s, axis=0, keepdims=True)
            p_ref[0, :, base + BLK * j : base + BLK * j + BLK] = jnp.exp(s - top).astype(BF16)
        lhs = jnp.concatenate([vals.T, jnp.ones((16, SPAN), BF16)], axis=0)
        product = dot(lhs, p_ref[0, :, base : base + width])
        recip = 1.0 / product[128:129, :]
        for j in range(count):
            cols = slice(BLK * j, BLK * j + BLK)
            half = head_half(j, kv_heads, v_low)
            outs.append(product[half : half + HD, cols] * recip[:, cols])
            recips.append(recip[:, cols])
        at += count
    mid_ref[...] = unturned(outs)
    recips.append(jnp.zeros((16 - len(recips), BLK), F32))
    rl_ref[0] = jnp.concatenate(recips, axis=0)


def fwd_call(tab, lo, q, kvs):
    blocks = q.shape[0] // BLK
    n_kv = len(kvs)
    lanes, heads = D, HQ
    return pl.pallas_call(
        lambda *refs: fwd_kernel(n_kv, *refs),
        grid=(blocks,),
        out_shape=(
            jax.ShapeDtypeStruct((q.shape[0], lanes), BF16),
            jax.ShapeDtypeStruct((blocks, 16, BLK), F32),
            jax.ShapeDtypeStruct((blocks, SPAN, heads * BLK), BF16),
        ),
        in_specs=[
            SMEM,
            pl.BlockSpec((1, 1, BLK), lambda i: (i, 0, 0)),
            pl.BlockSpec((BLK, lanes), lambda i: (i, 0)),
        ]
        + [ANY] * n_kv,
        out_specs=(
            pl.BlockSpec((BLK, lanes), lambda i: (i, 0)),
            pl.BlockSpec((1, 16, BLK), lambda i: (i, 0, 0)),
            pl.BlockSpec((1, SPAN, heads * BLK), lambda i: (i, 0, 0)),
        ),
        scratch_shapes=[
            pltpu.VMEM((2, SPAN, KV_LANES), BF16),
            pltpu.VMEM((SPAN, BLK), F32),
            pltpu.VMEM((SPAN, 2 * GRP * BLK), F32),
            pltpu.SemaphoreType.DMA((2,)),
        ],
        compiler_params=params(60, 1),
        cost_estimate=cost(32),
        name="attend",
    )(tab, lo, q, *kvs)


def bwd_kernel(
    n_kv, n_dep, first, prev, out_units, n_slots, tab, slots, q_ref, do_ref, mid_ref, rl_ref, p_ref, cos_ref, sin_ref, *refs
):
    kvs = refs[:n_kv]
    n_out = len(out_units)
    refs = refs[n_kv + n_dep :]
    earlier = refs[:n_out] if prev else ()
    refs = refs[len(earlier) :]
    dq_ref = refs[0]
    outs = refs[1 : 1 + n_out]
    win, acc, scores, stage, stage_in, sem, out_sem, in_sem = refs[1 + n_out :]
    i = pl.program_id(0)
    blk = i + first
    slot = next_window(tab, kvs, win, sem, first)
    lanes = acc.shape[1]

    @pl.when(i == 0)
    def _():
        def clear(b, _):
            acc[pl.ds(pl.multiple_of(b * BLK, BLK), BLK), :] = jnp.zeros((BLK, lanes), F32)
            return 0

        lax.fori_loop(0, n_slots, clear, 0)

    def add(slab, value):
        for j in range(NWB):
            r = pl.ds(pl.multiple_of(slots[blk, j] * BLK, BLK), BLK)
            acc[r, 128 * slab : 128 * slab + 128] += value[BLK * j : BLK * j + BLK]

    q_all = (turned(q_ref[...]) * (HD ** -0.5)).astype(BF16)
    do_all = turned(do_ref[...])
    o_all = turned(mid_ref[...])
    cos, sin = cos_ref[...], sin_ref[...]
    grads = []
    at = 0
    for k_slab, v_slab, kv_heads, k_low, v_low in PAIRS:
        keys = win[slot, :, 128 * k_slab : 128 * k_slab + 128]
        vals = win[slot, :, 128 * v_slab : 128 * v_slab + 128]
        count = GRP * len(kv_heads)
        width = BLK * count
        base = BLK * at
        q_rows, do_rows, dots = [], [], []
        for j in range(count):
            r = slice(HD * (at + j), HD * (at + j) + HD)
            q_rows.append(q_all[r])
            scaled = do_all[r] * rl_ref[0, at + j : at + j + 1, :]
            dots.append(jnp.sum(scaled * o_all[r], axis=0, keepdims=True))
            do_rows.append(scaled.astype(BF16))
        q_wide = spread_heads(q_rows, len(kv_heads), k_low)
        do_wide = spread_heads(do_rows, len(kv_heads), v_low)
        scores[:, :width] = dot(vals, do_wide)
        ds = []
        for j in range(count):
            p = p_ref[0, :, base + BLK * j : base + BLK * j + BLK].astype(F32)
            ds.append((p * (scores[:, BLK * j : BLK * j + BLK] - dots[j])).astype(BF16))
        ds = jnp.concatenate(ds, axis=1)
        probs = p_ref[0, :, base : base + width]
        if len(kv_heads) == 2:
            add(k_slab, dot_nt(ds, q_wide))
            add(v_slab, dot_nt(probs, do_wide))
        else:
            add(
                k_slab,
                dot_nt(
                    jnp.concatenate([ds, probs], axis=1),
                    jnp.concatenate([q_wide, do_wide], axis=1),
                ),
            )
        dq = dot(keys.T, ds) * (HD ** -0.5)
        for j in range(count):
            top = head_half(j, kv_heads, k_low)
            cols = slice(BLK * j, BLK * j + BLK)
            first = dq[top : top + 32, cols]
            second = dq[top + 32 : top + 64, cols]
            grads.append(first * cos + second * sin)
            grads.append(second * cos - first * sin)
        at += count
    dq_ref[...] = unturned(grads)

    @pl.when(i == pl.num_programs(0) - 1)
    def _():
        per = 6 * BLK
        places = [(n, u) for n, units in enumerate(out_units) for u in range(units)]
        copies, loads = [], []

        def load(t):
            if prev and t < len(places):
                n, u = places[t]
                c = pltpu.make_async_copy(
                    earlier[n].at[pl.ds(per * u, per)], stage_in.at[t % 2], in_sem.at[t % 2]
                )
                c.start()
                loads.append(c)

        load(0)
        load(1)
        for t, (n, u) in enumerate(places):
            s = t % 2
            if t >= 2:
                copies[t - 2].wait()
            value = acc[per * t : per * t + per, :]
            if prev:
                loads[t].wait()
                value = value + stage_in[s].astype(F32)
            stage[s] = value.astype(BF16)
            load(t + 2)
            c = pltpu.make_async_copy(stage.at[s], outs[n].at[pl.ds(per * u, per)], out_sem.at[s])
            c.start()
            copies.append(c)
        copies[-2].wait()
        copies[-1].wait()


def bwd_call(first, blocks, earlier, deps, tab, slots, out_units, q, do, mid, rl, p, cos, sin, kvs):
    n_kv = len(kvs)
    lanes, heads, width = D, HQ, KV_LANES
    n_slots = 6 * sum(out_units)
    flat = pl.BlockSpec((BLK, lanes), lambda i: (i + first, 0))
    table = pl.BlockSpec((32, BLK), lambda i: (0, i + first))
    prev = bool(earlier)
    return pl.pallas_call(
        lambda *refs: bwd_kernel(n_kv, len(deps), first, prev, out_units, n_slots, *refs),
        grid=(blocks,),
        out_shape=(jax.ShapeDtypeStruct((blocks * BLK, lanes), BF16),)
        + tuple(jax.ShapeDtypeStruct((6 * BLK * u, width), BF16) for u in out_units),
        in_specs=[
            SMEM,
            SMEM,
            flat,
            flat,
            flat,
            pl.BlockSpec((1, 16, BLK), lambda i: (i + first, 0, 0)),
            pl.BlockSpec((1, SPAN, heads * BLK), lambda i: (i + first, 0, 0)),
            table,
            table,
        ]
        + [ANY] * (n_kv + len(deps) + len(earlier)),
        out_specs=(pl.BlockSpec((BLK, lanes), lambda i: (i, 0)),) + (ANY,) * len(out_units),
        scratch_shapes=[
            pltpu.VMEM((2, SPAN, width), BF16),
            pltpu.VMEM((n_slots * BLK, width), F32),
            pltpu.VMEM((SPAN, 2 * GRP * BLK), F32),
            pltpu.VMEM((2, 6 * BLK, width), BF16),
            pltpu.VMEM((2, 6 * BLK, width), BF16),
            pltpu.SemaphoreType.DMA((2,)),
            pltpu.SemaphoreType.DMA((2,)),
            pltpu.SemaphoreType.DMA((2,)),
        ],
        compiler_params=params(60, 1),
        cost_estimate=cost(10000),
        name=f"attend_back_{first}",
    )(tab, slots, q, do, mid, rl, p, cos, sin, *kvs, *deps, *earlier)


def pro_kernel(info, mid_ref, x_ref, gain_ref, own, *refs):
    here, there = refs[0:3], refs[3:6]
    h1_ref, low_ref, w_out, _, _, w_ref, sems, out_sem = refs[9:]
    z, core = info[0], info[1]
    step = pl.program_id(0)
    out_copy = pltpu.make_async_copy(w_ref, w_out, out_sem)
    found = []

    def bring(src, row, size):
        dst = w_ref.at[pl.ds(pl.multiple_of(row, 16), size)]
        found.append((None, pltpu.make_async_copy(src, dst, sems.at[len(found)])))

    bring(own, z * ZR, ZR)
    skip = 16 * (1 - core)
    for i in range(3):
        base = rel_z(z, i) * ZR
        bring(here[i], base + (ZR - OUT_ROWS) * core, OUT_ROWS)
        bring(
            there[i].at[pl.ds(pl.multiple_of(skip, 16), OUT_ROWS - 16)],
            base + (ZR - OUT_ROWS) * (1 - core) + skip,
            OUT_ROWS - 16,
        )

    @pl.when(step == 0)
    def _():
        each(found, start)
        each(found, wait)
        out_copy.start()

    h = x_ref[...].astype(F32) + dot(mid_ref[...], w_ref[...])
    factor = lax.rsqrt(jnp.mean(h * h, axis=-1, keepdims=True) + NORM_EPS)
    h1_ref[...] = h
    low_ref[:, 0:D] = (h * factor * gain_ref[1:2, :]).astype(BF16)
    low_ref[:, D:WIDE] = jnp.zeros((ROWS, WIDE - D), BF16)

    @pl.when(step == pl.num_programs(0) - 1)
    def _():
        out_copy.wait()


def pro_call(info, mid, x, gains, own, here, there, dep, passed):
    t = x.shape[0]
    return pl.pallas_call(
        pro_kernel,
        grid=(t // ROWS,),
        out_shape=(
            jax.ShapeDtypeStruct((t, D), F32),
            jax.ShapeDtypeStruct((t, WIDE), BF16),
            jax.ShapeDtypeStruct((D, D), BF16),
            *[jax.ShapeDtypeStruct(p.shape, p.dtype) for p in passed],
        ),
        in_specs=[SMEM, by_rows(D), by_rows(D), whole((8, D))] + [ANY] * 10,
        out_specs=(by_rows(D), by_rows(WIDE), ANY, ANY, ANY),
        input_output_aliases={12: 3, 13: 4},
        scratch_shapes=[
            pltpu.VMEM((D, D), BF16),
            pltpu.SemaphoreType.DMA((7,)),
            pltpu.SemaphoreType.DMA,
        ],
        compiler_params=params(60, 1),
        cost_estimate=cost(7),
        name="out_projection",
    )(info, mid, x, gains, own, *here, *there, dep, *passed)


def ffn_kernel(info, a0, a1, c0, c1, own, *refs):
    here = refs[:4]
    acc_outs, p_ref, q_refs = refs[4:9], refs[9], refs[10:14]
    (
        wbuf, a_all, c_all, c_turn, hid_s, gg_s, gu_s, stage, acc_o, acc_g, send_o, send_lo, send_hi,
        io_sem, w_sem, out_sem, acc_sem,
    ) = refs[14:]
    z, chip, parity = info[0], info[3], info[4]
    t = a0.shape[0]
    units = wbuf.shape[1]
    ins = [
        pltpu.make_async_copy(a0, a_all.at[pl.ds(0, t)], io_sem.at[0]),
        pltpu.make_async_copy(a1, a_all.at[pl.ds(t, t)], io_sem.at[1]),
        pltpu.make_async_copy(c0, c_turn.at[0], io_sem.at[2]),
        pltpu.make_async_copy(c1, c_turn.at[1], io_sem.at[3]),
    ]
    copies = [pltpu.make_async_copy(own, wbuf.at[:, pl.ds(0, CORE_UNITS)], w_sem.at[0])]
    for n_par, par in enumerate((parity, 1 - parity)):
        for i in range(3):
            for n in range(3):
                a0_row = PACKED * i + QUARTER * n
                for ref, p0, p1 in ((here[2 * n_par], 0, CUT), (here[2 * n_par + 1], CUT, 2 * CUT)):
                    a, b = max(p0, a0_row), min(p1, a0_row + QUARTER)
                    if a < b:
                        row = CORE_UNITS * (i + 1) + QUARTER * par + (a - a0_row)
                        dst = wbuf.at[n, pl.ds(pl.multiple_of(row, 16), b - a)]
                        copies.append(
                            pltpu.make_async_copy(
                                ref.at[pl.ds(a - p0, b - a)], dst, w_sem.at[len(copies)]
                            )
                        )
    for c in ins[2:] + ins[:2] + copies:
        c.start()
    for h in range(2):
        ins[2 + h].wait()
        c_all[t * h : t * h + t, :] = c_turn[h].T
    for c in ins[:2] + copies[:1]:
        c.wait()

    def forward(c, _):
        @pl.when(c == 1)
        def _():
            for late in copies[1:]:
                late.wait()

        u = pl.ds(pl.multiple_of(c * UNITS, UNITS), UNITS)
        for h in range(2 * t // ROWS):
            r = slice(ROWS * h, ROWS * h + ROWS)
            gate = dot_nt(a_all[r, 0:D], wbuf[0, u, :])
            up = dot_nt(a_all[r, 0:D], wbuf[1, u, :])
            grad = dot_nt(c_all[r, :], wbuf[2, u, :])
            sig = lax.logistic(gate)
            swish = gate * sig
            hid_s[r, u] = (swish * up).astype(BF16)
            gg_s[r, u] = (grad * up * (sig * (1.0 + gate * (1.0 - sig)))).astype(BF16)
            gu_s[r, u] = (grad * swish).astype(BF16)
        return 0

    lax.fori_loop(0, units // UNITS, forward, 0)

    def sums(r):
        left = dot(hid_s[r, :], wbuf[2])
        right = dot(gg_s[r, :], wbuf[0]) + dot(gu_s[r, :], wbuf[1])
        return left, right

    def mine(i, _):
        r = pl.ds(pl.multiple_of(i * ROWS, ROWS), ROWS)
        acc_o[r, :], acc_g[r, :] = sums(r)
        return 0

    def others(i, _):
        r = pl.ds(pl.multiple_of(i * ROWS, ROWS), ROWS)
        left, right = sums(pl.ds(pl.multiple_of(t + i * ROWS, ROWS), ROWS))
        empty = jnp.zeros((ROWS, WIDE - D), BF16)
        send_o[r, 0:D] = left.astype(BF16)
        send_o[r, D:WIDE] = empty
        half = WIDE // 2
        send_lo[r, :] = right[:, 0:half].astype(BF16)
        send_hi[r, 0 : D - half] = right[:, half:D].astype(BF16)
        send_hi[r, D - half : half] = empty
        return 0

    lax.fori_loop(0, t // ROWS, others, 0)
    lax.fori_loop(0, t // ROWS, mine, 0)
    acc_copies = [
        pltpu.make_async_copy(src, dst, acc_sem.at[n])
        for n, (src, dst) in enumerate(zip((acc_o, acc_g, send_o, send_lo, send_hi), acc_outs))
    ]
    for c in acc_copies:
        c.start()

    def back_copies(c, slot):
        found = []
        per = CORE_UNITS // SEG
        for n in range(UNITS // SEG):
            j = c * (UNITS // SEG) + n
            within = lax.rem(j, per)
            zz = lax.rem(z + j // per, 4)
            n_p = P_ROWS // SEG
            first = within < n_p
            row = pl.multiple_of(jnp.minimum(within, n_p - 1) * SEG, SEG)
            src = stage.at[slot, :, pl.ds(SEG * n, SEG)]
            dst = p_ref.at[zz, :, pl.ds(row, SEG)]
            found.append((first, pltpu.make_async_copy(src, dst, out_sem.at[slot, 24 + n])))
            piece = 6 * n
            for k in range(per - n_p):
                at = SEG * k
                while at < SEG * k + SEG:
                    owner = at // Q_ROWS
                    size = min(SEG * k + SEG, Q_ROWS * (owner + 1)) - at
                    src = stage.at[slot, :, pl.ds(SEG * n + at - SEG * k, size)]
                    for r in range(4):
                        dst = q_refs[r].at[zz, :, pl.ds(at - Q_ROWS * owner, size)]
                        copy = pltpu.make_async_copy(src, dst, out_sem.at[slot, piece])
                        found.append(((within == n_p + k) & (chip ^ owner == r), copy))
                    at += size
                    piece += 1
        return found

    def backward(c, _):
        u = pl.ds(pl.multiple_of(c * UNITS, UNITS), UNITS)
        slot = lax.rem(c, 2)

        @pl.when(c >= 2)
        def _():
            each(back_copies(c - 2, slot), wait)

        stage[slot, 0] = dot_tn(gg_s[:, u], a_all[:, 0:D]).astype(BF16)
        stage[slot, 1] = dot_tn(gu_s[:, u], a_all[:, 0:D]).astype(BF16)
        stage[slot, 2] = dot_tn(hid_s[:, u], c_all[...]).astype(BF16)
        each(back_copies(c, slot), start)
        return 0

    n_chunks = units // UNITS
    lax.fori_loop(0, n_chunks, backward, 0)
    for c in (n_chunks - 2, n_chunks - 1):
        each(back_copies(jnp.int32(c), c % 2), wait)
    for c in acc_copies:
        c.wait()


def ffn_call(info, a0, a1, c0, c1, own, here):
    t = a0.shape[0]
    units = 4 * CORE_UNITS
    return pl.pallas_call(
        ffn_kernel,
        out_shape=(
            jax.ShapeDtypeStruct((t, D), F32),
            jax.ShapeDtypeStruct((t, D), F32),
            jax.ShapeDtypeStruct((t, WIDE), BF16),
            jax.ShapeDtypeStruct((t, WIDE // 2), BF16),
            jax.ShapeDtypeStruct((t, WIDE // 2), BF16),
            jax.ShapeDtypeStruct((4, 3, P_ROWS, D), BF16),
            *[jax.ShapeDtypeStruct((4, 3, Q_ROWS, D), BF16)] * 4,
        ),
        in_specs=[SMEM] + [ANY] * 9,
        out_specs=(ANY,) * 10,
        scratch_shapes=[
            pltpu.VMEM((3, units, D), BF16),
            pltpu.VMEM((2 * t, WIDE), BF16),
            pltpu.VMEM((2 * t, D), BF16),
            pltpu.VMEM((2, D, t), BF16),
            pltpu.VMEM((2 * t, units), BF16),
            pltpu.VMEM((2 * t, units), BF16),
            pltpu.VMEM((2 * t, units), BF16),
            pltpu.VMEM((2, 3, UNITS, D), BF16),
            pltpu.VMEM((t, D), F32),
            pltpu.VMEM((t, D), F32),
            pltpu.VMEM((t, WIDE), BF16),
            pltpu.VMEM((t, WIDE // 2), BF16),
            pltpu.VMEM((t, WIDE // 2), BF16),
            pltpu.SemaphoreType.DMA((4,)),
            pltpu.SemaphoreType.DMA((24,)),
            pltpu.SemaphoreType.DMA((2, 28)),
            pltpu.SemaphoreType.DMA((5,)),
        ],
        compiler_params=params(60),
        cost_estimate=cost(50),
        name="feed_forward",
    )(info, a0, a1, c0, c1, own, *here)


def put_shards(ref, product, gain_grad):
    extra = ref.shape[-1] - product.shape[1]
    if extra:
        product = jnp.concatenate([product, jnp.zeros((product.shape[0], extra), F32)], axis=1)
    width = product.shape[1]
    first_row = lax.broadcasted_iota(jnp.int32, (ZP - ZR, width), 0) == 0
    for n in range(4):
        ref[n, 0:ZR, :] = product[ZR * n : ZR * n + ZR].astype(BF16)
        if gain_grad is None:
            ref[n, ZR:ZP, :] = jnp.zeros((ZP - ZR, width), BF16)
        else:
            part = jnp.concatenate(
                [gain_grad[:, ZR * n : ZR * n + ZR], jnp.zeros((1, width - ZR), F32)], axis=1
            )
            ref[n, ZR:ZP, :] = jnp.where(first_row, part, 0.0).astype(BF16)


def put_halves(core, keep_ref, send_ref, product, gain_grad):
    extra = jnp.zeros((product.shape[0], WIDE - product.shape[1]), F32)
    wide = jnp.concatenate([product, extra], axis=1)
    half = WIDE // 2
    for side, (first, second) in enumerate(((keep_ref, send_ref), (send_ref, keep_ref))):
        @pl.when(core == side)
        def _():
            put_shards(first, wide[:, :half], gain_grad)
            put_shards(second, wide[:, half:], None)


def epi_kernel(
    info, h1_ref, acc_g, got_lo, got_hi, ct_ref, gain_ref, w_ref, mid_ref, *refs
):
    gh_ref, gm_ref, keep_ref, send_ref, acc, total = refs
    i = pl.program_id(0)

    @pl.when(i == 0)
    def _():
        acc[...] = jnp.zeros((D, D), F32)
        total[...] = jnp.zeros((8, D), F32)

    h = h1_ref[...]
    factor = lax.rsqrt(jnp.mean(h * h, axis=-1, keepdims=True) + NORM_EPS)
    normed = h * factor
    got = jnp.concatenate([got_lo[...], got_hi[...]], axis=1)
    g = acc_g[...] + got[:, 0:D].astype(F32)
    scaled = g * gain_ref[1:2, :]
    back = factor * (scaled - normed * jnp.mean(scaled * normed, axis=-1, keepdims=True))
    full = ct_ref[...].T.astype(F32) + back
    gh_ref[...] = full
    res = full.astype(BF16)
    gm_ref[...] = dot_nt(res, w_ref[...]).astype(BF16)
    total[0:1, :] += jnp.sum(g * normed, axis=0, keepdims=True)
    acc[...] += dot_tn(mid_ref[...], res)

    @pl.when(i == pl.num_programs(0) - 1)
    def _():
        put_halves(info[1], keep_ref, send_ref, acc[...], total[0:1, :])


def epi_call(info, h1, acc_g, got_lo, got_hi, cot_t, gains, w_out, mid):
    t = h1.shape[0]
    rows = pl.BlockSpec((ROWS, D), lambda i: (i, 0))
    return pl.pallas_call(
        epi_kernel,
        grid=(t // ROWS,),
        out_shape=(
            jax.ShapeDtypeStruct((t, D), F32),
            jax.ShapeDtypeStruct((t, D), BF16),
            jax.ShapeDtypeStruct((4, ZP, WIDE // 2), BF16),
            jax.ShapeDtypeStruct((4, ZP, WIDE // 2), BF16),
        ),
        in_specs=[
            SMEM,
            rows,
            rows,
            by_rows(WIDE // 2),
            by_rows(WIDE // 2),
            by_lanes(D),
            whole((8, D)),
            whole((D, D)),
            rows,
        ],
        out_specs=(rows, rows) + (whole((4, ZP, WIDE // 2)),) * 2,
        scratch_shapes=[pltpu.VMEM((D, D), F32), pltpu.VMEM((8, D), F32)],
        compiler_params=params(60, 1),
        cost_estimate=cost(12),
        name="feed_forward_norm_back",
    )(info, h1, acc_g, got_lo, got_hi, cot_t, gains, w_out, mid)


def post_q_kernel(info, a_ref, g_ref, w_ref, _, keep_ref, send_ref, part_ref, acc):
    step = pl.program_id(0)

    @pl.when(step == 0)
    def _():
        acc[...] = jnp.zeros((D, D), F32)

    g = g_ref[...]
    part_ref[...] = dot_nt(g, w_ref[:, 0:D])
    acc[...] += dot_tn(a_ref[...], g)

    @pl.when(step == pl.num_programs(0) - 1)
    def _():
        put_halves(info[1], keep_ref, send_ref, acc[...], None)


def post_q_call(info, a, g, w, dep):
    t = a.shape[0]
    piece = (4, ZP, WIDE // 2)
    return pl.pallas_call(
        post_q_kernel,
        grid=(t // ROWS,),
        out_shape=(
            jax.ShapeDtypeStruct(piece, BF16),
            jax.ShapeDtypeStruct(piece, BF16),
            jax.ShapeDtypeStruct((t, D), F32),
        ),
        in_specs=[SMEM, by_rows(D), by_rows(D), whole(w.shape), ANY],
        out_specs=(whole(piece), whole(piece), by_rows(D)),
        scratch_shapes=[pltpu.VMEM((D, D), F32)],
        compiler_params=params(60, 1),
        cost_estimate=cost(8),
        name="query_back",
    )(info, a, g, w, dep)


def turn_back(slab, cos, sin, first_half, low_head):
    mixed = slab(2)
    k4 = jnp.where(low_head, 0.0, rope_slab(mixed, cos, sin, first_half))
    k01 = rope_slab(slab(0), cos, sin, first_half)
    k23 = rope_slab(slab(1), cos, sin, first_half)
    v4 = jnp.where(low_head, mixed, 0.0)
    return jnp.concatenate([k4, k01, k23, slab(3), slab(4), v4], axis=1).astype(BF16)


def kv_weights_back(info, cos, sin, turned, totals, dep):
    t = turned[0].shape[1]
    piece = ((4, ZP, 384), BF16)
    n_chips = len(totals)

    def body(info, ins, outs, scratch):
        cos_ref, sin_ref = ins[0], ins[1]
        low, acc, a_buf, g_buf, sems = scratch
        first_half, low_head = lane_masks(ROWS)
        copies = []
        for c in range(n_chips):
            pairs = [(ins[2 + 2 * c + n], a_buf.at[2 * c + n]) for n in range(2)]
            pairs.append((ins[2 + len(turned) + c], g_buf.at[pl.ds(t * c, t)]))
            copies.append(
                [pltpu.make_async_copy(a, b, sems.at[c, n]) for n, (a, b) in enumerate(pairs)]
            )
            for copy in copies[-1]:
                copy.start()
        for c in range(n_chips):
            for copy in copies[c]:
                copy.wait()
            for i in range(t // ROWS):
                at = ROWS * i

                def slab(j):
                    return g_buf[t * c + at : t * c + at + ROWS, 128 * j : 128 * j + 128].astype(F32)

                r = slice(t * c + at, t * c + at + ROWS)
                cos, sin = wide_tables(cos_ref[:, r], -sin_ref[:, r])
                low[at : at + ROWS, :] = turn_back(slab, cos, sin, first_half, low_head)
            for n, rows in enumerate((slice(0, D // 2), slice(D // 2, D))):
                value = dot(a_buf[2 * c + n], low[...])
                if c == 0:
                    acc[rows, :] = value
                else:
                    acc[rows, :] += value
        for core, (k_out, v_out) in enumerate(((outs[0], outs[1]), (outs[1], outs[0]))):
            @pl.when(info[1] == core)
            def _():
                put_shards(k_out, acc[:, 0:384], None)
                put_shards(v_out, acc[:, 384:768], None)

    return step_call(
        "key_value_weights_back",
        body,
        info,
        (cos, sin, *turned, *totals),
        (piece, piece),
        far=range(2, 2 + len(turned) + len(totals)),
        scratch=(
            pltpu.VMEM((t, 768), BF16),
            pltpu.VMEM((D, 768), F32),
            pltpu.VMEM((len(turned),) + turned[0].shape, BF16),
            pltpu.VMEM((t * n_chips, KV_LANES), BF16),
            pltpu.SemaphoreType.DMA((n_chips, 3)),
        ),
        behind=(dep,),
    )


def post_kv_kernel(
    info, s0, s1, s2, cos_ref, sin_ref, part_ref, w_ref, x_ref, gh_ref, gain_ref, ig_ref,
):
    first_half, low_head = lane_masks(ROWS)

    def slab(j):
        c = slice(128 * j, 128 * j + 128)
        return s0[:, c].astype(F32) + s1[:, c].astype(F32) + s2[:, c].astype(F32)

    cos, sin = wide_tables(cos_ref[...], -sin_ref[...])
    low = turn_back(slab, cos, sin, first_half, low_head)
    g = (
        part_ref[...]
        + dot_nt(low[:, 0:384], w_ref[:, 0:384])
        + dot_nt(low[:, 384:704], w_ref[:, 384:704])
    )
    x = x_ref[...].astype(F32)
    factor = lax.rsqrt(jnp.mean(x * x, axis=-1, keepdims=True) + NORM_EPS)
    normed = x * factor
    scaled = g * gain_ref[0:1, :]
    back = factor * (scaled - normed * jnp.mean(scaled * normed, axis=-1, keepdims=True))
    ig_ref[...] = (gh_ref[...] + back).astype(BF16).T


def post_kv_call(info, sums, cos, sin, part, w, x, gh, gain, dep):
    t = x.shape[0]
    return pl.pallas_call(
        lambda *refs: post_kv_kernel(*refs[:11], refs[12]),
        grid=(t // ROWS,),
        out_shape=jax.ShapeDtypeStruct((D, t), BF16),
        in_specs=[SMEM]
        + [by_rows(KV_LANES)] * 3
        + [by_lanes(32)] * 2
        + [by_rows(D), whole(w.shape)]
        + [by_rows(D)] * 2
        + [whole((8, D)), ANY],
        out_specs=by_lanes(D),
        compiler_params=params(60, 1),
        cost_estimate=cost(8),
        name="key_value_back",
    )(info, *sums, cos, sin, part, w, x, gh, gain, dep)


def finish_ffn(info, mine, other, dep):
    out = ((D, 2 * CORE_UNITS), F32)

    def body(info, ins, outs, scratch):
        rows = scratch[0]
        for n in range(3):
            for ref, side in ((ins[0], info[1]), (ins[1], 1 - info[1])):
                at = pl.multiple_of(side * CORE_UNITS, 16)
                rows[pl.ds(at, CORE_UNITS), :] = ref[n].astype(F32)
            outs[n][...] = rows[...].T

    return step_call(
        "finish_feed_forward",
        body,
        info,
        (mine, other),
        (out,) * 3,
        scratch=(pltpu.VMEM((2 * CORE_UNITS, D), F32),),
        behind=(dep,),
    )


def finish_rest(info, mine, other, w_own):
    half = WIDE // 2

    def body(info, ins, outs, scratch):
        wq_ref, wo_ref, wk_ref, wv_ref, one_ref, two_ref = outs

        def emit(first, second):
            def both(at):
                lanes = slice(at, at + half)
                return jnp.concatenate([first[0:ZR, lanes], second[0:ZR, lanes]], axis=1)

            wo_ref[...] = both(0).astype(F32)[:, 0:D]
            query = both(half).astype(F32)[:, 0:D]
            wq_ref[...] = query
            k = first[:, WIDE : WIDE + 384].astype(F32)
            v = second[:, WIDE : WIDE + 384].astype(F32)
            k_t = k.T
            wk_ref[...] = jnp.concatenate([k_t[128:384], k_t[64:128]], axis=0)[:, 0:ZR]
            wv_ref[...] = v.T[0:320, 0:ZR]
            w = ins[2][...].astype(F32)
            total = jnp.sum(query * w[:, 0:D], axis=1, keepdims=True)
            total += jnp.sum(k[0:ZR, 128:384] * w[:, 1024:1280], axis=1, keepdims=True)
            total += jnp.sum(k[0:ZR, 64:128] * w[:, 960:1024], axis=1, keepdims=True)
            total += jnp.sum(v[0:ZR, 0:320] * w[:, 1280:1600], axis=1, keepdims=True)
            total = total / w[:, 1600:1601]
            one_ref[...] = jnp.broadcast_to(total, (ZR, 128)).T[0:1, :]
            two_ref[...] = first[ZR:ZP, :].astype(F32)[0:1, 0:ZR]

        for core, refs in enumerate(((ins[0], ins[1]), (ins[1], ins[0]))):
            @pl.when(info[1] == core)
            def _():
                emit(*refs)

    outs = (((ZR, D), F32), ((ZR, D), F32), ((320, ZR), F32), ((320, ZR), F32), ((1, ZR), F32), ((1, ZR), F32))
    return step_call("finish_rest", body, info, (mine, other, w_own), outs)


def sum_chips(info, terms, pair, passed, behind):
    n_terms = len(terms)

    def body(info, ins, outs, scratch):
        for zz in range(4):
            outs[0][zz] = sum(ins[k][zz].astype(F32) for k in range(n_terms)).astype(BF16)
        outs[1][...] = ins[n_terms][...] + ins[n_terms + 1][...]

    outs = ((terms[0].shape, BF16), (pair[0].shape, BF16))
    return step_call(
        "sum_chips", body, info, (*terms, *pair), outs, behind=behind, passed=passed
    )


def join_cores(info, keep, recv, over_z):
    rows = keep.shape[0] // 4
    cut = rows // 2
    p_cut = P_ROWS // 2

    def body(info, ins, outs, scratch):
        for n in range(3):
            r = slice(rows * n, rows * n + rows)
            outs[n][...] = ins[0][r, :] + ins[1][r, :]
        for n in range(2):
            r = slice(3 * rows + cut * n, 3 * rows + cut * n + cut)
            outs[3 + n][...] = ins[0][r, :] + ins[1][r, :]
            outs[5 + n][...] = ins[2][0, :, p_cut * n : p_cut * n + p_cut, :]

    outs = (((rows, KV_LANES), BF16),) * 3 + (((cut, KV_LANES), BF16),) * 2
    outs += (((3, p_cut, D), BF16),) * 2
    return step_call("join_cores", body, info, (keep, recv, over_z), outs)


def join_near(info, to_x, to_y, from_x, from_y, pairs, passed):
    cut = from_x.shape[0]

    def body(info, ins, outs, scratch):
        to_x, to_y, from_x, from_y = ins[:4]
        outs[0][0:cut, :] = to_x[0:cut, :]
        outs[0][cut : 2 * cut, :] = to_x[cut : 2 * cut, :] + from_y[...]
        outs[1][0:cut, :] = to_y[0:cut, :] + from_x[...]
        outs[1][cut : 2 * cut, :] = to_y[cut : 2 * cut, :]
        for n in range(2):
            outs[2 + n][...] = ins[4 + 2 * n][...] + ins[5 + 2 * n][...]

    flat = [a for pair in pairs for a in pair]
    outs = ((to_x.shape, BF16),) * 2 + tuple((a.shape, BF16) for a, _ in pairs)
    return step_call(
        "join_near", body, info, (to_x, to_y, from_x, from_y, *flat), outs, passed=passed
    )


def join_projections(info, q_pair, kv_pair, dep):
    half = WIDE // 2

    def body(info, ins, outs, scratch):
        outs[0][:, :, 0:half] = ins[0][...] + ins[1][...]
        outs[0][:, :, half : half + 384] = ins[2][...] + ins[3][...]

    out = ((4, ZP, half + 384), BF16)
    return step_call("join_projections", body, info, (*q_pair, *kv_pair), (out,), behind=(dep,))[0]


def join_output(info, h1, acc_o, got_o, dep):
    t = h1.shape[0]

    def body(info, ins, outs, scratch):
        for i in range(t // ROWS):
            r = slice(ROWS * i, ROWS * i + ROWS)
            value = ins[0][r, :] + ins[1][r, :] + ins[2][r, 0:D].astype(F32)
            outs[0][:, r] = value.astype(BF16).T

    out = ((D, t), BF16)
    return step_call("join_output", body, info, (h1, acc_o, got_o), (out,), behind=(dep,))[0]


def halve_rows(info, left, right, behind):
    rows = left.shape[1] // 2
    lanes = left.shape[2], right.shape[2]

    def body(info, ins, outs, scratch):
        for n in range(2):
            r = slice(rows * n, rows * n + rows)
            outs[n][:, 0 : lanes[0]] = ins[0][0, r, :]
            outs[n][:, lanes[0] : sum(lanes)] = ins[1][0, r, :]

    outs = (((rows, sum(lanes)), BF16),) * 2
    return step_call("halve_rows", body, info, (left, right), outs, behind=behind)


def add_pairs(info, pairs, passed=()):
    def body(info, ins, outs, scratch):
        for n in range(len(pairs)):
            outs[n][...] = ins[2 * n][...] + ins[2 * n + 1][...]

    flat = [a for pair in pairs for a in pair]
    outs = tuple((a.shape, BF16) for a, _ in pairs)
    return step_call("add_pairs", body, info, flat, outs, passed=passed)


def stack_two(info, first, second, behind):
    def body(info, ins, outs, scratch):
        for n in range(2):
            outs[0][n] = ins[n][...]

    out = ((2,) + first.shape, BF16)
    return step_call("stack_two", body, info, (first, second), (out,), behind=behind)[0]


def stack_pairs(info, pairs, dep):
    rows = pairs[0][0].shape[0]

    def body(info, ins, outs, scratch):
        for n in range(2):
            outs[0][rows * n : rows * n + rows, :] = ins[2 * n][...] + ins[2 * n + 1][...]

    flat = [a for pair in pairs for a in pair]
    shape = (2 * rows,) + pairs[0][0].shape[1:]
    return step_call("stack_pairs", body, info, flat, ((shape, BF16),), behind=(dep,))[0]


def join_ffn(info, pairs, near, far, dep):
    cut = P_ROWS // 2

    def body(info, ins, outs, scratch):
        chip = info[3]
        out = outs[0]
        for n in range(2):
            out[:, cut * n : cut * n + cut, :] = ins[2 * n][...] + ins[2 * n + 1][...]
        for r in range(4):
            at = pl.multiple_of(P_ROWS + Q_ROWS * (chip ^ r), 16)
            out[:, pl.ds(at, Q_ROWS), :] = ins[4 + r // 2][r % 2]

    flat = [a for pair in pairs for a in pair]
    return step_call(
        "join_feed_forward",
        body,
        info,
        (*flat, near, far),
        (((3, CORE_UNITS, D), BF16),),
        behind=(dep,),
    )[0]


def rows_after(x, start, size, tok, axis=0):
    return lax.dynamic_slice_in_dim(x, start + tok, size, axis=axis)


def z_shift(x, step):
    n = 4
    return lax.ppermute(x, "fsdp", [(i, (i + step) % n) for i in range(n)])


def c_swap(x, bit):
    n = lax.axis_size("ctx")
    return lax.ppermute(x, "ctx", [(i, i ^ bit) for i in range(n)])


def bits_from(b):
    bits = []
    while b < lax.axis_size("ctx"):
        bits.append(b)
        b *= 2
    return bits


def chip_near(kv):
    if lax.axis_size("ctx") != 8:
        return ()
    return c_swap(kv, 2), c_swap(kv, 4)


def chip_far(kv, near):
    if not near:
        return [lax.all_gather(kv, "ctx", axis=0, tiled=True)]
    cut = kv.shape[0] // 2
    across_x, across_y = near
    far_lo = c_swap(across_x[:cut], 4)
    far_hi = c_swap(across_y[cut:], 2)
    chip = [kv, across_x, across_y, far_lo, far_hi]
    return chip + [c_swap(part, 1) for part in chip]


def kv_entry(position, per_dev, me, n):
    if n != 8:
        return position
    owner, within = position // per_dev, position % per_dev
    rel = owner ^ me
    cut = per_dev // 2
    far = (rel // 2) == 3
    late = far & (within >= cut)
    which = (rel % 2) * 5 + rel // 2 + late.astype(jnp.int32)
    return which * 1024 + jnp.where(late, within - cut, within)


def kv_slot(position, per_dev, me):
    owner, within = position // per_dev, position % per_dev
    rel = owner ^ me
    return ((rel % 2) * 4 + rel // 2) * per_dev + within


def on_device(
    tokens,
    cotangent,
    doc_lengths,
    deal,
    attn_gain,
    w_query,
    w_key,
    w_value,
    w_out,
    mlp_gain,
    w_gate,
    w_up,
    w_down,
):
    me = lax.axis_index("ctx")
    n_ctx = lax.axis_size("ctx")
    z = lax.axis_index("fsdp")
    core = me % 2
    near_me = me % 8
    chip = near_me // 2
    parity = (chip + chip // 2) % 2
    info = jnp.stack([z, core, near_me, chip, parity]).astype(jnp.int32)
    tok_rows = tokens.shape[1]
    per_dev = tok_rows // BLK
    deal_row = deal[0]
    blocks = deal_row.shape[0]
    group_size = blocks * BLK
    doc_lens = doc_lengths[0]
    seq_count = doc_lens.shape[0]
    length = group_size // seq_count
    x_turned = tokens[0].T
    cot_turned = cotangent[0].T

    block_ids = jnp.arange(blocks, dtype=jnp.int32)
    mine = lax.dynamic_slice_in_dim(deal_row, me * per_dev, per_dev)
    seq_blocks = jnp.maximum(
        mine[:, None] - (NWB - 1) + jnp.arange(NWB, dtype=jnp.int32)[None, :], 0
    )
    position = jnp.sum(
        jnp.where(seq_blocks[:, :, None] == deal_row[None, None, :], block_ids, 0), axis=-1
    )
    tab = kv_entry(position, per_dev, me, n_ctx).astype(jnp.int32)
    doc_ends = (
        jnp.cumsum(doc_lens, axis=1) + (jnp.arange(seq_count, dtype=jnp.int32) * length)[:, None]
    ).reshape(-1)
    doc_starts = doc_ends - doc_lens.reshape(-1)
    q_time = mine[:, None] * BLK + jnp.arange(BLK, dtype=jnp.int32)[None, :]
    begin = jnp.max(jnp.where(q_time[..., None] >= doc_starts, doc_starts, 0), axis=-1)
    lo = jnp.maximum(begin, q_time - (WIN - 1)) - (mine[:, None] * BLK - WIN)
    lo = lo[:, None, :].astype(jnp.int32)
    n_chips = 3 if n_ctx == 8 else 1
    owners = jnp.stack([me ^ (2 * r) for r in range(n_chips)])
    theirs = jnp.sum(
        jnp.where(
            block_ids == (owners[:, None] * per_dev + jnp.arange(per_dev, dtype=jnp.int32))[..., None],
            deal_row,
            0,
        ),
        axis=-1,
    )
    their_time = theirs[:, :, None] * BLK + jnp.arange(BLK, dtype=jnp.int32)
    their_begin = jnp.max(jnp.where(their_time[..., None] >= doc_starts, doc_starts, 0), axis=-1)
    pos = (their_time - their_begin).reshape(-1)
    half_dim = HD // 2
    freqs = ROPE_THETA ** (-jnp.arange(half_dim, dtype=F32) * (2.0 / HD))
    angle = freqs[:, None] * pos.astype(F32)[None, :]
    cos_turn, sin_turn = jnp.cos(angle), jnp.sin(angle)

    gains_wide = jnp.concatenate(
        [attn_gain[:, None], mlp_gain[:, None], jnp.zeros((ZR, QKV - 1602), BF16)], axis=1
    )
    w_parts = [w_query, w_key[:, 256:], w_key[:, :256], w_value, gains_wide]
    start = jnp.minimum(32 * near_me, ZR - 32)
    w_mine = jnp.concatenate(
        [lax.dynamic_slice_in_dim(w, start, 32, axis=0) for w in w_parts], axis=1
    )
    w_z = [z_shift(w_mine, -1), z_shift(w_mine, 2), z_shift(w_mine, 1)]
    own_half, packed, out_mine = prep_weights(info, w_gate, w_up, w_down.T, w_out)
    w_got, packed = stack_weights(info, w_z, (cos_turn, sin_turn), (packed,))
    over_z = lax.all_gather(packed, "fsdp", axis=0, tiled=False)
    cot_there = c_swap(cot_turned, 1)
    w_chips = [w_got, c_swap(w_got, 2), c_swap(w_got, 4), c_swap(w_got, 6)]
    w_pieces = [jnp.concatenate(w_parts, axis=1)]
    for piece in w_chips:
        w_pieces += [piece, c_swap(piece, 1)]

    attn_in, attn_up, attn_lo, q_low, kv_low, x, gains, w_q, w_kv = pre_call(
        info, x_turned, cos_turn, sin_turn, w_pieces
    )
    kvs = chip_far(kv_low, chip_near(kv_low))

    first, second = split_quarters(info, over_z, (*kvs, cot_there))
    first_on, second_on = c_swap(first, 2), c_swap(second, 4)
    out_mine = meet(info, (out_mine,), (first,))[0]
    out_here = [z_shift(out_mine, -1), z_shift(out_mine, 2), z_shift(out_mine, 1)]
    mid_low, recips, probs = fwd_call(tab, lo, q_low, kvs)
    *out_here, first_on, second_on = meet(info, (*out_here, first_on, second_on), (mid_low,))
    out_there = [c_swap(p, 1) for p in out_here]
    here = (first, second, first_on, second_on)
    h1, mlp_in, w_out_all, attn_up, attn_lo = pro_call(
        info, mid_low, x, gains, w_out, out_here, out_there, cot_there, (attn_up, attn_lo)
    )
    acc_o, acc_g, send_o, send_lo, send_hi, p_both, *q_both = ffn_call(
        info, mlp_in, c_swap(mlp_in, 1), cot_turned, cot_there, own_half, here
    )
    p_sum = lax.psum_scatter(p_both, "fsdp", scatter_dimension=0, tiled=True)
    q_got = [c_swap(q_both[r], 2 * r) for r in range(1, 4)]
    got_o = c_swap(send_o, 1)
    attn_turned = [attn_up, attn_lo]
    a_x = [c_swap(a, 2) for a in attn_turned]
    a_y = [c_swap(a, 4) for a in attn_turned]
    send_lo, send_hi, *a_near = meet(info, (send_lo, send_hi, *a_x, *a_y))
    got_lo, got_hi = c_swap(send_lo, 1), c_swap(send_hi, 1)
    grad_hidden, grad_mid, go_keep, go_send = epi_call(
        info, h1, acc_g, got_lo, got_hi, cot_turned, gains, w_out_all, mid_low
    )
    a_turned = [*attn_turned, *a_near]

    if n_ctx == 8:
        out_units = (4, 4)
        slots = kv_slot(position, per_dev, me).astype(jnp.int32)
    else:
        out_units = (NWB,)
        n_slots = per_dev * NWB
        flat_pos = position.reshape(-1)
        order = jnp.arange(n_slots, dtype=jnp.int32)
        slots = jnp.min(
            jnp.where(flat_pos[:, None] == flat_pos[None, :], order[None, :], n_slots), axis=1
        ).reshape(per_dev, NWB)
        source = jnp.min(
            jnp.where(block_ids[:, None] == flat_pos[None, :], order[None, :], n_slots), axis=1
        )

    def own_rows(parts):
        width = parts[0].shape[1]
        padded = jnp.concatenate(
            [parts[0].reshape(n_slots, BLK, width), jnp.zeros((1, BLK, width), BF16)], axis=0
        )
        spread = jnp.take(padded, source, axis=0).reshape(group_size, width)
        own = lax.psum_scatter(spread, "ctx", scatter_dimension=0, tiled=True)
        return own, (own, jnp.zeros_like(own), jnp.zeros_like(own))

    back_args = (
        tab, slots, out_units, q_low, grad_mid, mid_low, recips, probs, cos_turn, sin_turn, kvs
    )
    dq, *kv_parts = bwd_call(0, per_dev, (), (), *back_args)
    q_terms = (q_both[0], *q_got)
    go_pair = (go_keep, c_swap(go_send, 1))
    if n_ctx == 8:
        kv_keep, kv_send = kv_parts
        q_sum, go_both, kv_send = sum_chips(info, q_terms, go_pair, (kv_send,), (dq,))
        own, to_x, to_y, far_lo, far_hi, p_l, p_r = join_cores(
            info, kv_keep, c_swap(kv_send, 1), p_sum
        )
    else:
        q_sum, go_both = sum_chips(info, q_terms, go_pair, (), (dq,))
        own, sums = own_rows(kv_parts)
        a_turned = a_turned[:2]
        p_cut = P_ROWS // 2
        p_l, p_r = p_sum[0, :, :p_cut], p_sum[0, :, p_cut:]
    q_mine = lax.psum_scatter(q_sum, "fsdp", scatter_dimension=0, tiled=True)[0]
    for b in bits_from(8):
        q_mine = q_mine + c_swap(q_mine, b)
    go_sum = lax.psum_scatter(go_both, "fsdp", scatter_dimension=0, tiled=True)
    gq_keep, gq_send, part = post_q_call(info, attn_in, dq, w_q, own)
    p_pairs = ((p_l, c_swap(p_l, 2)), (p_r, c_swap(p_r, 4)))
    if n_ctx == 8:
        to_x, to_y, p_l, p_r, gq_send, q_mine = join_near(
            info,
            to_x,
            to_y,
            c_swap(far_lo, 2),
            c_swap(far_hi, 4),
            p_pairs,
            (gq_send, q_mine),
        )
        totals = (own, to_x, to_y)
        sums = (own, c_swap(to_x, 2), c_swap(to_y, 4))
    else:
        p_l, p_r = (a + b for a, b in p_pairs)
        totals = (own,)
    gkv_keep, gkv_send = kv_weights_back(info, cos_turn, sin_turn, a_turned, totals, p_l)
    p_pairs = ((p_l, c_swap(p_l, 4)), (p_r, c_swap(p_r, 2)))
    g_both = join_projections(
        info, (gq_keep, c_swap(gq_send, 1)), (gkv_keep, c_swap(gkv_send, 1)), p_l
    )
    output = join_output(info, h1, acc_o, got_o, g_both)
    g_sum = lax.psum_scatter(g_both, "fsdp", scatter_dimension=0, tiled=True)
    q_near = stack_two(info, q_mine, c_swap(q_mine, 2), (output,))
    q_far = c_swap(q_near, 4)
    input_grad = post_kv_call(
        info, sums, cos_turn, sin_turn, part, w_kv, x, grad_hidden, gains, q_near
    )
    for b in bits_from(8):
        p_pairs = tuple((a + c_swap(a, b), g + c_swap(g, b)) for a, g in p_pairs)
    g_l, g_r = halve_rows(info, go_sum, g_sum, (input_grad,))
    ffn_sum = join_ffn(info, p_pairs, q_near, q_far, g_l)
    g_l, g_r, ffn_sum = add_pairs(
        info, ((g_l, c_swap(g_l, 2)), (g_r, c_swap(g_r, 4))), (ffn_sum,)
    )
    gate_grad, up_grad, down_grad = finish_ffn(info, ffn_sum, c_swap(ffn_sum, 1), g_l)
    g_sum = stack_pairs(info, ((g_l, c_swap(g_l, 4)), (g_r, c_swap(g_r, 2))), gate_grad)
    for b in bits_from(8):
        g_sum = g_sum + c_swap(g_sum, b)
    query_grad, out_grad, key_grad, value_grad, gain_one, gain_two = finish_rest(
        info, g_sum, c_swap(g_sum, 1), w_pieces[0]
    )

    return (
        output.T[None],
        input_grad.T[None],
        gain_one.reshape(ZR),
        query_grad,
        key_grad.T,
        value_grad.T,
        out_grad,
        gain_two.reshape(ZR),
        gate_grad,
        up_grad,
        down_grad.T,
    )


def solution(mesh):
    in_specs = (
        P("fsdp", "ctx", None),
        P("fsdp", "ctx", None),
        P("fsdp", None, None),
        P("fsdp", None),
        P("fsdp"),
        P("fsdp", None),
        P("fsdp", None),
        P("fsdp", None),
        P("fsdp", None),
        P("fsdp"),
        P(None, "fsdp"),
        P(None, "fsdp"),
        P("fsdp", None),
    )
    out_specs = (
        P("fsdp", "ctx", None),
        P("fsdp", "ctx", None),
        P("fsdp"),
        P("fsdp", None),
        P("fsdp", None),
        P("fsdp", None),
        P("fsdp", None),
        P("fsdp"),
        P(None, "fsdp"),
        P(None, "fsdp"),
        P("fsdp", None),
    )
    return jax.shard_map(
        on_device, mesh=mesh, in_specs=in_specs, out_specs=out_specs, check_vma=False
    )
```

```python
import jax
import jax.numpy as jnp
from jax import lax
from jax.experimental import pallas as pl
from jax.experimental.pallas import tpu as pltpu
from jax.sharding import PartitionSpec as P

HQ = 15
KVH = 5
HD = 64
BLK = 128
WIN = 1024
D = 960
GRP = HQ // KVH
SPAN = WIN + BLK
NWB = SPAN // BLK
ROWS = 256
ZR = 240
ZP = 256
UNITS = 256
WIDE = 1024
QKV = 1664

NORM_EPS = 1e-05
ROPE_THETA = 100000.0
MASK_FILL = -1e30
F32 = jnp.float32
BF16 = jnp.bfloat16
MIB = 1024 * 1024

VMEM = pl.BlockSpec(memory_space=pltpu.VMEM)
SMEM = pl.BlockSpec(memory_space=pltpu.SMEM)
ANY = pl.BlockSpec(memory_space=pl.ANY)

KV_LANES = 640
PAIRS = (
    (0, 3, (0, 1), True, True),
    (1, 4, (2, 3), True, True),
    (2, 2, (4,), False, True),
)

CORE_UNITS = 320
QUARTER = 160
OUT_ROWS = 128
PACKED = 3 * QUARTER
CUT = 3 * PACKED // 2

P_ROWS = 128
Q_ROWS = 48
SEG = 64


def dot(a, b):
    return jnp.dot(a, b, preferred_element_type=F32)


def dot_nt(a, b):
    return lax.dot_general(a, b, (((1,), (1,)), ((), ())), preferred_element_type=F32)


def dot_tn(a, b):
    return lax.dot_general(a, b, (((0,), (0,)), ((), ())), preferred_element_type=F32)


def params(mib, grid_dims=0):
    return pltpu.CompilerParams(
        vmem_limit_bytes=mib * MIB,
        dimension_semantics=("arbitrary",) * grid_dims if grid_dims else None,
    )


def cost(micros):
    return pl.CostEstimate(flops=int(3.5e8 * micros), bytes_accessed=1, transcendentals=0)


def rope_slab(t, cos, sin_signed, first_half):
    swapped = jnp.where(first_half, pltpu.roll(t, 96, 1), pltpu.roll(t, 32, 1))
    return t * cos + swapped * sin_signed


def wide_tables(cos, sin):
    return (
        jnp.concatenate([cos] * 4, axis=0).T,
        jnp.concatenate([-sin, sin, -sin, sin], axis=0).T,
    )


def lane_masks(rows):
    lane = lax.broadcasted_iota(jnp.int32, (rows, 128), 1)
    return (lane % HD) < HD // 2, lane < HD


def rel_z(z, i):
    return lax.rem(z + 1 + i, 4)


def each(found, act):
    for cond, c in found:
        if cond is None:
            act(c)
        else:
            pl.when(cond)(lambda c=c: act(c))


def start(c):
    c.start()


def wait(c):
    c.wait()


def run_copies(pairs, sems):
    copies = [pltpu.make_async_copy(a, b, sems.at[i]) for i, (a, b) in enumerate(pairs)]
    for c in copies:
        c.start()
    for c in copies:
        c.wait()


MICROS = {
    "stack_two": 1,
    "meet": 1,
    "prep_weights": 5,
    "stack_weights": 2,
    "split_quarters": 5,
    "pick_out_rows": 3,
    "sum_chips": 4,
    "join_cores": 5,
    "key_value_weights_back": 11,
    "join_near": 4,
    "join_projections": 3,
    "join_output": 5,
    "add_pairs": 3,
    "stack_pairs": 2,
    "halve_rows": 2,
    "join_feed_forward": 3,
    "finish_feed_forward": 6,
    "finish_rest": 4,
}


def whole(shape):
    return pl.BlockSpec(shape, lambda i: (0,) * len(shape))


def step_call(
    name, body, info, ins, outs, far=(), scratch=(), behind=(), passed=()
):
    n_in, n_out, n_behind, n_passed = len(ins), len(outs), len(behind), len(passed)

    def kernel(info_ref, *refs):
        after = refs[n_in + n_behind + n_passed :]
        body(info_ref, refs[:n_in], after[:n_out], after[n_out + n_passed :])

    return pl.pallas_call(
        kernel,
        grid=(1,),
        out_shape=tuple(jax.ShapeDtypeStruct(shape, dtype) for shape, dtype in outs)
        + tuple(jax.ShapeDtypeStruct(p.shape, p.dtype) for p in passed),
        in_specs=[SMEM]
        + [ANY if n in far else whole(x.shape) for n, x in enumerate(ins)]
        + [ANY] * (n_behind + n_passed),
        out_specs=tuple(whole(shape) for shape, _ in outs) + (ANY,) * n_passed,
        scratch_shapes=list(scratch),
        input_output_aliases={1 + n_in + n_behind + n: n_out + n for n in range(n_passed)},
        compiler_params=params(60, 1),
        cost_estimate=cost(MICROS[name]),
        name=name,
    )(info, *ins, *behind, *passed)


def meet(info, passed, behind=()):
    return step_call("meet", lambda *refs: None, info, (), (), behind=behind, passed=passed)


def prep_weights(info, w_gate, w_up, w_down_turned, w_out):
    def body(info, ins, outs, scratch):
        core, parity = info[1], info[4]
        turn, given, sems = scratch
        base = core * CORE_UNITS
        copies = [pltpu.make_async_copy(ins[n], given.at[n], sems.at[n]) for n in range(3)]
        for c in copies:
            c.start()
        row = pl.multiple_of((ZR - OUT_ROWS) * core, 16)
        outs[2][...] = ins[3][pl.ds(row, OUT_ROWS), :]
        for n in range(3):
            copies[n].wait()
            turn[...] = given[n].T
            outs[0][n] = turn[pl.ds(pl.multiple_of(base, 16), CORE_UNITS), :]
            quarter = pl.ds(pl.multiple_of(base + QUARTER * parity, 16), QUARTER)
            outs[1][QUARTER * n : QUARTER * n + QUARTER, :] = turn[quarter, :]

    return step_call(
        "prep_weights",
        body,
        info,
        (w_gate, w_up, w_down_turned, w_out),
        (((3, CORE_UNITS, D), BF16), ((PACKED, D), BF16), ((OUT_ROWS, D), BF16)),
        far=range(3),
        scratch=(
            pltpu.VMEM((2 * CORE_UNITS, D), BF16),
            pltpu.VMEM((3,) + w_gate.shape, BF16),
            pltpu.SemaphoreType.DMA((3,)),
        ),
    )


def stack_weights(info, parts, behind, passed):
    def body(info, ins, outs, scratch):
        for n in range(3):
            outs[0][n] = ins[n][...]

    out = ((3,) + parts[0].shape, BF16)
    return step_call("stack_weights", body, info, parts, (out,), behind=behind, passed=passed)


def split_quarters(info, over_z, deps):
    at = CUT - PACKED

    def body(info, ins, outs, scratch):
        src = ins[0]
        z = info[0]
        zs = [rel_z(z, i) for i in range(3)]
        pairs = [
            (src.at[zs[0]], outs[0].at[pl.ds(0, PACKED)]),
            (src.at[zs[1], pl.ds(0, at)], outs[0].at[pl.ds(PACKED, at)]),
            (src.at[zs[1], pl.ds(at, PACKED - at)], outs[1].at[pl.ds(0, PACKED - at)]),
            (src.at[zs[2]], outs[1].at[pl.ds(PACKED - at, PACKED)]),
        ]
        run_copies(pairs, scratch[0])

    half = (CUT, D)
    return step_call(
        "split_quarters",
        body,
        info,
        (over_z, *deps),
        ((half, BF16), (half, BF16)),
        range(1 + len(deps)),
        scratch=(pltpu.SemaphoreType.DMA((4,)),),
    )


def pre_kernel(info, xt_ref, cos_ref, sin_ref, *refs):
    own, pieces = refs[0], refs[1:9]
    attn_ref, attn_up, attn_lo, q_ref, kv_ref, x_ref, gains_ref, wq_out, wkv_out = refs[9:18]
    w_ref, sems, out_sems = refs[18:]
    step = pl.program_id(0)
    z, me = info[0], info[2]
    outs = [
        pltpu.make_async_copy(w_ref.at[:, pl.ds(0, WIDE)], wq_out, out_sems.at[0]),
        pltpu.make_async_copy(w_ref.at[:, pl.ds(896, QKV - 896)], wkv_out, out_sems.at[1]),
    ]

    def pieces_do(act):
        found = []

        def add(src, row, size, cond=None):
            view = w_ref.at[pl.ds(pl.multiple_of(row, 16), size)]
            found.append((cond, pltpu.make_async_copy(src, view, sems.at[len(found)])))

        add(own, z * ZR, ZR)
        for rel, piece in enumerate(pieces):
            c = me ^ rel
            for i in range(3):
                base = rel_z(z, i) * ZR
                add(piece.at[i, pl.ds(0, 16)], base + 32 * c, 16, c < 7)
                add(piece.at[i, pl.ds(16, 16)], base + jnp.minimum(32 * c + 16, ZR - 16), 16)
        each(found, act)

    @pl.when(step == 0)
    def _():
        pieces_do(start)

    first_half, low_head = lane_masks(ROWS)
    cos, sin = wide_tables(cos_ref[...], sin_ref[...])
    x_low = xt_ref[...].T
    x_ref[...] = x_low
    x = x_low.astype(F32)
    factor = lax.rsqrt(jnp.mean(x * x, axis=-1, keepdims=True) + NORM_EPS)

    @pl.when(step == 0)
    def _():
        pieces_do(wait)
        for c in outs:
            c.start()
        gains_ref[...] = w_ref[:, 1536:QKV].astype(F32).T[64:72]

    a = (x * factor * gains_ref[0:1, :]).astype(BF16)
    attn_ref[...] = a
    turned_a = a.T
    attn_up[...] = turned_a[0 : D // 2]
    attn_lo[...] = turned_a[D // 2 :]
    qk = dot(a, w_ref[:, 0:1280])
    vv = dot(a, w_ref[:, 1280:QKV])
    slabs = [rope_slab(qk[:, 128 * j : 128 * j + 128], cos, sin, first_half) for j in range(10)]
    for j in range(7):
        q_ref[:, 128 * j : 128 * j + 128] = slabs[j].astype(BF16)
    q_ref[:, 896:960] = slabs[7][:, :64].astype(BF16)
    mixed = jnp.where(low_head, vv[:, 256:384], slabs[7])
    for j, part in enumerate((slabs[8], slabs[9], mixed, vv[:, 0:128], vv[:, 128:256])):
        kv_ref[:, 128 * j : 128 * j + 128] = part.astype(BF16)

    @pl.when(step == pl.num_programs(0) - 1)
    def _():
        for c in outs:
            c.wait()


def by_rows(width):
    return pl.BlockSpec((ROWS, width), lambda i: (i, 0))


def by_lanes(height):
    return pl.BlockSpec((height, ROWS), lambda i: (0, i))


def pre_call(info, xt, cos, sin, pieces):
    t = xt.shape[1]
    return pl.pallas_call(
        pre_kernel,
        grid=(t // ROWS,),
        out_shape=(
            jax.ShapeDtypeStruct((t, D), BF16),
            jax.ShapeDtypeStruct((D // 2, t), BF16),
            jax.ShapeDtypeStruct((D // 2, t), BF16),
            jax.ShapeDtypeStruct((t, D), BF16),
            jax.ShapeDtypeStruct((t, KV_LANES), BF16),
            jax.ShapeDtypeStruct((t, D), BF16),
            jax.ShapeDtypeStruct((8, D), F32),
            jax.ShapeDtypeStruct((D, WIDE), BF16),
            jax.ShapeDtypeStruct((D, QKV - 896), BF16),
        ),
        in_specs=[SMEM, by_lanes(D), by_lanes(32), by_lanes(32)] + [ANY] * 9,
        out_specs=(
            by_rows(D), by_lanes(D // 2), by_lanes(D // 2), by_rows(D), by_rows(KV_LANES), by_rows(D), whole((8, D)),
            ANY, ANY,
        ),
        scratch_shapes=[
            pltpu.VMEM((D, QKV), BF16),
            pltpu.SemaphoreType.DMA((49,)),
            pltpu.SemaphoreType.DMA((2,)),
        ],
        compiler_params=params(60, 1),
        cost_estimate=cost(12),
        name="pre",
    )(info, xt, cos, sin, *pieces)


def start_window(tab, kvs, win, sem, blk, slot):
    def body(j, _):
        entry = tab[blk, j]
        which = entry // 1024
        idx = lax.rem(entry, 1024)
        dst = win.at[slot, pl.ds(pl.multiple_of(j * BLK, BLK), BLK)]
        for n, ref in enumerate(kvs):
            @pl.when(which == n)
            def _():
                src = ref.at[pl.ds(pl.multiple_of(idx * BLK, BLK), BLK)]
                pltpu.make_async_copy(src, dst, sem.at[slot]).start()
        return 0

    lax.fori_loop(0, NWB, body, 0)


def next_window(tab, kvs, win, sem, first=0, meanwhile=None):
    i = pl.program_id(0)
    slot = lax.rem(i, 2)

    @pl.when(i == 0)
    def _():
        start_window(tab, kvs, win, sem, i + first, slot)

    @pl.when(i + 1 < pl.num_programs(0))
    def _():
        start_window(tab, kvs, win, sem, i + first + 1, 1 - slot)

    if meanwhile is not None:
        meanwhile()
    pltpu.make_async_copy(win.at[slot], win.at[slot], sem.at[slot]).wait()
    return slot


def turned(flat):
    rows = flat.astype(F32)
    extra = -rows.shape[1] % 128
    if extra:
        rows = jnp.concatenate([rows, jnp.zeros((rows.shape[0], extra), F32)], axis=1)
    return rows.T


def unturned(parts):
    rows = sum(p.shape[0] for p in parts)
    extra = -rows % 128
    if extra:
        parts = parts + [jnp.zeros((extra, parts[0].shape[1]), F32)]
    return jnp.concatenate(parts, axis=0).T[:, :rows].astype(BF16)


def spread_heads(rows, count, low):
    width = GRP * BLK
    sides = [jnp.concatenate(rows[GRP * n : GRP * n + GRP], axis=1) for n in range(count)]
    empty = jnp.zeros((HD, width), rows[0].dtype)
    if count == 2:
        return jnp.concatenate(
            [jnp.concatenate([sides[0], empty], axis=1), jnp.concatenate([empty, sides[1]], axis=1)],
            axis=0,
        )
    return jnp.concatenate([sides[0], empty] if low else [empty, sides[0]], axis=0)


def head_half(j, kv_heads, low):
    upper = j >= GRP if len(kv_heads) == 2 else not low
    return HD if upper else 0


def fwd_kernel(n_kv, tab, lo_ref, q_ref, *refs):
    kvs = refs[:n_kv]
    mid_ref, rl_ref, p_ref, win, bias, scores, sem = refs[n_kv:]
    slot = next_window(tab, kvs, win, sem)
    row = lax.broadcasted_iota(jnp.int32, (SPAN, BLK), 0)
    lane = lax.broadcasted_iota(jnp.int32, (SPAN, BLK), 1)
    allowed = (row >= lo_ref[0]) & (row <= lane + WIN)
    bias[...] = jnp.where(allowed, 0.0, MASK_FILL)
    q_all = (turned(q_ref[...]) * (HD ** -0.5)).astype(BF16)
    outs, recips = [], []
    at = 0
    for k_slab, v_slab, kv_heads, k_low, v_low in PAIRS:
        keys = win[slot, :, 128 * k_slab : 128 * k_slab + 128]
        vals = win[slot, :, 128 * v_slab : 128 * v_slab + 128]
        count = GRP * len(kv_heads)
        width = BLK * count
        base = BLK * at
        q_rows = [q_all[HD * (at + j) : HD * (at + j) + HD] for j in range(count)]
        scores[:, :width] = dot(keys, spread_heads(q_rows, len(kv_heads), k_low))
        for j in range(count):
            s = scores[:, BLK * j : BLK * j + BLK] + bias[...]
            top = jnp.max(s, axis=0, keepdims=True)
            p_ref[0, :, base + BLK * j : base + BLK * j + BLK] = jnp.exp(s - top).astype(BF16)
        lhs = jnp.concatenate([vals.T, jnp.ones((16, SPAN), BF16)], axis=0)
        product = dot(lhs, p_ref[0, :, base : base + width])
        recip = 1.0 / product[128:129, :]
        for j in range(count):
            cols = slice(BLK * j, BLK * j + BLK)
            half = head_half(j, kv_heads, v_low)
            outs.append(product[half : half + HD, cols] * recip[:, cols])
            recips.append(recip[:, cols])
        at += count
    mid_ref[...] = unturned(outs)
    recips.append(jnp.zeros((16 - len(recips), BLK), F32))
    rl_ref[0] = jnp.concatenate(recips, axis=0)


def fwd_call(tab, lo, q, kvs):
    blocks = q.shape[0] // BLK
    n_kv = len(kvs)
    lanes, heads = D, HQ
    return pl.pallas_call(
        lambda *refs: fwd_kernel(n_kv, *refs),
        grid=(blocks,),
        out_shape=(
            jax.ShapeDtypeStruct((q.shape[0], lanes), BF16),
            jax.ShapeDtypeStruct((blocks, 16, BLK), F32),
            jax.ShapeDtypeStruct((blocks, SPAN, heads * BLK), BF16),
        ),
        in_specs=[
            SMEM,
            pl.BlockSpec((1, 1, BLK), lambda i: (i, 0, 0)),
            pl.BlockSpec((BLK, lanes), lambda i: (i, 0)),
        ]
        + [ANY] * n_kv,
        out_specs=(
            pl.BlockSpec((BLK, lanes), lambda i: (i, 0)),
            pl.BlockSpec((1, 16, BLK), lambda i: (i, 0, 0)),
            pl.BlockSpec((1, SPAN, heads * BLK), lambda i: (i, 0, 0)),
        ),
        scratch_shapes=[
            pltpu.VMEM((2, SPAN, KV_LANES), BF16),
            pltpu.VMEM((SPAN, BLK), F32),
            pltpu.VMEM((SPAN, 2 * GRP * BLK), F32),
            pltpu.SemaphoreType.DMA((2,)),
        ],
        compiler_params=params(60, 1),
        cost_estimate=cost(32),
        name="attend",
    )(tab, lo, q, *kvs)


def bwd_kernel(
    n_kv, n_dep, first, prev, out_units, n_slots, tab, slots, q_ref, do_ref, mid_ref, rl_ref, p_ref, cos_ref, sin_ref, *refs
):
    kvs = refs[:n_kv]
    n_out = len(out_units)
    refs = refs[n_kv + n_dep :]
    earlier = refs[:n_out] if prev else ()
    refs = refs[len(earlier) :]
    dq_ref = refs[0]
    outs = refs[1 : 1 + n_out]
    win, acc, scores, stage, stage_in, sem, out_sem, in_sem = refs[1 + n_out :]
    i = pl.program_id(0)
    blk = i + first
    lanes = acc.shape[1]

    def clear_all():
        @pl.when(i == 0)
        def _():
            def clear(b, _):
                acc[pl.ds(pl.multiple_of(b * BLK, BLK), BLK), :] = jnp.zeros((BLK, lanes), F32)
                return 0

            lax.fori_loop(0, n_slots, clear, 0)

    slot = next_window(tab, kvs, win, sem, first, clear_all)

    def add(slab, value):
        for j in range(NWB):
            r = pl.ds(pl.multiple_of(slots[blk, j] * BLK, BLK), BLK)
            acc[r, 128 * slab : 128 * slab + 128] += value[BLK * j : BLK * j + BLK]

    q_all = (turned(q_ref[...]) * (HD ** -0.5)).astype(BF16)
    do_all = turned(do_ref[...])
    o_all = turned(mid_ref[...])
    cos, sin = cos_ref[...], sin_ref[...]
    grads = []
    at = 0
    for k_slab, v_slab, kv_heads, k_low, v_low in PAIRS:
        keys = win[slot, :, 128 * k_slab : 128 * k_slab + 128]
        vals = win[slot, :, 128 * v_slab : 128 * v_slab + 128]
        count = GRP * len(kv_heads)
        width = BLK * count
        base = BLK * at
        q_rows, do_rows, dots = [], [], []
        for j in range(count):
            r = slice(HD * (at + j), HD * (at + j) + HD)
            q_rows.append(q_all[r])
            scaled = do_all[r] * rl_ref[0, at + j : at + j + 1, :]
            dots.append(jnp.sum(scaled * o_all[r], axis=0, keepdims=True))
            do_rows.append(scaled.astype(BF16))
        q_wide = spread_heads(q_rows, len(kv_heads), k_low)
        do_wide = spread_heads(do_rows, len(kv_heads), v_low)
        scores[:, :width] = dot(vals, do_wide)
        ds = []
        for j in range(count):
            p = p_ref[0, :, base + BLK * j : base + BLK * j + BLK].astype(F32)
            ds.append((p * (scores[:, BLK * j : BLK * j + BLK] - dots[j])).astype(BF16))
        ds = jnp.concatenate(ds, axis=1)
        probs = p_ref[0, :, base : base + width]
        if len(kv_heads) == 2:
            add(k_slab, dot_nt(ds, q_wide))
            add(v_slab, dot_nt(probs, do_wide))
        else:
            add(
                k_slab,
                dot_nt(
                    jnp.concatenate([ds, probs], axis=1),
                    jnp.concatenate([q_wide, do_wide], axis=1),
                ),
            )
        dq = dot(keys.T, ds) * (HD ** -0.5)
        for j in range(count):
            top = head_half(j, kv_heads, k_low)
            cols = slice(BLK * j, BLK * j + BLK)
            first = dq[top : top + 32, cols]
            second = dq[top + 32 : top + 64, cols]
            grads.append(first * cos + second * sin)
            grads.append(second * cos - first * sin)
        at += count
    dq_ref[...] = unturned(grads)

    @pl.when(i == pl.num_programs(0) - 1)
    def _():
        per = 6 * BLK
        places = [(n, u) for n, units in enumerate(out_units) for u in range(units)]
        copies, loads = [], []

        def load(t):
            if prev and t < len(places):
                n, u = places[t]
                c = pltpu.make_async_copy(
                    earlier[n].at[pl.ds(per * u, per)], stage_in.at[t % 2], in_sem.at[t % 2]
                )
                c.start()
                loads.append(c)

        load(0)
        load(1)
        for t, (n, u) in enumerate(places):
            s = t % 2
            if t >= 2:
                copies[t - 2].wait()
            value = acc[per * t : per * t + per, :]
            if prev:
                loads[t].wait()
                value = value + stage_in[s].astype(F32)
            stage[s] = value.astype(BF16)
            load(t + 2)
            c = pltpu.make_async_copy(stage.at[s], outs[n].at[pl.ds(per * u, per)], out_sem.at[s])
            c.start()
            copies.append(c)
        copies[-2].wait()
        copies[-1].wait()


def bwd_call(first, blocks, earlier, deps, tab, slots, out_units, q, do, mid, rl, p, cos, sin, kvs):
    n_kv = len(kvs)
    lanes, heads, width = D, HQ, KV_LANES
    n_slots = 6 * sum(out_units)
    flat = pl.BlockSpec((BLK, lanes), lambda i: (i + first, 0))
    table = pl.BlockSpec((32, BLK), lambda i: (0, i + first))
    prev = bool(earlier)
    return pl.pallas_call(
        lambda *refs: bwd_kernel(n_kv, len(deps), first, prev, out_units, n_slots, *refs),
        grid=(blocks,),
        out_shape=(jax.ShapeDtypeStruct((blocks * BLK, lanes), BF16),)
        + tuple(jax.ShapeDtypeStruct((6 * BLK * u, width), BF16) for u in out_units),
        in_specs=[
            SMEM,
            SMEM,
            flat,
            flat,
            flat,
            pl.BlockSpec((1, 16, BLK), lambda i: (i + first, 0, 0)),
            pl.BlockSpec((1, SPAN, heads * BLK), lambda i: (i + first, 0, 0)),
            table,
            table,
        ]
        + [ANY] * (n_kv + len(deps) + len(earlier)),
        out_specs=(pl.BlockSpec((BLK, lanes), lambda i: (i, 0)),) + (ANY,) * len(out_units),
        scratch_shapes=[
            pltpu.VMEM((2, SPAN, width), BF16),
            pltpu.VMEM((n_slots * BLK, width), F32),
            pltpu.VMEM((SPAN, 2 * GRP * BLK), F32),
            pltpu.VMEM((2, 6 * BLK, width), BF16),
            pltpu.VMEM((2, 6 * BLK, width), BF16),
            pltpu.SemaphoreType.DMA((2,)),
            pltpu.SemaphoreType.DMA((2,)),
            pltpu.SemaphoreType.DMA((2,)),
        ],
        compiler_params=params(60, 1),
        cost_estimate=cost(10000),
        name=f"attend_back_{first}",
    )(tab, slots, q, do, mid, rl, p, cos, sin, *kvs, *deps, *earlier)


def pro_kernel(info, mid_ref, x_ref, gain_ref, own, *refs):
    here, there = refs[0:3], refs[3:6]
    h1_ref, low_ref, w_out, _, _, w_ref, sems, out_sem = refs[9:]
    z, core = info[0], info[1]
    step = pl.program_id(0)
    out_copy = pltpu.make_async_copy(w_ref, w_out, out_sem)
    found = []

    def bring(src, row, size):
        dst = w_ref.at[pl.ds(pl.multiple_of(row, 16), size)]
        found.append((None, pltpu.make_async_copy(src, dst, sems.at[len(found)])))

    bring(own, z * ZR, ZR)
    skip = 16 * (1 - core)
    for i in range(3):
        base = rel_z(z, i) * ZR
        bring(here[i], base + (ZR - OUT_ROWS) * core, OUT_ROWS)
        bring(
            there[i].at[pl.ds(pl.multiple_of(skip, 16), OUT_ROWS - 16)],
            base + (ZR - OUT_ROWS) * (1 - core) + skip,
            OUT_ROWS - 16,
        )

    @pl.when(step == 0)
    def _():
        each(found, start)
        each(found, wait)
        out_copy.start()

    h = x_ref[...].astype(F32) + dot(mid_ref[...], w_ref[...])
    factor = lax.rsqrt(jnp.mean(h * h, axis=-1, keepdims=True) + NORM_EPS)
    h1_ref[...] = h
    low_ref[:, 0:D] = (h * factor * gain_ref[1:2, :]).astype(BF16)
    low_ref[:, D:WIDE] = jnp.zeros((ROWS, WIDE - D), BF16)

    @pl.when(step == pl.num_programs(0) - 1)
    def _():
        out_copy.wait()


def pro_call(info, mid, x, gains, own, here, there, dep, passed):
    t = x.shape[0]
    return pl.pallas_call(
        pro_kernel,
        grid=(t // ROWS,),
        out_shape=(
            jax.ShapeDtypeStruct((t, D), F32),
            jax.ShapeDtypeStruct((t, WIDE), BF16),
            jax.ShapeDtypeStruct((D, D), BF16),
            *[jax.ShapeDtypeStruct(p.shape, p.dtype) for p in passed],
        ),
        in_specs=[SMEM, by_rows(D), by_rows(D), whole((8, D))] + [ANY] * 10,
        out_specs=(by_rows(D), by_rows(WIDE), ANY, ANY, ANY),
        input_output_aliases={12: 3, 13: 4},
        scratch_shapes=[
            pltpu.VMEM((D, D), BF16),
            pltpu.SemaphoreType.DMA((7,)),
            pltpu.SemaphoreType.DMA,
        ],
        compiler_params=params(60, 1),
        cost_estimate=cost(7),
        name="out_projection",
    )(info, mid, x, gains, own, *here, *there, dep, *passed)


def ffn_kernel(info, a0, a1, c0, c1, own, *refs):
    here = refs[:4]
    acc_outs, p_ref, q_refs = refs[4:9], refs[9], refs[10:14]
    (
        wbuf, a_all, c_all, c_turn, hid_s, gg_s, gu_s, stage, acc_o, acc_g, send_o, send_lo, send_hi,
        io_sem, w_sem, out_sem, acc_sem,
    ) = refs[14:]
    z, chip, parity = info[0], info[3], info[4]
    t = a0.shape[0]
    units = wbuf.shape[1]
    ins = [
        pltpu.make_async_copy(a0, a_all.at[pl.ds(0, t)], io_sem.at[0]),
        pltpu.make_async_copy(a1, a_all.at[pl.ds(t, t)], io_sem.at[1]),
        pltpu.make_async_copy(c0, c_turn.at[0], io_sem.at[2]),
        pltpu.make_async_copy(c1, c_turn.at[1], io_sem.at[3]),
    ]
    copies = [pltpu.make_async_copy(own, wbuf.at[:, pl.ds(0, CORE_UNITS)], w_sem.at[0])]
    for n_par, par in enumerate((parity, 1 - parity)):
        for i in range(3):
            for n in range(3):
                a0_row = PACKED * i + QUARTER * n
                for ref, p0, p1 in ((here[2 * n_par], 0, CUT), (here[2 * n_par + 1], CUT, 2 * CUT)):
                    a, b = max(p0, a0_row), min(p1, a0_row + QUARTER)
                    if a < b:
                        row = CORE_UNITS * (i + 1) + QUARTER * par + (a - a0_row)
                        dst = wbuf.at[n, pl.ds(pl.multiple_of(row, 16), b - a)]
                        copies.append(
                            pltpu.make_async_copy(
                                ref.at[pl.ds(a - p0, b - a)], dst, w_sem.at[len(copies)]
                            )
                        )
    for c in ins[2:] + ins[:2] + copies:
        c.start()
    for h in range(2):
        ins[2 + h].wait()
        c_all[t * h : t * h + t, :] = c_turn[h].T
    for c in ins[:2] + copies[:1]:
        c.wait()

    def forward(c, _):
        @pl.when(c == 1)
        def _():
            for late in copies[1:]:
                late.wait()

        u = pl.ds(pl.multiple_of(c * UNITS, UNITS), UNITS)
        for h in range(2 * t // ROWS):
            r = slice(ROWS * h, ROWS * h + ROWS)
            gate = dot_nt(a_all[r, 0:D], wbuf[0, u, :])
            up = dot_nt(a_all[r, 0:D], wbuf[1, u, :])
            grad = dot_nt(c_all[r, :], wbuf[2, u, :])
            sig = lax.logistic(gate)
            swish = gate * sig
            hid_s[r, u] = (swish * up).astype(BF16)
            gg_s[r, u] = (grad * up * (sig * (1.0 + gate * (1.0 - sig)))).astype(BF16)
            gu_s[r, u] = (grad * swish).astype(BF16)
        return 0

    lax.fori_loop(0, units // UNITS, forward, 0)

    def sums(r):
        left = dot(hid_s[r, :], wbuf[2])
        right = dot(gg_s[r, :], wbuf[0]) + dot(gu_s[r, :], wbuf[1])
        return left, right

    def mine(i, _):
        r = pl.ds(pl.multiple_of(i * ROWS, ROWS), ROWS)
        acc_o[r, :], acc_g[r, :] = sums(r)
        return 0

    def others(i, _):
        r = pl.ds(pl.multiple_of(i * ROWS, ROWS), ROWS)
        left, right = sums(pl.ds(pl.multiple_of(t + i * ROWS, ROWS), ROWS))
        empty = jnp.zeros((ROWS, WIDE - D), BF16)
        send_o[r, 0:D] = left.astype(BF16)
        send_o[r, D:WIDE] = empty
        half = WIDE // 2
        send_lo[r, :] = right[:, 0:half].astype(BF16)
        send_hi[r, 0 : D - half] = right[:, half:D].astype(BF16)
        send_hi[r, D - half : half] = empty
        return 0

    lax.fori_loop(0, t // ROWS, others, 0)
    lax.fori_loop(0, t // ROWS, mine, 0)
    acc_copies = [
        pltpu.make_async_copy(src, dst, acc_sem.at[n])
        for n, (src, dst) in enumerate(zip((acc_o, acc_g, send_o, send_lo, send_hi), acc_outs))
    ]
    for c in acc_copies:
        c.start()

    def back_copies(c, slot):
        found = []
        per = CORE_UNITS // SEG
        for n in range(UNITS // SEG):
            j = c * (UNITS // SEG) + n
            within = lax.rem(j, per)
            zz = lax.rem(z + j // per, 4)
            n_p = P_ROWS // SEG
            first = within < n_p
            row = pl.multiple_of(jnp.minimum(within, n_p - 1) * SEG, SEG)
            src = stage.at[slot, :, pl.ds(SEG * n, SEG)]
            dst = p_ref.at[zz, :, pl.ds(row, SEG)]
            found.append((first, pltpu.make_async_copy(src, dst, out_sem.at[slot, 24 + n])))
            piece = 6 * n
            for k in range(per - n_p):
                at = SEG * k
                while at < SEG * k + SEG:
                    owner = at // Q_ROWS
                    size = min(SEG * k + SEG, Q_ROWS * (owner + 1)) - at
                    src = stage.at[slot, :, pl.ds(SEG * n + at - SEG * k, size)]
                    for r in range(4):
                        dst = q_refs[r].at[zz, :, pl.ds(at - Q_ROWS * owner, size)]
                        copy = pltpu.make_async_copy(src, dst, out_sem.at[slot, piece])
                        found.append(((within == n_p + k) & (chip ^ owner == r), copy))
                    at += size
                    piece += 1
        return found

    def backward(c, _):
        u = pl.ds(pl.multiple_of(c * UNITS, UNITS), UNITS)
        slot = lax.rem(c, 2)

        @pl.when(c >= 2)
        def _():
            each(back_copies(c - 2, slot), wait)

        stage[slot, 0] = dot_tn(gg_s[:, u], a_all[:, 0:D]).astype(BF16)
        stage[slot, 1] = dot_tn(gu_s[:, u], a_all[:, 0:D]).astype(BF16)
        stage[slot, 2] = dot_tn(hid_s[:, u], c_all[...]).astype(BF16)
        each(back_copies(c, slot), start)
        return 0

    n_chunks = units // UNITS
    lax.fori_loop(0, n_chunks, backward, 0)
    for c in (n_chunks - 2, n_chunks - 1):
        each(back_copies(jnp.int32(c), c % 2), wait)
    for c in acc_copies:
        c.wait()


def ffn_call(info, a0, a1, c0, c1, own, here):
    t = a0.shape[0]
    units = 4 * CORE_UNITS
    return pl.pallas_call(
        ffn_kernel,
        out_shape=(
            jax.ShapeDtypeStruct((t, D), F32),
            jax.ShapeDtypeStruct((t, D), F32),
            jax.ShapeDtypeStruct((t, WIDE), BF16),
            jax.ShapeDtypeStruct((t, WIDE // 2), BF16),
            jax.ShapeDtypeStruct((t, WIDE // 2), BF16),
            jax.ShapeDtypeStruct((4, 3, P_ROWS, D), BF16),
            *[jax.ShapeDtypeStruct((4, 3, Q_ROWS, D), BF16)] * 4,
        ),
        in_specs=[SMEM] + [ANY] * 9,
        out_specs=(ANY,) * 10,
        scratch_shapes=[
            pltpu.VMEM((3, units, D), BF16),
            pltpu.VMEM((2 * t, WIDE), BF16),
            pltpu.VMEM((2 * t, D), BF16),
            pltpu.VMEM((2, D, t), BF16),
            pltpu.VMEM((2 * t, units), BF16),
            pltpu.VMEM((2 * t, units), BF16),
            pltpu.VMEM((2 * t, units), BF16),
            pltpu.VMEM((2, 3, UNITS, D), BF16),
            pltpu.VMEM((t, D), F32),
            pltpu.VMEM((t, D), F32),
            pltpu.VMEM((t, WIDE), BF16),
            pltpu.VMEM((t, WIDE // 2), BF16),
            pltpu.VMEM((t, WIDE // 2), BF16),
            pltpu.SemaphoreType.DMA((4,)),
            pltpu.SemaphoreType.DMA((24,)),
            pltpu.SemaphoreType.DMA((2, 28)),
            pltpu.SemaphoreType.DMA((5,)),
        ],
        compiler_params=params(60),
        cost_estimate=cost(50),
        name="feed_forward",
    )(info, a0, a1, c0, c1, own, *here)


def put_shards(ref, product, gain_grad):
    extra = ref.shape[-1] - product.shape[1]
    if extra:
        product = jnp.concatenate([product, jnp.zeros((product.shape[0], extra), F32)], axis=1)
    width = product.shape[1]
    first_row = lax.broadcasted_iota(jnp.int32, (ZP - ZR, width), 0) == 0
    for n in range(4):
        ref[n, 0:ZR, :] = product[ZR * n : ZR * n + ZR].astype(BF16)
        if gain_grad is None:
            ref[n, ZR:ZP, :] = jnp.zeros((ZP - ZR, width), BF16)
        else:
            part = jnp.concatenate(
                [gain_grad[:, ZR * n : ZR * n + ZR], jnp.zeros((1, width - ZR), F32)], axis=1
            )
            ref[n, ZR:ZP, :] = jnp.where(first_row, part, 0.0).astype(BF16)


def put_halves(core, keep_ref, send_ref, product, gain_grad):
    extra = jnp.zeros((product.shape[0], WIDE - product.shape[1]), F32)
    wide = jnp.concatenate([product, extra], axis=1)
    half = WIDE // 2
    for side, (first, second) in enumerate(((keep_ref, send_ref), (send_ref, keep_ref))):
        @pl.when(core == side)
        def _():
            put_shards(first, wide[:, :half], gain_grad)
            put_shards(second, wide[:, half:], None)


def epi_kernel(
    info, h1_ref, acc_g, got_lo, got_hi, ct_ref, gain_ref, w_ref, mid_ref, *refs
):
    gh_ref, gm_ref, keep_ref, send_ref, acc, total = refs
    i = pl.program_id(0)

    @pl.when(i == 0)
    def _():
        acc[...] = jnp.zeros((D, D), F32)
        total[...] = jnp.zeros((8, D), F32)

    h = h1_ref[...]
    factor = lax.rsqrt(jnp.mean(h * h, axis=-1, keepdims=True) + NORM_EPS)
    normed = h * factor
    got = jnp.concatenate([got_lo[...], got_hi[...]], axis=1)
    g = acc_g[...] + got[:, 0:D].astype(F32)
    scaled = g * gain_ref[1:2, :]
    back = factor * (scaled - normed * jnp.mean(scaled * normed, axis=-1, keepdims=True))
    full = ct_ref[...].T.astype(F32) + back
    gh_ref[...] = full
    res = full.astype(BF16)
    gm_ref[...] = dot_nt(res, w_ref[...]).astype(BF16)
    total[0:1, :] += jnp.sum(g * normed, axis=0, keepdims=True)
    acc[...] += dot_tn(mid_ref[...], res)

    @pl.when(i == pl.num_programs(0) - 1)
    def _():
        put_halves(info[1], keep_ref, send_ref, acc[...], total[0:1, :])


def epi_call(info, h1, acc_g, got_lo, got_hi, cot_t, gains, w_out, mid):
    t = h1.shape[0]
    rows = pl.BlockSpec((ROWS, D), lambda i: (i, 0))
    return pl.pallas_call(
        epi_kernel,
        grid=(t // ROWS,),
        out_shape=(
            jax.ShapeDtypeStruct((t, D), F32),
            jax.ShapeDtypeStruct((t, D), BF16),
            jax.ShapeDtypeStruct((4, ZP, WIDE // 2), BF16),
            jax.ShapeDtypeStruct((4, ZP, WIDE // 2), BF16),
        ),
        in_specs=[
            SMEM,
            rows,
            rows,
            by_rows(WIDE // 2),
            by_rows(WIDE // 2),
            by_lanes(D),
            whole((8, D)),
            whole((D, D)),
            rows,
        ],
        out_specs=(rows, rows) + (whole((4, ZP, WIDE // 2)),) * 2,
        scratch_shapes=[pltpu.VMEM((D, D), F32), pltpu.VMEM((8, D), F32)],
        compiler_params=params(60, 1),
        cost_estimate=cost(12),
        name="feed_forward_norm_back",
    )(info, h1, acc_g, got_lo, got_hi, cot_t, gains, w_out, mid)


def post_q_kernel(info, a_ref, g_ref, w_ref, _, keep_ref, send_ref, part_ref, acc):
    step = pl.program_id(0)

    @pl.when(step == 0)
    def _():
        acc[...] = jnp.zeros((D, D), F32)

    g = g_ref[...]
    part_ref[...] = dot_nt(g, w_ref[:, 0:D])
    acc[...] += dot_tn(a_ref[...], g)

    @pl.when(step == pl.num_programs(0) - 1)
    def _():
        put_halves(info[1], keep_ref, send_ref, acc[...], None)


def post_q_call(info, a, g, w, dep):
    t = a.shape[0]
    piece = (4, ZP, WIDE // 2)
    return pl.pallas_call(
        post_q_kernel,
        grid=(t // ROWS,),
        out_shape=(
            jax.ShapeDtypeStruct(piece, BF16),
            jax.ShapeDtypeStruct(piece, BF16),
            jax.ShapeDtypeStruct((t, D), F32),
        ),
        in_specs=[SMEM, by_rows(D), by_rows(D), whole(w.shape), ANY],
        out_specs=(whole(piece), whole(piece), by_rows(D)),
        scratch_shapes=[pltpu.VMEM((D, D), F32)],
        compiler_params=params(60, 1),
        cost_estimate=cost(8),
        name="query_back",
    )(info, a, g, w, dep)


def turn_back(slab, cos, sin, first_half, low_head):
    mixed = slab(2)
    k4 = jnp.where(low_head, 0.0, rope_slab(mixed, cos, sin, first_half))
    k01 = rope_slab(slab(0), cos, sin, first_half)
    k23 = rope_slab(slab(1), cos, sin, first_half)
    v4 = jnp.where(low_head, mixed, 0.0)
    return jnp.concatenate([k4, k01, k23, slab(3), slab(4), v4], axis=1).astype(BF16)


def kv_weights_back(info, cos, sin, turned, totals, dep):
    t = turned[0].shape[1]
    piece = ((4, ZP, 384), BF16)
    n_chips = len(totals)

    def body(info, ins, outs, scratch):
        cos_ref, sin_ref = ins[0], ins[1]
        low, acc, a_buf, g_buf, sems = scratch
        first_half, low_head = lane_masks(ROWS)
        copies = []
        for c in range(n_chips):
            pairs = [(ins[2 + 2 * c + n], a_buf.at[2 * c + n]) for n in range(2)]
            pairs.append((ins[2 + len(turned) + c], g_buf.at[pl.ds(t * c, t)]))
            copies.append(
                [pltpu.make_async_copy(a, b, sems.at[c, n]) for n, (a, b) in enumerate(pairs)]
            )
            for copy in copies[-1]:
                copy.start()
        for c in range(n_chips):
            for copy in copies[c]:
                copy.wait()
            for i in range(t // ROWS):
                at = ROWS * i

                def slab(j):
                    return g_buf[t * c + at : t * c + at + ROWS, 128 * j : 128 * j + 128].astype(F32)

                r = slice(t * c + at, t * c + at + ROWS)
                cos, sin = wide_tables(cos_ref[:, r], -sin_ref[:, r])
                low[at : at + ROWS, :] = turn_back(slab, cos, sin, first_half, low_head)
            for n, rows in enumerate((slice(0, D // 2), slice(D // 2, D))):
                value = dot(a_buf[2 * c + n], low[...])
                if c == 0:
                    acc[rows, :] = value
                else:
                    acc[rows, :] += value
        for core, (k_out, v_out) in enumerate(((outs[0], outs[1]), (outs[1], outs[0]))):
            @pl.when(info[1] == core)
            def _():
                put_shards(k_out, acc[:, 0:384], None)
                put_shards(v_out, acc[:, 384:768], None)

    return step_call(
        "key_value_weights_back",
        body,
        info,
        (cos, sin, *turned, *totals),
        (piece, piece),
        far=range(2, 2 + len(turned) + len(totals)),
        scratch=(
            pltpu.VMEM((t, 768), BF16),
            pltpu.VMEM((D, 768), F32),
            pltpu.VMEM((len(turned),) + turned[0].shape, BF16),
            pltpu.VMEM((t * n_chips, KV_LANES), BF16),
            pltpu.SemaphoreType.DMA((n_chips, 3)),
        ),
        behind=(dep,),
    )


def post_kv_kernel(
    info, s0, s1, s2, cos_ref, sin_ref, part_ref, w_ref, x_ref, gh_ref, gain_ref, ig_ref,
):
    first_half, low_head = lane_masks(ROWS)

    def slab(j):
        c = slice(128 * j, 128 * j + 128)
        return s0[:, c].astype(F32) + s1[:, c].astype(F32) + s2[:, c].astype(F32)

    cos, sin = wide_tables(cos_ref[...], -sin_ref[...])
    low = turn_back(slab, cos, sin, first_half, low_head)
    g = (
        part_ref[...]
        + dot_nt(low[:, 0:384], w_ref[:, 0:384])
        + dot_nt(low[:, 384:704], w_ref[:, 384:704])
    )
    x = x_ref[...].astype(F32)
    factor = lax.rsqrt(jnp.mean(x * x, axis=-1, keepdims=True) + NORM_EPS)
    normed = x * factor
    scaled = g * gain_ref[0:1, :]
    back = factor * (scaled - normed * jnp.mean(scaled * normed, axis=-1, keepdims=True))
    ig_ref[...] = (gh_ref[...] + back).astype(BF16).T


def post_kv_call(info, sums, cos, sin, part, w, x, gh, gain, dep):
    t = x.shape[0]
    return pl.pallas_call(
        lambda *refs: post_kv_kernel(*refs[:11], refs[12]),
        grid=(t // ROWS,),
        out_shape=jax.ShapeDtypeStruct((D, t), BF16),
        in_specs=[SMEM]
        + [by_rows(KV_LANES)] * 3
        + [by_lanes(32)] * 2
        + [by_rows(D), whole(w.shape)]
        + [by_rows(D)] * 2
        + [whole((8, D)), ANY],
        out_specs=by_lanes(D),
        compiler_params=params(60, 1),
        cost_estimate=cost(8),
        name="key_value_back",
    )(info, *sums, cos, sin, part, w, x, gh, gain, dep)


def finish_ffn(info, mine, other, dep):
    out = ((D, 2 * CORE_UNITS), F32)

    def body(info, ins, outs, scratch):
        rows = scratch[0]
        for n in range(3):
            for ref, side in ((ins[0], info[1]), (ins[1], 1 - info[1])):
                at = pl.multiple_of(side * CORE_UNITS, 16)
                rows[pl.ds(at, CORE_UNITS), :] = ref[n].astype(F32)
            outs[n][...] = rows[...].T

    return step_call(
        "finish_feed_forward",
        body,
        info,
        (mine, other),
        (out,) * 3,
        scratch=(pltpu.VMEM((2 * CORE_UNITS, D), F32),),
        behind=(dep,),
    )


def finish_rest(info, mine, other, w_own):
    half = WIDE // 2

    def body(info, ins, outs, scratch):
        wq_ref, wo_ref, wk_ref, wv_ref, one_ref, two_ref = outs

        def emit(first, second):
            def both(at):
                lanes = slice(at, at + half)
                return jnp.concatenate([first[0:ZR, lanes], second[0:ZR, lanes]], axis=1)

            wo_ref[...] = both(0).astype(F32)[:, 0:D]
            query = both(half).astype(F32)[:, 0:D]
            wq_ref[...] = query
            k = first[:, WIDE : WIDE + 384].astype(F32)
            v = second[:, WIDE : WIDE + 384].astype(F32)
            k_t = k.T
            wk_ref[...] = jnp.concatenate([k_t[128:384], k_t[64:128]], axis=0)[:, 0:ZR]
            wv_ref[...] = v.T[0:320, 0:ZR]
            w = ins[2][...].astype(F32)
            total = jnp.sum(query * w[:, 0:D], axis=1, keepdims=True)
            total += jnp.sum(k[0:ZR, 128:384] * w[:, 1024:1280], axis=1, keepdims=True)
            total += jnp.sum(k[0:ZR, 64:128] * w[:, 960:1024], axis=1, keepdims=True)
            total += jnp.sum(v[0:ZR, 0:320] * w[:, 1280:1600], axis=1, keepdims=True)
            total = total / w[:, 1600:1601]
            one_ref[...] = jnp.broadcast_to(total, (ZR, 128)).T[0:1, :]
            two_ref[...] = first[ZR:ZP, :].astype(F32)[0:1, 0:ZR]

        for core, refs in enumerate(((ins[0], ins[1]), (ins[1], ins[0]))):
            @pl.when(info[1] == core)
            def _():
                emit(*refs)

    outs = (((ZR, D), F32), ((ZR, D), F32), ((320, ZR), F32), ((320, ZR), F32), ((1, ZR), F32), ((1, ZR), F32))
    return step_call("finish_rest", body, info, (mine, other, w_own), outs)


def sum_chips(info, terms, pair, passed, behind):
    n_terms = len(terms)
    half, lanes = pair[0].shape[1] // 2, pair[0].shape[2]
    q_rows = 3 * Q_ROWS

    def body(info, ins, outs, scratch):
        out = outs[0]
        for zz in range(4):
            value = sum(ins[k][zz].astype(F32) for k in range(n_terms)).astype(BF16)
            for n in range(3):
                out[zz, Q_ROWS * n : Q_ROWS * n + Q_ROWS, 0:D] = value[n]
            out[zz, 0:q_rows, D:WIDE] = jnp.zeros((q_rows, WIDE - D), BF16)
        for n in range(2):
            r = slice(half * n, half * n + half)
            value = ins[n_terms][:, r, :] + ins[n_terms + 1][:, r, :]
            out[:, q_rows : q_rows + half, lanes * n : lanes * n + lanes] = value

    outs = (((4, q_rows + half, WIDE), BF16),)
    return step_call(
        "sum_chips", body, info, (*terms, *pair), outs, behind=behind, passed=passed
    )


def join_cores(info, keep, recv, over_z):
    rows = keep.shape[0] // 4
    cut = rows // 2
    p_cut = P_ROWS // 2

    def body(info, ins, outs, scratch):
        for n in range(3):
            r = slice(rows * n, rows * n + rows)
            outs[n][...] = ins[0][r, :] + ins[1][r, :]
        for n in range(2):
            r = slice(3 * rows + cut * n, 3 * rows + cut * n + cut)
            outs[3 + n][...] = ins[0][r, :] + ins[1][r, :]
            outs[5 + n][...] = ins[2][0, :, p_cut * n : p_cut * n + p_cut, :]

    outs = (((rows, KV_LANES), BF16),) * 3 + (((cut, KV_LANES), BF16),) * 2
    outs += (((3, p_cut, D), BF16),) * 2
    return step_call("join_cores", body, info, (keep, recv, over_z), outs)


def join_near(info, to_x, to_y, from_x, from_y, pairs, passed):
    cut = from_x.shape[0]

    def body(info, ins, outs, scratch):
        to_x, to_y, from_x, from_y = ins[:4]
        outs[0][0:cut, :] = to_x[0:cut, :]
        outs[0][cut : 2 * cut, :] = to_x[cut : 2 * cut, :] + from_y[...]
        outs[1][0:cut, :] = to_y[0:cut, :] + from_x[...]
        outs[1][cut : 2 * cut, :] = to_y[cut : 2 * cut, :]
        for n in range(2):
            outs[2 + n][...] = ins[4 + 2 * n][...] + ins[5 + 2 * n][...]

    flat = [a for pair in pairs for a in pair]
    outs = ((to_x.shape, BF16),) * 2 + tuple((a.shape, BF16) for a, _ in pairs)
    return step_call(
        "join_near", body, info, (to_x, to_y, from_x, from_y, *flat), outs, passed=passed
    )


def join_projections(info, q_pair, kv_pair, over_z, dep):
    half = WIDE // 2

    def body(info, ins, outs, scratch):
        outs[0][:, :, 0:half] = ins[0][...] + ins[1][...]
        outs[0][:, :, half : half + 384] = ins[2][...] + ins[3][...]
        for n in range(3):
            outs[1][n] = ins[4][0, Q_ROWS * n : Q_ROWS * n + Q_ROWS, 0:D]

    outs = (((4, ZP, half + 384), BF16), ((3, Q_ROWS, D), BF16))
    return step_call(
        "join_projections", body, info, (*q_pair, *kv_pair, over_z), outs, behind=(dep,)
    )


def join_output(info, h1, acc_o, got_o, dep):
    t = h1.shape[0]

    def body(info, ins, outs, scratch):
        for i in range(t // ROWS):
            r = slice(ROWS * i, ROWS * i + ROWS)
            value = ins[0][r, :] + ins[1][r, :] + ins[2][r, 0:D].astype(F32)
            outs[0][:, r] = value.astype(BF16).T

    out = ((D, t), BF16)
    return step_call("join_output", body, info, (h1, acc_o, got_o), (out,), behind=(dep,))[0]


def halve_rows(info, left, right, behind):
    rows = right.shape[1] // 2
    lanes = left.shape[2] // 2, right.shape[2]
    at = 3 * Q_ROWS

    def body(info, ins, outs, scratch):
        for n in range(2):
            outs[n][:, 0 : lanes[0]] = ins[0][0, at : at + rows, lanes[0] * n : lanes[0] * n + lanes[0]]
            outs[n][:, lanes[0] : sum(lanes)] = ins[1][0, rows * n : rows * n + rows, :]

    outs = (((rows, sum(lanes)), BF16),) * 2
    return step_call("halve_rows", body, info, (left, right), outs, behind=behind)


def add_pairs(info, pairs, passed=()):
    def body(info, ins, outs, scratch):
        for n in range(len(pairs)):
            outs[n][...] = ins[2 * n][...] + ins[2 * n + 1][...]

    flat = [a for pair in pairs for a in pair]
    outs = tuple((a.shape, BF16) for a, _ in pairs)
    return step_call("add_pairs", body, info, flat, outs, passed=passed)


def stack_two(info, first, second, behind):
    def body(info, ins, outs, scratch):
        for n in range(2):
            outs[0][n] = ins[n][...]

    out = ((2,) + first.shape, BF16)
    return step_call("stack_two", body, info, (first, second), (out,), behind=behind)[0]


def stack_pairs(info, pairs, dep):
    rows = pairs[0][0].shape[0]

    def body(info, ins, outs, scratch):
        for n in range(2):
            outs[0][rows * n : rows * n + rows, :] = ins[2 * n][...] + ins[2 * n + 1][...]

    flat = [a for pair in pairs for a in pair]
    shape = (2 * rows,) + pairs[0][0].shape[1:]
    return step_call("stack_pairs", body, info, flat, ((shape, BF16),), behind=(dep,))[0]


def join_ffn(info, pairs, near, far, dep):
    cut = P_ROWS // 2

    def body(info, ins, outs, scratch):
        chip = info[3]
        out = outs[0]
        for n in range(2):
            out[:, cut * n : cut * n + cut, :] = ins[2 * n][...] + ins[2 * n + 1][...]
        for r in range(4):
            at = pl.multiple_of(P_ROWS + Q_ROWS * (chip ^ r), 16)
            out[:, pl.ds(at, Q_ROWS), :] = ins[4 + r // 2][r % 2]

    flat = [a for pair in pairs for a in pair]
    return step_call(
        "join_feed_forward",
        body,
        info,
        (*flat, near, far),
        (((3, CORE_UNITS, D), BF16),),
        behind=(dep,),
    )[0]


def rows_after(x, start, size, tok, axis=0):
    return lax.dynamic_slice_in_dim(x, start + tok, size, axis=axis)


def z_shift(x, step):
    n = 4
    return lax.ppermute(x, "fsdp", [(i, (i + step) % n) for i in range(n)])


def c_swap(x, bit):
    n = lax.axis_size("ctx")
    return lax.ppermute(x, "ctx", [(i, i ^ bit) for i in range(n)])


def bits_from(b):
    bits = []
    while b < lax.axis_size("ctx"):
        bits.append(b)
        b *= 2
    return bits


def chip_near(kv):
    if lax.axis_size("ctx") != 8:
        return ()
    return c_swap(kv, 2), c_swap(kv, 4)


def chip_far(kv, near):
    if not near:
        return [lax.all_gather(kv, "ctx", axis=0, tiled=True)]
    cut = kv.shape[0] // 2
    across_x, across_y = near
    far_lo = c_swap(across_x[:cut], 4)
    far_hi = c_swap(across_y[cut:], 2)
    chip = [kv, across_x, across_y, far_lo, far_hi]
    return chip + [c_swap(part, 1) for part in chip]


def kv_entry(position, per_dev, me, n):
    if n != 8:
        return position
    owner, within = position // per_dev, position % per_dev
    rel = owner ^ me
    cut = per_dev // 2
    far = (rel // 2) == 3
    late = far & (within >= cut)
    which = (rel % 2) * 5 + rel // 2 + late.astype(jnp.int32)
    return which * 1024 + jnp.where(late, within - cut, within)


def kv_slot(position, per_dev, me):
    owner, within = position // per_dev, position % per_dev
    rel = owner ^ me
    return ((rel % 2) * 4 + rel // 2) * per_dev + within


def on_device(
    tokens,
    cotangent,
    doc_lengths,
    deal,
    attn_gain,
    w_query,
    w_key,
    w_value,
    w_out,
    mlp_gain,
    w_gate,
    w_up,
    w_down,
):
    me = lax.axis_index("ctx")
    n_ctx = lax.axis_size("ctx")
    z = lax.axis_index("fsdp")
    core = me % 2
    near_me = me % 8
    chip = near_me // 2
    parity = (chip + chip // 2) % 2
    info = jnp.stack([z, core, near_me, chip, parity]).astype(jnp.int32)
    tok_rows = tokens.shape[1]
    per_dev = tok_rows // BLK
    deal_row = deal[0]
    blocks = deal_row.shape[0]
    group_size = blocks * BLK
    doc_lens = doc_lengths[0]
    seq_count = doc_lens.shape[0]
    length = group_size // seq_count
    x_turned = tokens[0].T
    cot_turned = cotangent[0].T

    block_ids = jnp.arange(blocks, dtype=jnp.int32)
    mine = lax.dynamic_slice_in_dim(deal_row, me * per_dev, per_dev)
    seq_blocks = jnp.maximum(
        mine[:, None] - (NWB - 1) + jnp.arange(NWB, dtype=jnp.int32)[None, :], 0
    )
    position = jnp.sum(
        jnp.where(seq_blocks[:, :, None] == deal_row[None, None, :], block_ids, 0), axis=-1
    )
    tab = kv_entry(position, per_dev, me, n_ctx).astype(jnp.int32)
    doc_ends = (
        jnp.cumsum(doc_lens, axis=1) + (jnp.arange(seq_count, dtype=jnp.int32) * length)[:, None]
    ).reshape(-1)
    doc_starts = doc_ends - doc_lens.reshape(-1)
    q_time = mine[:, None] * BLK + jnp.arange(BLK, dtype=jnp.int32)[None, :]
    begin = jnp.max(jnp.where(q_time[..., None] >= doc_starts, doc_starts, 0), axis=-1)
    lo = jnp.maximum(begin, q_time - (WIN - 1)) - (mine[:, None] * BLK - WIN)
    lo = lo[:, None, :].astype(jnp.int32)
    n_chips = 3 if n_ctx == 8 else 1
    owners = jnp.stack([me ^ (2 * r) for r in range(n_chips)])
    theirs = jnp.sum(
        jnp.where(
            block_ids == (owners[:, None] * per_dev + jnp.arange(per_dev, dtype=jnp.int32))[..., None],
            deal_row,
            0,
        ),
        axis=-1,
    )
    their_time = theirs[:, :, None] * BLK + jnp.arange(BLK, dtype=jnp.int32)
    their_begin = jnp.max(jnp.where(their_time[..., None] >= doc_starts, doc_starts, 0), axis=-1)
    pos = (their_time - their_begin).reshape(-1)
    half_dim = HD // 2
    freqs = ROPE_THETA ** (-jnp.arange(half_dim, dtype=F32) * (2.0 / HD))
    angle = freqs[:, None] * pos.astype(F32)[None, :]
    cos_turn, sin_turn = jnp.cos(angle), jnp.sin(angle)

    gains_wide = jnp.concatenate(
        [attn_gain[:, None], mlp_gain[:, None], jnp.zeros((ZR, QKV - 1602), BF16)], axis=1
    )
    w_parts = [w_query, w_key[:, 256:], w_key[:, :256], w_value, gains_wide]
    start = jnp.minimum(32 * near_me, ZR - 32)
    w_mine = jnp.concatenate(
        [lax.dynamic_slice_in_dim(w, start, 32, axis=0) for w in w_parts], axis=1
    )
    w_z = [z_shift(w_mine, -1), z_shift(w_mine, 2), z_shift(w_mine, 1)]
    own_half, packed, out_mine = prep_weights(info, w_gate, w_up, w_down.T, w_out)
    w_got, packed = stack_weights(info, w_z, (cos_turn, sin_turn), (packed,))
    over_z = lax.all_gather(packed, "fsdp", axis=0, tiled=False)
    cot_there = c_swap(cot_turned, 1)
    w_chips = [w_got, c_swap(w_got, 2), c_swap(w_got, 4), c_swap(w_got, 6)]
    w_pieces = [jnp.concatenate(w_parts, axis=1)]
    for piece in w_chips:
        w_pieces += [piece, c_swap(piece, 1)]

    attn_in, attn_up, attn_lo, q_low, kv_low, x, gains, w_q, w_kv = pre_call(
        info, x_turned, cos_turn, sin_turn, w_pieces
    )
    kvs = chip_far(kv_low, chip_near(kv_low))

    first, second = split_quarters(info, over_z, (*kvs, cot_there))
    first_on, second_on = c_swap(first, 2), c_swap(second, 4)
    out_mine = meet(info, (out_mine,), (first,))[0]
    out_here = [z_shift(out_mine, -1), z_shift(out_mine, 2), z_shift(out_mine, 1)]
    mid_low, recips, probs = fwd_call(tab, lo, q_low, kvs)
    *out_here, first_on, second_on = meet(info, (*out_here, first_on, second_on), (mid_low,))
    out_there = [c_swap(p, 1) for p in out_here]
    here = (first, second, first_on, second_on)
    h1, mlp_in, w_out_all, attn_up, attn_lo = pro_call(
        info, mid_low, x, gains, w_out, out_here, out_there, cot_there, (attn_up, attn_lo)
    )
    acc_o, acc_g, send_o, send_lo, send_hi, p_both, *q_both = ffn_call(
        info, mlp_in, c_swap(mlp_in, 1), cot_turned, cot_there, own_half, here
    )
    p_sum = lax.psum_scatter(p_both, "fsdp", scatter_dimension=0, tiled=True)
    q_got = [c_swap(q_both[r], 2 * r) for r in range(1, 4)]
    got_o = c_swap(send_o, 1)
    attn_turned = [attn_up, attn_lo]
    a_x = [c_swap(a, 2) for a in attn_turned]
    a_y = [c_swap(a, 4) for a in attn_turned]
    send_lo, send_hi, *a_near = meet(info, (send_lo, send_hi, *a_x, *a_y))
    got_lo, got_hi = c_swap(send_lo, 1), c_swap(send_hi, 1)
    grad_hidden, grad_mid, go_keep, go_send = epi_call(
        info, h1, acc_g, got_lo, got_hi, cot_turned, gains, w_out_all, mid_low
    )
    a_turned = [*attn_turned, *a_near]

    if n_ctx == 8:
        out_units = (4, 4)
        slots = kv_slot(position, per_dev, me).astype(jnp.int32)
    else:
        out_units = (NWB,)
        n_slots = per_dev * NWB
        flat_pos = position.reshape(-1)
        order = jnp.arange(n_slots, dtype=jnp.int32)
        slots = jnp.min(
            jnp.where(flat_pos[:, None] == flat_pos[None, :], order[None, :], n_slots), axis=1
        ).reshape(per_dev, NWB)
        source = jnp.min(
            jnp.where(block_ids[:, None] == flat_pos[None, :], order[None, :], n_slots), axis=1
        )

    def own_rows(parts):
        width = parts[0].shape[1]
        padded = jnp.concatenate(
            [parts[0].reshape(n_slots, BLK, width), jnp.zeros((1, BLK, width), BF16)], axis=0
        )
        spread = jnp.take(padded, source, axis=0).reshape(group_size, width)
        own = lax.psum_scatter(spread, "ctx", scatter_dimension=0, tiled=True)
        return own, (own, jnp.zeros_like(own), jnp.zeros_like(own))

    back_args = (
        tab, slots, out_units, q_low, grad_mid, mid_low, recips, probs, cos_turn, sin_turn, kvs
    )
    dq, *kv_parts = bwd_call(0, per_dev, (), (), *back_args)
    q_terms = (q_both[0], *q_got)
    go_pair = (go_keep, c_swap(go_send, 1))
    if n_ctx == 8:
        kv_keep, kv_send = kv_parts
        both, kv_send = sum_chips(info, q_terms, go_pair, (kv_send,), (dq,))
        own, to_x, to_y, far_lo, far_hi, p_l, p_r = join_cores(
            info, kv_keep, c_swap(kv_send, 1), p_sum
        )
    else:
        both = sum_chips(info, q_terms, go_pair, (), (dq,))[0]
        own, sums = own_rows(kv_parts)
        a_turned = a_turned[:2]
        p_cut = P_ROWS // 2
        p_l, p_r = p_sum[0, :, :p_cut], p_sum[0, :, p_cut:]
    both = lax.psum_scatter(both, "fsdp", scatter_dimension=0, tiled=True)
    gq_keep, gq_send, part = post_q_call(info, attn_in, dq, w_q, own)
    p_pairs = ((p_l, c_swap(p_l, 2)), (p_r, c_swap(p_r, 4)))
    if n_ctx == 8:
        to_x, to_y, p_l, p_r, gq_send = join_near(
            info,
            to_x,
            to_y,
            c_swap(far_lo, 2),
            c_swap(far_hi, 4),
            p_pairs,
            (gq_send,),
        )
        totals = (own, to_x, to_y)
        sums = (own, c_swap(to_x, 2), c_swap(to_y, 4))
    else:
        p_l, p_r = (a + b for a, b in p_pairs)
        totals = (own,)
    gkv_keep, gkv_send = kv_weights_back(info, cos_turn, sin_turn, a_turned, totals, p_l)
    p_pairs = ((p_l, c_swap(p_l, 4)), (p_r, c_swap(p_r, 2)))
    g_both, q_mine = join_projections(
        info, (gq_keep, c_swap(gq_send, 1)), (gkv_keep, c_swap(gkv_send, 1)), both, p_l
    )
    for b in bits_from(8):
        q_mine = q_mine + c_swap(q_mine, b)
    output = join_output(info, h1, acc_o, got_o, g_both)
    g_sum = lax.psum_scatter(g_both, "fsdp", scatter_dimension=0, tiled=True)
    q_near = stack_two(info, q_mine, c_swap(q_mine, 2), (output,))
    q_far = c_swap(q_near, 4)
    input_grad = post_kv_call(
        info, sums, cos_turn, sin_turn, part, w_kv, x, grad_hidden, gains, q_near
    )
    for b in bits_from(8):
        p_pairs = tuple((a + c_swap(a, b), g + c_swap(g, b)) for a, g in p_pairs)
    g_l, g_r = halve_rows(info, both, g_sum, (input_grad,))
    ffn_sum = join_ffn(info, p_pairs, q_near, q_far, g_l)
    g_l, g_r, ffn_sum = add_pairs(
        info, ((g_l, c_swap(g_l, 2)), (g_r, c_swap(g_r, 4))), (ffn_sum,)
    )
    gate_grad, up_grad, down_grad = finish_ffn(info, ffn_sum, c_swap(ffn_sum, 1), g_l)
    g_sum = stack_pairs(info, ((g_l, c_swap(g_l, 4)), (g_r, c_swap(g_r, 2))), gate_grad)
    for b in bits_from(8):
        g_sum = g_sum + c_swap(g_sum, b)
    query_grad, out_grad, key_grad, value_grad, gain_one, gain_two = finish_rest(
        info, g_sum, c_swap(g_sum, 1), w_pieces[0]
    )

    return (
        output.T[None],
        input_grad.T[None],
        gain_one.reshape(ZR),
        query_grad,
        key_grad.T,
        value_grad.T,
        out_grad,
        gain_two.reshape(ZR),
        gate_grad,
        up_grad,
        down_grad.T,
    )


def solution(mesh):
    in_specs = (
        P("fsdp", "ctx", None),
        P("fsdp", "ctx", None),
        P("fsdp", None, None),
        P("fsdp", None),
        P("fsdp"),
        P("fsdp", None),
        P("fsdp", None),
        P("fsdp", None),
        P("fsdp", None),
        P("fsdp"),
        P(None, "fsdp"),
        P(None, "fsdp"),
        P("fsdp", None),
    )
    out_specs = (
        P("fsdp", "ctx", None),
        P("fsdp", "ctx", None),
        P("fsdp"),
        P("fsdp", None),
        P("fsdp", None),
        P("fsdp", None),
        P("fsdp", None),
        P("fsdp"),
        P(None, "fsdp"),
        P(None, "fsdp"),
        P("fsdp", None),
    )
    return jax.shard_map(
        on_device, mesh=mesh, in_specs=in_specs, out_specs=out_specs, check_vma=False
    )
```
